128 devices in a mesh: gx: 32 (over y, x, core), gy: 4 (over z).
Axes of the slice: x: 4, y: 4, z: 4, core: 2. Of those that a mesh axis runs over, the one named last changes fastest.
Arguments:
- thermal_anomaly_field: float32 [256, 128, 256], P('gx', 'gy'), may hold values from -6 to 6
- airflow_vector_field: float32 [3, 256, 128, 256], P(None, 'gx', 'gy'), may hold values from -5 to 5
- entry_matrix_first: bfloat16 [128, 128, 512], P(('gx', 'gy')), may hold values from -0.5 to 0.5
- hidden_matrix_second: bfloat16 [128, 512, 512], P(('gx', 'gy')), may hold values from -0.25 to 0.25
- final_readout_matrix: bfloat16 [128, 512, 128], P(('gx', 'gy')), may hold values from -0.25 to 0.25
- electrical_zone_offset: bfloat16 [2048, 512], P(('gx', 'gy')), may hold values from -5 to 5
- intake_source_tile: int32 [128, 128, 32], P(('gx', 'gy')), may hold values from 0 to 511
- machine_electrical_zone: int32 [128, 128, 32], P(('gx', 'gy')), may hold values from 0 to 15
- machine_tally_matrix: int32 [128, 128], P(('gx', 'gy')), may hold values from 0 to 32, as said below
- exhaust_source_tile: int32 [128, 128, 32], P(('gx', 'gy')), may hold values from 0 to 511
Outputs:
- final_field: float32 [256, 128, 256], P('gx', 'gy')
The draws below stay inside these ranges and needn't reach their ends.
Inputs may be any that keep to these rules, and one draw needn't show every extreme that they name: machine_tally_matrix[s, s] = 32, and for one device d every machine_tally_matrix[s, d] = 32.
All inputs are finite; a program needn't handle non-finite values.
Results may differ from the reference program's by a relative error of at most 0.0046.
Values may be sent and summed in bfloat16 or wider, within the bound.
No kernel may reach another device: no remote copies, remote signals or barrier semaphores. Data moves between devices by JAX's collectives and lax.ppermute only.
A program may use at most 64 MiB of HBM per device.

```python
import jax
import jax.numpy as jnp
from jax import lax

IN = 128
HID = 512
CX = 8
CY = 32
VERTICAL_POINTS = 256
CAP = 32
DOM_DEV = 16
LONGWISE_POINTS = 256
CROSSWISE_POINTS = 128
BLK_DEV = 512
DOMAINS = 2048
N_GX = 32
N_GY = 4
DEVICES = 128


def draw_machine_tally_matrix(key, part):
    key = jax.random.fold_in(key, 7)
    key_heavy, key_high, key_low, key_star = jax.random.split(key, 4)
    heavy = jax.random.randint(key_heavy, (DEVICES,), 0, 4) == 0
    high_counts = CAP - jax.random.randint(key_high, (DEVICES, DEVICES), 0, CAP // 2 + 1)
    low_counts = jax.random.randint(key_low, (DEVICES, DEVICES), 0, 3 * CAP // 4 + 1)
    counts = jnp.where(heavy[None, :], high_counts, low_counts)
    star = jax.random.randint(key_star, (), 0, DEVICES)
    columns = jnp.arange(DEVICES, dtype=jnp.int32)
    counts = jnp.where(columns[None, :] == star, CAP, counts)
    counts = jnp.where(columns[:, None] == columns[None, :], CAP, counts)
    return counts.astype(jnp.int32)


def set_ends(values, key, smallest, largest):
    longest = values.shape.index(max(values.shape))
    spots = []
    for shift in (0, 1):
        where = [jax.random.randint(jax.random.fold_in(key, axis), (), 0, length) for axis, length in enumerate(values.shape)]
        where[longest] = (where[longest] + shift) % values.shape[longest]
        spots.append(tuple(where))
    return values.at[spots[0]].set(smallest).at[spots[1]].set(largest)


def shard_levels(stream_key, extent, cuts, low, top_value):
    def one(axis_at, blocks):
        steps = jax.random.uniform(jax.random.fold_in(jax.random.fold_in(stream_key, 6), axis_at), (blocks,), jnp.float32, low / len(cuts), top_value / len(cuts))
        return jnp.repeat(jnp.exp(steps), extent[axis_at] // blocks).reshape((-1,) + (1,) * (len(extent) - axis_at - 1))

    loudness = one(*cuts[0])
    for cut in cuts[1:]:
        loudness = loudness * one(*cut)
    return loudness


def centred(rng, extent, scale, reach, cuts=(), kind=jnp.bfloat16):
    array = jax.random.normal(rng, extent, jnp.float32) * scale
    if len(cuts) > 0:
        array = shard_levels(rng, extent, cuts, -0.22, 0.18) * array
    return jnp.clip(array, min=-reach, max=reach).astype(kind)


def setup_inputs(seed: int = 0) -> dict:
    keys = jax.random.split(jax.random.key(seed), 11)
    return {
        "thermal_anomaly_field": centred(keys[0], (LONGWISE_POINTS, CROSSWISE_POINTS, VERTICAL_POINTS), 1.0, 6.0, ((0, 32), (1, 4)), jnp.float32),
        "airflow_vector_field": centred(keys[1], (3, LONGWISE_POINTS, CROSSWISE_POINTS, VERTICAL_POINTS), 1.0, 5.0, ((1, 32), (2, 4)), jnp.float32),
        "entry_matrix_first": centred(keys[2], (DEVICES, IN, HID), IN ** -0.5, 0.5, ((0, 128),)),
        "hidden_matrix_second": centred(keys[3], (DEVICES, HID, HID), HID ** -0.5, 0.25, ((0, 128),)),
        "final_readout_matrix": centred(keys[4], (DEVICES, HID, IN), HID ** -0.5, 0.25, ((0, 128),)),
        "electrical_zone_offset": centred(keys[5], (DOMAINS, HID), 1.0, 5.0, ((0, 128),)),
        "intake_source_tile": set_ends(jax.random.randint(keys[6], (DEVICES, DEVICES, CAP), 0, BLK_DEV), jax.random.fold_in(keys[6], 1), 0, BLK_DEV - 1).astype(jnp.int32),
        "machine_electrical_zone": set_ends(jax.random.randint(keys[7], (DEVICES, DEVICES, CAP), 0, DOM_DEV), jax.random.fold_in(keys[7], 1), 0, DOM_DEV - 1).astype(jnp.int32),
        "machine_tally_matrix": draw_machine_tally_matrix(jax.random.fold_in(keys[10], 71), 0),
        "exhaust_source_tile": set_ends(jax.random.randint(keys[9], (DEVICES, DEVICES, CAP), 0, BLK_DEV), jax.random.fold_in(keys[9], 1), 0, BLK_DEV - 1).astype(jnp.int32),
    }


time_step = 0.1
diffusivity = 0.5
buoyancy = 0.5


def substep(padded, airflow_vector_field):
    z_padded = jnp.pad(padded, ((0, 0), (0, 0), (1, 1)))
    center = z_padded[1:-1, 1:-1, 1:-1]
    east_side = z_padded[2:, 1:-1, 1:-1]
    west_side = z_padded[:-2, 1:-1, 1:-1]
    north_side = z_padded[1:-1, 2:, 1:-1]
    south_side = z_padded[1:-1, :-2, 1:-1]
    upper_side = z_padded[1:-1, 1:-1, 2:]
    lower_side = z_padded[1:-1, 1:-1, :-2]
    laplace = east_side + west_side + north_side + south_side + upper_side + lower_side - 6.0 * center
    transport = airflow_vector_field[0] * (east_side - west_side) * 0.5
    transport = transport + airflow_vector_field[1] * (north_side - south_side) * 0.5
    transport = transport + (airflow_vector_field[2] + buoyancy * center) * (upper_side - lower_side) * 0.5
    return center + time_step * (diffusivity * laplace - transport)


def surrogate(inlet_rows, domain_term, entry_matrix_first, hidden_matrix_second, final_readout_matrix):
    pre_act = jnp.dot(inlet_rows, entry_matrix_first, preferred_element_type=jnp.float32) + domain_term
    hidden = jax.nn.silu(pre_act).astype(jnp.bfloat16)
    second = jax.nn.silu(jnp.dot(hidden, hidden_matrix_second, preferred_element_type=jnp.float32)).astype(jnp.bfloat16)
    return jnp.dot(second, final_readout_matrix, preferred_element_type=jnp.float32).astype(jnp.bfloat16)


def reference(thermal_anomaly_field, airflow_vector_field, entry_matrix_first, hidden_matrix_second, final_readout_matrix, electrical_zone_offset, intake_source_tile, machine_electrical_zone, machine_tally_matrix, exhaust_source_tile):
    present_fields = thermal_anomaly_field
    for substep_index in range(2):
        present_fields = substep(jnp.pad(present_fields, ((1, 1), (1, 1), (0, 0))), airflow_vector_field)
    blocks = present_fields.reshape(N_GX, CX, N_GY, CY, VERTICAL_POINTS).transpose(0, 2, 1, 3, 4).reshape(DEVICES, BLK_DEV, IN)
    owners = jnp.arange(DEVICES, dtype=jnp.int32)[:, None]
    slot_ids = jnp.arange(CAP, dtype=jnp.int32)

    def visit(totals, receiver):
        block_ids = lax.dynamic_index_in_dim(intake_source_tile, receiver, 1, keepdims=False)
        inlet_rows = blocks[owners, block_ids].astype(jnp.bfloat16)
        domain_ids = lax.dynamic_index_in_dim(machine_electrical_zone, receiver, 1, keepdims=False) + receiver * DOM_DEV
        domain_term = electrical_zone_offset[domain_ids.reshape(-1)].astype(jnp.float32)
        heat_rows = surrogate(inlet_rows.reshape(-1, IN), domain_term, entry_matrix_first[receiver], hidden_matrix_second[receiver], final_readout_matrix[receiver])
        heat_rows = heat_rows.reshape(DEVICES, CAP, IN).astype(jnp.float32)
        served = lax.dynamic_index_in_dim(machine_tally_matrix, receiver, 1, keepdims=False)
        usable = slot_ids[None, :] < served[:, None]
        contrib = jnp.where(usable[:, :, None], heat_rows, jnp.float32(0.0))
        outlet_ids = lax.dynamic_index_in_dim(exhaust_source_tile, receiver, 1, keepdims=False)
        totals = totals.at[owners, outlet_ids].add(contrib)
        return totals, None

    totals = jnp.zeros((DEVICES, BLK_DEV, IN), jnp.float32)
    totals, unused = lax.scan(visit, totals, jnp.arange(DEVICES, dtype=jnp.int32))
    result = blocks + totals
    return result.reshape(N_GX, N_GY, CX, CY, VERTICAL_POINTS).transpose(0, 2, 1, 3, 4).reshape(LONGWISE_POINTS, CROSSWISE_POINTS, VERTICAL_POINTS)
```

```python
import jax
import jax.numpy as jnp
from jax import lax
from jax.experimental import pallas as pl
from jax.experimental.pallas import tpu as pltpu
from jax.sharding import PartitionSpec as P

time_step = 0.1
diffusivity = 0.5
buoyancy = 0.5

CELLS = 128
SLOTS = 32
ZONES = 16
MESSAGE_ROWS = 40
ROWS_STEP = 16


def advance(center, east, west, north, south, u0, u1, u2):
    lanes = center.shape[1]
    lane = lax.broadcasted_iota(jnp.int32, center.shape, 1)
    upper = jnp.where(lane == lanes - 1, 0.0, pltpu.roll(center, lanes - 1, 1))
    lower = jnp.where(lane == 0, 0.0, pltpu.roll(center, 1, 1))
    laplace = east + west + north + south + upper + lower - 6.0 * center
    transport = u0 * (east - west) + u1 * (north - south)
    transport = transport + (u2 + buoyancy * center) * (upper - lower)
    return center + time_step * (diffusivity * laplace - 0.5 * transport)


def field_kernel(
    inside_ref,
    f_ref,
    u_ref,
    xlo_ref,
    xhi_ref,
    ylo_ref,
    yhi_ref,
    intake_ref,
    zone_ref,
    warmed_ref,
    message_ref,
    first_ref,
    second_ref,
    rounded_ref,
    zone_rows_ref,
):
    nx, ny, _ = f_ref.shape
    top = 8
    bottom = top + ny
    first_ref[0:2, top:bottom, :] = xlo_ref[0:2]
    first_ref[2 : nx + 2, top:bottom, :] = f_ref[...]
    first_ref[nx + 2 : nx + 4, top:bottom, :] = xhi_ref[0:2]
    for i in range(nx + 2):
        first_ref[1 + i, top - 1 : top, :] = ylo_ref[i : i + 1, :]
        first_ref[1 + i, bottom : bottom + 1, :] = yhi_ref[i : i + 1, :]

    def slab(ref, at, u0, u1, u2):
        return advance(
            ref[at, top:bottom, :],
            ref[at + 1, top:bottom, :],
            ref[at - 1, top:bottom, :],
            ref[at, top + 1 : bottom + 1, :],
            ref[at, top - 1 : bottom - 1, :],
            u0,
            u1,
            u2,
        )

    for x in range(nx):
        second_ref[x + 1, top:bottom, :] = slab(first_ref, x + 2, u_ref[0, x], u_ref[1, x], u_ref[2, x])
    west_face = slab(first_ref, 1, xlo_ref[2], xlo_ref[3], xlo_ref[4])
    second_ref[0, top:bottom, :] = jnp.where(inside_ref[0] > 0, west_face, 0.0)
    east_face = slab(first_ref, nx + 2, xhi_ref[2], xhi_ref[3], xhi_ref[4])
    second_ref[nx + 1, top:bottom, :] = jnp.where(inside_ref[1] > 0, east_face, 0.0)
    edge = jnp.concatenate([f_ref[x, 0:1, :] for x in range(nx)], axis=0)
    south_face = advance(
        ylo_ref[1 : nx + 1],
        ylo_ref[2 : nx + 2],
        ylo_ref[0:nx],
        edge,
        ylo_ref[16 : 16 + nx],
        ylo_ref[24:32],
        ylo_ref[32:40],
        ylo_ref[40:48],
    )
    south_face = jnp.where(inside_ref[2] > 0, south_face, 0.0)
    edge = jnp.concatenate([f_ref[x, ny - 1 : ny, :] for x in range(nx)], axis=0)
    north_face = advance(
        yhi_ref[1 : nx + 1],
        yhi_ref[2 : nx + 2],
        yhi_ref[0:nx],
        yhi_ref[16 : 16 + nx],
        edge,
        yhi_ref[24:32],
        yhi_ref[32:40],
        yhi_ref[40:48],
    )
    north_face = jnp.where(inside_ref[3] > 0, north_face, 0.0)
    for x in range(nx):
        second_ref[x + 1, top - 1 : top, :] = south_face[x : x + 1]
        second_ref[x + 1, bottom : bottom + 1, :] = north_face[x : x + 1]

    for x in range(nx):
        warm = slab(second_ref, x + 1, u_ref[0, x], u_ref[1, x], u_ref[2, x])
        warmed_ref[x * ny : (x + 1) * ny, :] = warm
        rounded_ref[x * ny : (x + 1) * ny, :] = warm.astype(jnp.bfloat16)

    peers = intake_ref.shape[1]
    zones = jnp.transpose(zone_ref[...].astype(jnp.float32)).astype(jnp.bfloat16)
    groups = SLOTS // 8
    wide = groups * CELLS
    slot = lax.broadcasted_iota(jnp.int32, (SLOTS, wide), 0)
    lane = lax.broadcasted_iota(jnp.int32, (SLOTS, wide), 1)
    spread = (lane // ZONES == slot).astype(jnp.float32).astype(jnp.bfloat16)
    zone_wide = jnp.dot(zones, spread, preferred_element_type=jnp.float32)
    which = lax.broadcasted_iota(jnp.int32, (peers, wide), 1) % ZONES
    hot = (zone_wide == which.astype(jnp.float32)).astype(jnp.float32)
    zone_rows_ref[...] = jnp.zeros_like(zone_rows_ref)
    for j in range(groups):
        zone_rows_ref[pl.ds(j, peers, stride=8), :] = hot[:, j * CELLS : (j + 1) * CELLS]
    message_ref[:, SLOTS:MESSAGE_ROWS, :] = (
        zone_rows_ref[...].astype(jnp.bfloat16).reshape(peers, 8, CELLS)
    )

    intake = intake_ref[...]
    lane = lax.broadcasted_iota(jnp.int32, (SLOTS, CELLS), 1)
    brick = rounded_ref[...]
    one, none = jnp.float32(1), jnp.float32(0)
    for start in range(0, peers, 8):
        picks, odds = [], []
        for d in range(start, start + 8):
            block = jnp.broadcast_to(intake[:, d : d + 1], (SLOTS, CELLS))
            row = block >> 1
            odds.append((block & 1) == 1)
            picks.append(
                jnp.concatenate(
                    [jnp.where(row == lane, one, none), jnp.where(row == lane + CELLS, one, none)],
                    axis=1,
                ).astype(jnp.bfloat16)
            )
        rows = jnp.dot(jnp.concatenate(picks, axis=0), brick, preferred_element_type=jnp.float32)
        for k in range(8):
            pair = rows[k * SLOTS : (k + 1) * SLOTS]
            message_ref[start + k, 0:SLOTS, :] = jnp.where(
                odds[k], pair[:, CELLS:], pair[:, :CELLS]
            ).astype(jnp.bfloat16)


def surrogate_kernel(message_ref, first_ref, second_ref, last_ref, offset_ref, heat_ref, entry_ref):
    peers = message_ref.shape[0]
    entry_ref[0:CELLS, :] = first_ref[...]
    for k in range(CELLS // ZONES):
        entry_ref[CELLS + k * ZONES : CELLS + (k + 1) * ZONES, :] = offset_ref[...]
    sub = lax.broadcasted_iota(jnp.int32, (8, CELLS), 0)
    lane = lax.broadcasted_iota(jnp.int32, (8, CELLS), 1)
    mine = (lane // ZONES == sub).astype(jnp.float32)

    def silu(x):
        half = 0.5 * x
        return (half + half * jnp.tanh(half)).astype(jnp.bfloat16)

    def part(i, carry):
        at = i * ROWS_STEP
        rows = message_ref[pl.ds(at, ROWS_STEP), 0:SLOTS, :].reshape(ROWS_STEP * SLOTS, CELLS)
        zone = message_ref[pl.ds(at, ROWS_STEP), SLOTS:MESSAGE_ROWS, :].astype(jnp.float32)
        hots = [
            jnp.broadcast_to(zone[s, j : j + 1, :], (8, CELLS)) * mine
            for s in range(ROWS_STEP)
            for j in range(SLOTS // 8)
        ]
        hot = jnp.concatenate(hots, axis=0).astype(jnp.bfloat16)
        inputs = jnp.concatenate([rows, hot], axis=1)
        hidden = silu(jnp.dot(inputs, entry_ref[...], preferred_element_type=jnp.float32))
        second = silu(jnp.dot(hidden, second_ref[...], preferred_element_type=jnp.float32))
        heat = jnp.dot(second, last_ref[...], preferred_element_type=jnp.float32)
        heat_ref[pl.ds(at, ROWS_STEP)] = heat.astype(jnp.bfloat16).reshape(ROWS_STEP, SLOTS, CELLS)
        return carry

    lax.fori_loop(0, peers // ROWS_STEP, part, 0)


def exhaust_kernel(warmed_ref, heat_ref, outlet_ref, out_ref):
    rows = warmed_ref.shape[0]
    chunks = outlet_ref.shape[0]
    place = lax.broadcasted_iota(jnp.int32, (2 * rows, CELLS), 0)
    place = jnp.where(place < rows, 2 * place, 2 * (place - rows) + 1)
    one, none = jnp.float32(1), jnp.float32(0)
    total = jnp.zeros((2 * rows, CELLS), jnp.float32)
    for i in range(0, chunks, 2):
        hits = [
            jnp.where(place == outlet_ref[k : k + 1, :], one, none).astype(jnp.bfloat16)
            for k in (i, i + 1)
        ]
        total = total + jnp.dot(
            jnp.concatenate(hits, axis=1),
            heat_ref[i * CELLS : (i + 2) * CELLS, :],
            preferred_element_type=jnp.float32,
        )
    out_ref[:, :CELLS] = warmed_ref[:, :CELLS] + total[:rows]
    out_ref[:, CELLS:] = warmed_ref[:, CELLS:] + total[rows:]


def in_vmem(count):
    return [pl.BlockSpec(memory_space=pltpu.VMEM)] * count


def shards(
    thermal_anomaly_field,
    airflow_vector_field,
    entry_matrix_first,
    hidden_matrix_second,
    final_readout_matrix,
    electrical_zone_offset,
    intake_source_tile,
    machine_electrical_zone,
    machine_tally_matrix,
    exhaust_source_tile,
):
    f = thermal_anomaly_field
    u = airflow_vector_field
    nx, ny, nz = f.shape
    gx, gy = lax.axis_index("gx"), lax.axis_index("gy")
    n_gx, n_gy = lax.axis_size("gx"), lax.axis_size("gy")
    up_x = [(i, i + 1) for i in range(n_gx - 1)]
    down_x = [(i + 1, i) for i in range(n_gx - 1)]
    up_y = [(i, i + 1) for i in range(n_gy - 1)]
    down_y = [(i + 1, i) for i in range(n_gy - 1)]
    xlo = lax.ppermute(jnp.concatenate([f[nx - 2 :], u[:, nx - 1]], axis=0), "gx", up_x)
    xhi = lax.ppermute(jnp.concatenate([f[:2], u[:, 0]], axis=0), "gx", down_x)

    def face(edge, next_edge):
        near = jnp.concatenate([xlo[1:2, edge], f[:, edge], xhi[0:1, edge]], axis=0)
        near = jnp.pad(near, ((0, 16 - near.shape[0]), (0, 0)))
        return jnp.concatenate([near, f[:, next_edge], u[:, :, edge].reshape(3 * nx, nz)], axis=0)

    ylo = lax.ppermute(face(ny - 1, ny - 2), "gy", up_y)
    yhi = lax.ppermute(face(0, 1), "gy", down_y)
    inside = jnp.stack([gx > 0, gx < n_gx - 1, gy > 0, gy < n_gy - 1]).astype(jnp.int32)

    peers = intake_source_tile.shape[1]
    warmed, message = pl.pallas_call(
        field_kernel,
        out_shape=(
            jax.ShapeDtypeStruct((nx * ny, nz), jnp.float32),
            jax.ShapeDtypeStruct((peers, MESSAGE_ROWS, CELLS), jnp.bfloat16),
        ),
        in_specs=[pl.BlockSpec(memory_space=pltpu.SMEM)] + in_vmem(8),
        out_specs=tuple(in_vmem(2)),
        scratch_shapes=[
            pltpu.VMEM((nx + 4, ny + 16, nz), jnp.float32),
            pltpu.VMEM((nx + 2, ny + 16, nz), jnp.float32),
            pltpu.VMEM((nx * ny, nz), jnp.bfloat16),
            pltpu.VMEM((peers * 8, CELLS), jnp.float32),
        ],
        compiler_params=pltpu.CompilerParams(vmem_limit_bytes=32 * 1024 * 1024),
        name="field",
    )(
        inside,
        f,
        u,
        xlo,
        xhi,
        ylo,
        yhi,
        jnp.transpose(intake_source_tile[0]),
        jnp.transpose(machine_electrical_zone[0]),
    )

    arrived = lax.all_to_all(message, ("gx", "gy"), split_axis=0, concat_axis=0, tiled=True)
    heat = pl.pallas_call(
        surrogate_kernel,
        out_shape=jax.ShapeDtypeStruct((peers, SLOTS, CELLS), jnp.bfloat16),
        in_specs=in_vmem(5),
        out_specs=in_vmem(1)[0],
        scratch_shapes=[pltpu.VMEM((2 * CELLS, entry_matrix_first.shape[2]), jnp.bfloat16)],
        compiler_params=pltpu.CompilerParams(vmem_limit_bytes=40 * 1024 * 1024),
        name="surrogate",
    )(
        arrived,
        entry_matrix_first[0],
        hidden_matrix_second[0],
        final_readout_matrix[0],
        electrical_zone_offset,
    )
    returned = lax.all_to_all(heat, ("gx", "gy"), split_axis=0, concat_axis=0, tiled=True)

    slot = lax.broadcasted_iota(jnp.int32, exhaust_source_tile.shape[1:], 1)
    outlet = jnp.where(slot < machine_tally_matrix[0][:, None], exhaust_source_tile[0], -1)
    final = pl.pallas_call(
        exhaust_kernel,
        out_shape=jax.ShapeDtypeStruct((nx * ny, nz), jnp.float32),
        in_specs=in_vmem(3),
        out_specs=in_vmem(1)[0],
        compiler_params=pltpu.CompilerParams(vmem_limit_bytes=32 * 1024 * 1024),
        name="exhaust",
    )(warmed, returned.reshape(peers * SLOTS, CELLS), outlet.reshape(-1, CELLS))
    return final.reshape(nx, ny, nz)


def solution(mesh):
    return jax.shard_map(
        shards,
        mesh=mesh,
        in_specs=(
            P("gx", "gy", None),
            P(None, "gx", "gy", None),
            P(("gx", "gy"), None, None),
            P(("gx", "gy"), None, None),
            P(("gx", "gy"), None, None),
            P(("gx", "gy"), None),
            P(("gx", "gy"), None, None),
            P(("gx", "gy"), None, None),
            P(("gx", "gy"), None),
            P(("gx", "gy"), None, None),
        ),
        out_specs=P("gx", "gy", None),
        check_vma=False,
    )
```

```python
import jax
import jax.numpy as jnp
from jax import lax
from jax.experimental import pallas as pl
from jax.experimental.pallas import tpu as pltpu
from jax.sharding import Mesh
from jax.sharding import PartitionSpec as P

time_step = 0.1
diffusivity = 0.5
buoyancy = 0.5

CELLS = 128
SLOTS = 32
ZONES = 16
HEAD_ROWS = 256
MESSAGE_ROWS = 272


def advance(center, east, west, north, south, u0, u1, u2):
    lanes = center.shape[1]
    lane = lax.broadcasted_iota(jnp.int32, center.shape, 1)
    upper = jnp.where(lane == lanes - 1, 0.0, pltpu.roll(center, lanes - 1, 1))
    lower = jnp.where(lane == 0, 0.0, pltpu.roll(center, 1, 1))
    laplace = east + west + north + south + upper + lower - 6.0 * center
    transport = u0 * (east - west) + u1 * (north - south)
    transport = transport + (u2 + buoyancy * center) * (upper - lower)
    return center + time_step * (diffusivity * laplace - 0.5 * transport)


def field_kernel(
    inside_ref,
    f_ref,
    u_ref,
    xlo_ref,
    xhi_ref,
    ylo_ref,
    yhi_ref,
    intake_ref,
    zone_ref,
    warmed_ref,
    message_ref,
    first_ref,
    second_ref,
    rounded_ref,
):
    nx, ny, _ = f_ref.shape
    top = 8
    bottom = top + ny
    first_ref[0:2, top:bottom, :] = xlo_ref[0:2]
    first_ref[2 : nx + 2, top:bottom, :] = f_ref[...]
    first_ref[nx + 2 : nx + 4, top:bottom, :] = xhi_ref[0:2]
    for i in range(nx + 2):
        first_ref[1 + i, top - 1 : top, :] = ylo_ref[i : i + 1, :]
        first_ref[1 + i, bottom : bottom + 1, :] = yhi_ref[i : i + 1, :]

    def slab(ref, at, u0, u1, u2):
        return advance(
            ref[at, top:bottom, :],
            ref[at + 1, top:bottom, :],
            ref[at - 1, top:bottom, :],
            ref[at, top + 1 : bottom + 1, :],
            ref[at, top - 1 : bottom - 1, :],
            u0,
            u1,
            u2,
        )

    for x in range(nx):
        second_ref[x + 1, top:bottom, :] = slab(first_ref, x + 2, u_ref[0, x], u_ref[1, x], u_ref[2, x])
    west_face = slab(first_ref, 1, xlo_ref[2], xlo_ref[3], xlo_ref[4])
    second_ref[0, top:bottom, :] = jnp.where(inside_ref[0] > 0, west_face, 0.0)
    east_face = slab(first_ref, nx + 2, xhi_ref[2], xhi_ref[3], xhi_ref[4])
    second_ref[nx + 1, top:bottom, :] = jnp.where(inside_ref[1] > 0, east_face, 0.0)
    edge = jnp.concatenate([f_ref[x, 0:1, :] for x in range(nx)], axis=0)
    south_face = advance(
        ylo_ref[1 : nx + 1],
        ylo_ref[2 : nx + 2],
        ylo_ref[0:nx],
        edge,
        ylo_ref[16 : 16 + nx],
        ylo_ref[24:32],
        ylo_ref[32:40],
        ylo_ref[40:48],
    )
    south_face = jnp.where(inside_ref[2] > 0, south_face, 0.0)
    edge = jnp.concatenate([f_ref[x, ny - 1 : ny, :] for x in range(nx)], axis=0)
    north_face = advance(
        yhi_ref[1 : nx + 1],
        yhi_ref[2 : nx + 2],
        yhi_ref[0:nx],
        yhi_ref[16 : 16 + nx],
        edge,
        yhi_ref[24:32],
        yhi_ref[32:40],
        yhi_ref[40:48],
    )
    north_face = jnp.where(inside_ref[3] > 0, north_face, 0.0)
    for x in range(nx):
        second_ref[x + 1, top - 1 : top, :] = south_face[x : x + 1]
        second_ref[x + 1, bottom : bottom + 1, :] = north_face[x : x + 1]

    for x in range(nx):
        warm = slab(second_ref, x + 1, u_ref[0, x], u_ref[1, x], u_ref[2, x])
        warmed_ref[x * ny : (x + 1) * ny, :] = warm
        rounded_ref[x * ny : (x + 1) * ny, :] = warm.astype(jnp.bfloat16)

    message_ref[:, HEAD_ROWS:MESSAGE_ROWS, :] = zone_ref[...]

    peers = intake_ref.shape[1]
    intake = intake_ref[...]
    lane = lax.broadcasted_iota(jnp.int32, (SLOTS, CELLS), 1)
    brick = rounded_ref[...]
    one, none = jnp.float32(1), jnp.float32(0)
    for start in range(0, peers, 8):
        picks, odds = [], []
        for d in range(start, start + 8):
            block = jnp.broadcast_to(intake[:, d : d + 1], (SLOTS, CELLS))
            row = block >> 1
            odds.append((block & 1) == 1)
            picks.append(
                jnp.concatenate(
                    [jnp.where(row == lane, one, none), jnp.where(row == lane + CELLS, one, none)],
                    axis=1,
                ).astype(jnp.bfloat16)
            )
        rows = jnp.dot(jnp.concatenate(picks, axis=0), brick, preferred_element_type=jnp.float32)
        for k in range(8):
            pair = rows[k * SLOTS : (k + 1) * SLOTS]
            at = (start + k) * SLOTS % HEAD_ROWS
            message_ref[(start + k) * SLOTS // HEAD_ROWS, at : at + SLOTS, :] = jnp.where(
                odds[k], pair[:, CELLS:], pair[:, :CELLS]
            ).astype(jnp.bfloat16)


def surrogate_kernel(message_ref, weights_ref, heat_ref, entry_ref, hot_ref):
    member = pl.program_id(0)
    senders = message_ref.shape[0]
    hid = weights_ref.shape[2] - CELLS
    members = pl.num_programs(0)

    @pl.when(member == 0)
    def _():
        entry_ref[...] = jnp.zeros_like(entry_ref)
        lane = lax.broadcasted_iota(jnp.int32, (SLOTS, CELLS), 1).astype(jnp.float32)
        zones = message_ref[:, HEAD_ROWS : HEAD_ROWS + 8, :].astype(jnp.float32)
        zones = jnp.transpose(zones.reshape(senders * 8, CELLS))
        for s in range(senders):
            for m in range(HEAD_ROWS // SLOTS):
                at = (m % 4) * SLOTS
                column = s * 8 + m // 4
                zone = jnp.broadcast_to(zones[at : at + SLOTS, column : column + 1], lane.shape)
                hot = jnp.where(zone == lane, jnp.float32(1), jnp.float32(0))
                hot_ref[m, s * SLOTS : (s + 1) * SLOTS, :] = hot.astype(jnp.bfloat16)

    entry_ref[0 : CELLS + ZONES, :] = weights_ref[0, hid:, 0:hid]

    def silu(x):
        half = 0.5 * x
        return (half + half * jnp.tanh(half)).astype(jnp.bfloat16)

    at = pl.multiple_of(member * SLOTS, SLOTS)
    rows = message_ref[:, pl.ds(at, SLOTS), :].reshape(senders * SLOTS, CELLS)
    inputs = jnp.concatenate([rows, hot_ref[member]], axis=1)
    hidden = silu(jnp.dot(inputs, entry_ref[...], preferred_element_type=jnp.float32))
    second = silu(
        jnp.dot(hidden, weights_ref[0, 0:hid, 0:hid], preferred_element_type=jnp.float32)
    )
    heat = jnp.dot(second, weights_ref[0, 0:hid, hid:], preferred_element_type=jnp.float32)
    heat_ref[:, pl.ds(at, SLOTS), :] = heat.astype(jnp.bfloat16).reshape(senders, SLOTS, CELLS)


def exhaust_kernel(warmed_ref, heat_ref, outlet_ref, out_ref):
    rows = warmed_ref.shape[0]
    chunks = outlet_ref.shape[0]
    place = lax.broadcasted_iota(jnp.int32, (2 * rows, CELLS), 0)
    place = jnp.where(place < rows, 2 * place, 2 * (place - rows) + 1)
    one, none = jnp.float32(1), jnp.float32(0)
    total = jnp.zeros((2 * rows, CELLS), jnp.float32)
    for i in range(0, chunks, 2):
        hits = [
            jnp.where(place == outlet_ref[k : k + 1, :], one, none).astype(jnp.bfloat16)
            for k in (i, i + 1)
        ]
        total = total + jnp.dot(
            jnp.concatenate(hits, axis=1),
            heat_ref[i * CELLS : (i + 2) * CELLS, :],
            preferred_element_type=jnp.float32,
        )
    out_ref[:, :CELLS] = warmed_ref[:, :CELLS] + total[:rows]
    out_ref[:, CELLS:] = warmed_ref[:, CELLS:] + total[rows:]


def in_vmem(count):
    return [pl.BlockSpec(memory_space=pltpu.VMEM)] * count


def shards(
    thermal_anomaly_field,
    airflow_vector_field,
    entry_matrix_first,
    hidden_matrix_second,
    final_readout_matrix,
    electrical_zone_offset,
    intake_source_tile,
    machine_electrical_zone,
    machine_tally_matrix,
    exhaust_source_tile,
):
    tail = jnp.concatenate([entry_matrix_first[0], electrical_zone_offset], axis=0)
    weights = jnp.concatenate(
        [
            jnp.concatenate([hidden_matrix_second[0], final_readout_matrix[0]], axis=1),
            jnp.pad(tail, ((0, 0), (0, CELLS))),
        ],
        axis=0,
    )
    weights = lax.all_gather(weights, ("core", "z"), axis=0)

    f = thermal_anomaly_field
    u = airflow_vector_field
    nx, ny, nz = f.shape
    length, width = ("y", "x", "core"), "z"
    gx, gy = lax.axis_index(length), lax.axis_index(width)
    n_gx, n_gy = lax.axis_size(length), lax.axis_size(width)
    up_x = [(i, i + 1) for i in range(n_gx - 1)]
    down_x = [(i + 1, i) for i in range(n_gx - 1)]
    up_y = [(i, i + 1) for i in range(n_gy - 1)]
    down_y = [(i + 1, i) for i in range(n_gy - 1)]
    xlo = lax.ppermute(jnp.concatenate([f[nx - 2 :], u[:, nx - 1]], axis=0), length, up_x)
    xhi = lax.ppermute(jnp.concatenate([f[:2], u[:, 0]], axis=0), length, down_x)

    def face(edge, next_edge):
        near = jnp.concatenate([xlo[1:2, edge], f[:, edge], xhi[0:1, edge]], axis=0)
        near = jnp.pad(near, ((0, 16 - near.shape[0]), (0, 0)))
        return jnp.concatenate([near, f[:, next_edge], u[:, :, edge].reshape(3 * nx, nz)], axis=0)

    ylo = lax.ppermute(face(ny - 1, ny - 2), width, up_y)
    yhi = lax.ppermute(face(0, 1), width, down_y)
    inside = jnp.stack([gx > 0, gx < n_gx - 1, gy > 0, gy < n_gy - 1]).astype(jnp.int32)

    peers = intake_source_tile.shape[1]
    columns = peers * SLOTS // HEAD_ROWS
    zones = machine_electrical_zone[0].astype(jnp.bfloat16).reshape(columns, -1, CELLS)
    zones = jnp.pad(zones, ((0, 0), (0, MESSAGE_ROWS - HEAD_ROWS - zones.shape[1]), (0, 0)))
    warmed, message = pl.pallas_call(
        field_kernel,
        out_shape=(
            jax.ShapeDtypeStruct((nx * ny, nz), jnp.float32),
            jax.ShapeDtypeStruct((columns, MESSAGE_ROWS, CELLS), jnp.bfloat16),
        ),
        in_specs=[pl.BlockSpec(memory_space=pltpu.SMEM)] + in_vmem(8),
        out_specs=tuple(in_vmem(2)),
        scratch_shapes=[
            pltpu.VMEM((nx + 4, ny + 16, nz), jnp.float32),
            pltpu.VMEM((nx + 2, ny + 16, nz), jnp.float32),
            pltpu.VMEM((nx * ny, nz), jnp.bfloat16),
        ],
        compiler_params=pltpu.CompilerParams(vmem_limit_bytes=32 * 1024 * 1024),
        name="field",
    )(
        inside,
        f,
        u,
        xlo,
        xhi,
        ylo,
        yhi,
        jnp.transpose(intake_source_tile[0]),
        zones,
    )

    arrived = lax.all_to_all(message, ("y", "x"), split_axis=0, concat_axis=0, tiled=True)
    members, depth, breadth = weights.shape
    whole = lambda i: (0, 0, 0)
    heat = pl.pallas_call(
        surrogate_kernel,
        grid=(members,),
        out_shape=jax.ShapeDtypeStruct((columns, HEAD_ROWS, CELLS), jnp.bfloat16),
        in_specs=[
            pl.BlockSpec((columns, MESSAGE_ROWS, CELLS), whole),
            pl.BlockSpec((1, depth, breadth), lambda i: (i, 0, 0)),
        ],
        out_specs=pl.BlockSpec((columns, HEAD_ROWS, CELLS), whole),
        scratch_shapes=[
            pltpu.VMEM((2 * CELLS, breadth - CELLS), jnp.bfloat16),
            pltpu.VMEM((members, columns * SLOTS, CELLS), jnp.bfloat16),
        ],
        compiler_params=pltpu.CompilerParams(vmem_limit_bytes=40 * 1024 * 1024),
        name="surrogate",
    )(arrived, weights)
    returned = lax.all_to_all(heat, ("y", "x"), split_axis=0, concat_axis=0, tiled=True)

    slot = lax.broadcasted_iota(jnp.int32, exhaust_source_tile.shape[1:], 1)
    outlet = jnp.where(slot < machine_tally_matrix[0][:, None], exhaust_source_tile[0], -1)
    final = pl.pallas_call(
        exhaust_kernel,
        out_shape=jax.ShapeDtypeStruct((nx * ny, nz), jnp.float32),
        in_specs=in_vmem(3),
        out_specs=in_vmem(1)[0],
        compiler_params=pltpu.CompilerParams(vmem_limit_bytes=32 * 1024 * 1024),
        name="exhaust",
    )(warmed, returned.reshape(peers * SLOTS, CELLS), outlet.reshape(-1, CELLS))
    return final.reshape(nx, ny, nz)


def solution(mesh):
    devices = mesh.devices
    split = Mesh(devices.reshape(4, 4, 2, devices.shape[1]), ("y", "x", "core", "z"))
    length = ("y", "x", "core")
    every = length + ("z",)
    return jax.shard_map(
        shards,
        mesh=split,
        in_specs=(
            P(length, "z", None),
            P(None, length, "z", None),
            P(every, None, None),
            P(every, None, None),
            P(every, None, None),
            P(every, None),
            P(every, None, None),
            P(every, None, None),
            P(every, None),
            P(every, None, None),
        ),
        out_specs=P(length, "z", None),
        check_vma=False,
    )
```

```python
import jax
import jax.numpy as jnp
from jax import lax
from jax.experimental import pallas as pl
from jax.experimental.pallas import tpu as pltpu
from jax.sharding import PartitionSpec as P

time_step = 0.1
diffusivity = 0.5
buoyancy = 0.5

CELLS = 128
SLOTS = 32
ZONES = 16
MESSAGE_ROWS = 40
ROWS_STEP = 16


def advance(center, east, west, north, south, u0, u1, u2):
    lanes = center.shape[1]
    lane = lax.broadcasted_iota(jnp.int32, center.shape, 1)
    upper = jnp.where(lane == lanes - 1, 0.0, pltpu.roll(center, lanes - 1, 1))
    lower = jnp.where(lane == 0, 0.0, pltpu.roll(center, 1, 1))
    laplace = east + west + north + south + upper + lower - 6.0 * center
    transport = u0 * (east - west) + u1 * (north - south)
    transport = transport + (u2 + buoyancy * center) * (upper - lower)
    return center + time_step * (diffusivity * laplace - 0.5 * transport)


def faces_kernel(f_ref, u_ref, across_ref, beside_ref, held_ref, sems):
    nx = f_ref.shape[0]
    odd = lax.axis_index("gx") % 2
    copies = []
    for k, high in enumerate((odd, 1 - odd)):
        copies.append(
            (
                pltpu.make_async_copy(
                    f_ref.at[pl.ds(high * (nx - 2), 2)], held_ref.at[k, pl.ds(0, 2)], sems.at[k, 0]
                ),
                pltpu.make_async_copy(
                    u_ref.at[:, high * (nx - 1)], held_ref.at[k, pl.ds(2, 3)], sems.at[k, 1]
                ),
            )
        )
    for pair in copies:
        for copy in pair:
            copy.start()
    for k, ref in enumerate((across_ref, beside_ref)):
        for copy in copies[k]:
            copy.wait()
        ref[...] = held_ref[k].astype(jnp.bfloat16)


def field_kernel(
    inside_ref,
    f_ref,
    u_ref,
    x_across_ref,
    x_beside_ref,
    y_then_ref,
    y_first_ref,
    intake_ref,
    zone_ref,
    warmed_ref,
    message_ref,
    first_ref,
    second_ref,
    rounded_ref,
    zone_rows_ref,
):
    nx, ny, _ = f_ref.shape
    top = 8
    bottom = top + ny
    odd_x, odd_y = inside_ref[4] > 0, inside_ref[5] > 0
    x_across = x_across_ref[...].astype(jnp.float32)
    x_beside = x_beside_ref[...].astype(jnp.float32)
    y_first = y_first_ref[...].astype(jnp.float32)
    y_then = y_then_ref[...].astype(jnp.float32)
    xlo, xhi = jnp.where(odd_x, x_beside, x_across), jnp.where(odd_x, x_across, x_beside)
    ylo, yhi = jnp.where(odd_y, y_first, y_then), jnp.where(odd_y, y_then, y_first)
    first_ref[0:2, top:bottom, :] = xlo[0:2]
    first_ref[2 : nx + 2, top:bottom, :] = f_ref[...]
    first_ref[nx + 2 : nx + 4, top:bottom, :] = xhi[0:2]
    for i in range(nx + 2):
        first_ref[1 + i, top - 1 : top, :] = ylo[i : i + 1, :]
        first_ref[1 + i, bottom : bottom + 1, :] = yhi[i : i + 1, :]

    def slab(ref, at, u0, u1, u2):
        return advance(
            ref[at, top:bottom, :],
            ref[at + 1, top:bottom, :],
            ref[at - 1, top:bottom, :],
            ref[at, top + 1 : bottom + 1, :],
            ref[at, top - 1 : bottom - 1, :],
            u0,
            u1,
            u2,
        )

    for x in range(nx):
        second_ref[x + 1, top:bottom, :] = slab(first_ref, x + 2, u_ref[0, x], u_ref[1, x], u_ref[2, x])
    west_face = slab(first_ref, 1, xlo[2], xlo[3], xlo[4])
    second_ref[0, top:bottom, :] = jnp.where(inside_ref[0] > 0, west_face, 0.0)
    east_face = slab(first_ref, nx + 2, xhi[2], xhi[3], xhi[4])
    second_ref[nx + 1, top:bottom, :] = jnp.where(inside_ref[1] > 0, east_face, 0.0)
    edge = jnp.concatenate([f_ref[x, 0:1, :] for x in range(nx)], axis=0)
    south_face = advance(
        ylo[1 : nx + 1],
        ylo[2 : nx + 2],
        ylo[0:nx],
        edge,
        ylo[16 : 16 + nx],
        ylo[24:32],
        ylo[32:40],
        ylo[40:48],
    )
    south_face = jnp.where(inside_ref[2] > 0, south_face, 0.0)
    edge = jnp.concatenate([f_ref[x, ny - 1 : ny, :] for x in range(nx)], axis=0)
    north_face = advance(
        yhi[1 : nx + 1],
        yhi[2 : nx + 2],
        yhi[0:nx],
        yhi[16 : 16 + nx],
        edge,
        yhi[24:32],
        yhi[32:40],
        yhi[40:48],
    )
    north_face = jnp.where(inside_ref[3] > 0, north_face, 0.0)
    for x in range(nx):
        second_ref[x + 1, top - 1 : top, :] = south_face[x : x + 1]
        second_ref[x + 1, bottom : bottom + 1, :] = north_face[x : x + 1]

    for x in range(nx):
        warm = slab(second_ref, x + 1, u_ref[0, x], u_ref[1, x], u_ref[2, x])
        warmed_ref[x * ny : (x + 1) * ny, :] = warm
        rounded_ref[x * ny : (x + 1) * ny, :] = warm.astype(jnp.bfloat16)

    peers = intake_ref.shape[1]
    zones = jnp.transpose(zone_ref[...].astype(jnp.float32)).astype(jnp.bfloat16)
    groups = SLOTS // 8
    wide = groups * CELLS
    slot = lax.broadcasted_iota(jnp.int32, (SLOTS, wide), 0)
    lane = lax.broadcasted_iota(jnp.int32, (SLOTS, wide), 1)
    spread = (lane // ZONES == slot).astype(jnp.float32).astype(jnp.bfloat16)
    zone_wide = jnp.dot(zones, spread, preferred_element_type=jnp.float32)
    which = lax.broadcasted_iota(jnp.int32, (peers, wide), 1) % ZONES
    hot = (zone_wide == which.astype(jnp.float32)).astype(jnp.float32)
    zone_rows_ref[...] = jnp.zeros_like(zone_rows_ref)
    for j in range(groups):
        zone_rows_ref[pl.ds(j, peers, stride=8), :] = hot[:, j * CELLS : (j + 1) * CELLS]
    message_ref[:, SLOTS:MESSAGE_ROWS, :] = (
        zone_rows_ref[...].astype(jnp.bfloat16).reshape(peers, 8, CELLS)
    )

    intake = intake_ref[...]
    lane = lax.broadcasted_iota(jnp.int32, (SLOTS, CELLS), 1)
    brick = rounded_ref[...]
    one, none = jnp.float32(1), jnp.float32(0)
    for start in range(0, peers, 8):
        picks, odds = [], []
        for d in range(start, start + 8):
            block = jnp.broadcast_to(intake[:, d : d + 1], (SLOTS, CELLS))
            row = block >> 1
            odds.append((block & 1) == 1)
            picks.append(
                jnp.concatenate(
                    [jnp.where(row == lane, one, none), jnp.where(row == lane + CELLS, one, none)],
                    axis=1,
                ).astype(jnp.bfloat16)
            )
        rows = jnp.dot(jnp.concatenate(picks, axis=0), brick, preferred_element_type=jnp.float32)
        for k in range(8):
            pair = rows[k * SLOTS : (k + 1) * SLOTS]
            message_ref[start + k, 0:SLOTS, :] = jnp.where(
                odds[k], pair[:, CELLS:], pair[:, :CELLS]
            ).astype(jnp.bfloat16)


def surrogate_kernel(
    message_ref, first_ref, second_ref, last_ref, offset_ref, heat_ref, entry_ref, rows_ref, sems
):
    peers = message_ref.shape[0]
    entry_ref[0:CELLS, :] = first_ref[...]
    for k in range(CELLS // ZONES):
        entry_ref[CELLS + k * ZONES : CELLS + (k + 1) * ZONES, :] = offset_ref[...]
    sub = lax.broadcasted_iota(jnp.int32, (8, CELLS), 0)
    lane = lax.broadcasted_iota(jnp.int32, (8, CELLS), 1)
    mine = (lane // ZONES == sub).astype(jnp.float32)

    def silu(x):
        half = 0.5 * x
        return (half + half * jnp.tanh(half)).astype(jnp.bfloat16)

    copies = []
    for at in range(0, peers, ROWS_STEP):
        rows = message_ref[at : at + ROWS_STEP, 0:SLOTS, :].reshape(ROWS_STEP * SLOTS, CELLS)
        zone = message_ref[at : at + ROWS_STEP, SLOTS:MESSAGE_ROWS, :].astype(jnp.float32)
        hots = [
            jnp.broadcast_to(zone[s, j : j + 1, :], (8, CELLS)) * mine
            for s in range(ROWS_STEP)
            for j in range(SLOTS // 8)
        ]
        hot = jnp.concatenate(hots, axis=0).astype(jnp.bfloat16)
        inputs = jnp.concatenate([rows, hot], axis=1)
        hidden = silu(jnp.dot(inputs, entry_ref[...], preferred_element_type=jnp.float32))
        second = silu(jnp.dot(hidden, second_ref[...], preferred_element_type=jnp.float32))
        heat = jnp.dot(second, last_ref[...], preferred_element_type=jnp.float32)
        rows_ref[at : at + ROWS_STEP] = heat.astype(jnp.bfloat16).reshape(ROWS_STEP, SLOTS, CELLS)
        part = pl.ds(at, ROWS_STEP)
        copy = pltpu.make_async_copy(
            rows_ref.at[part], heat_ref.at[part], sems.at[at // ROWS_STEP]
        )
        copy.start()
        copies.append(copy)
    for copy in copies:
        copy.wait()


def exhaust_kernel(warmed_ref, heat_ref, outlet_ref, out_ref):
    rows = warmed_ref.shape[0]
    chunks = outlet_ref.shape[0]
    place = lax.broadcasted_iota(jnp.int32, (2 * rows, CELLS), 0)
    place = jnp.where(place < rows, 2 * place, 2 * (place - rows) + 1)
    one, none = jnp.float32(1), jnp.float32(0)
    total = jnp.zeros((2 * rows, CELLS), jnp.float32)
    for i in range(0, chunks, 2):
        hits = [
            jnp.where(place == outlet_ref[k : k + 1, :], one, none).astype(jnp.bfloat16)
            for k in (i, i + 1)
        ]
        total = total + jnp.dot(
            jnp.concatenate(hits, axis=1),
            heat_ref[i * CELLS : (i + 2) * CELLS, :],
            preferred_element_type=jnp.float32,
        )
    out_ref[:, :CELLS] = warmed_ref[:, :CELLS] + total[:rows]
    out_ref[:, CELLS:] = warmed_ref[:, CELLS:] + total[rows:]


def in_vmem(count):
    return [pl.BlockSpec(memory_space=pltpu.VMEM)] * count


def shards(
    thermal_anomaly_field,
    airflow_vector_field,
    entry_matrix_first,
    hidden_matrix_second,
    final_readout_matrix,
    electrical_zone_offset,
    intake_source_tile,
    machine_electrical_zone,
    machine_tally_matrix,
    exhaust_source_tile,
):
    f = thermal_anomaly_field
    u = airflow_vector_field
    nx, ny, nz = f.shape
    gx, gy = lax.axis_index("gx"), lax.axis_index("gy")
    n_gx, n_gy = lax.axis_size("gx"), lax.axis_size("gy")
    odd_x, odd_y = gx % 2, gy % 2
    across = [(i, i + 1) for i in range(1, n_gx - 1, 2)] + [(i + 1, i) for i in range(1, n_gx - 1, 2)]
    beside = [(i, i ^ 1) for i in range(n_gx)]

    faces = jax.ShapeDtypeStruct((5, ny, nz), jnp.bfloat16)
    face_across, face_beside = pl.pallas_call(
        faces_kernel,
        out_shape=(faces, faces),
        in_specs=[pl.BlockSpec(memory_space=pl.ANY)] * 2,
        out_specs=tuple(in_vmem(2)),
        scratch_shapes=[
            pltpu.VMEM((2, 5, ny, nz), jnp.float32),
            pltpu.SemaphoreType.DMA((2, 2)),
        ],
        name="faces",
    )(f, u)
    x_across = lax.ppermute(face_across, "gx", across)
    x_beside = lax.ppermute(face_beside, "gx", beside)
    first_y = [(i, i ^ 1) for i in range(n_gy)]
    then_y = [(i, i + 1) for i in range(1, n_gy - 1, 2)] + [(i + 1, i) for i in range(1, n_gy - 1, 2)]
    below = jnp.where(odd_x == 1, x_beside[1:2], x_across[1:2])
    above = jnp.where(odd_x == 1, x_across[0:1], x_beside[0:1])

    def face_y(high):
        edge, next_edge = high * (ny - 1), high * (ny - 3) + 1
        at = lambda a, i: lax.dynamic_index_in_dim(a, i, a.ndim - 2, False)
        own = at(f, edge).astype(jnp.bfloat16)
        near = jnp.concatenate([at(below, edge), own, at(above, edge)], axis=0)
        near = jnp.pad(near, ((0, 16 - near.shape[0]), (0, 0)))
        rest = jnp.concatenate([at(f, next_edge), at(u, edge).reshape(3 * nx, nz)], axis=0)
        return jnp.concatenate([near, rest.astype(jnp.bfloat16)], axis=0)

    y_then = lax.ppermute(face_y(odd_y), "gy", then_y)
    y_first = lax.ppermute(face_y(1 - odd_y), "gy", first_y)
    inside = jnp.stack(
        [gx > 0, gx < n_gx - 1, gy > 0, gy < n_gy - 1, odd_x == 1, odd_y == 1]
    ).astype(jnp.int32)

    peers = intake_source_tile.shape[1]
    warmed, message = pl.pallas_call(
        field_kernel,
        out_shape=(
            jax.ShapeDtypeStruct((nx * ny, nz), jnp.float32),
            jax.ShapeDtypeStruct((peers, MESSAGE_ROWS, CELLS), jnp.bfloat16),
        ),
        in_specs=[pl.BlockSpec(memory_space=pltpu.SMEM)] + in_vmem(8),
        out_specs=tuple(in_vmem(2)),
        scratch_shapes=[
            pltpu.VMEM((nx + 4, ny + 16, nz), jnp.float32),
            pltpu.VMEM((nx + 2, ny + 16, nz), jnp.float32),
            pltpu.VMEM((nx * ny, nz), jnp.bfloat16),
            pltpu.VMEM((peers * 8, CELLS), jnp.float32),
        ],
        compiler_params=pltpu.CompilerParams(vmem_limit_bytes=32 * 1024 * 1024),
        name="field",
    )(
        inside,
        f,
        u,
        x_across,
        x_beside,
        y_then,
        y_first,
        jnp.transpose(intake_source_tile[0]),
        jnp.transpose(machine_electrical_zone[0]),
    )

    arrived = lax.all_to_all(message, ("gx", "gy"), split_axis=0, concat_axis=0, tiled=True)
    heat = pl.pallas_call(
        surrogate_kernel,
        out_shape=jax.ShapeDtypeStruct((peers, SLOTS, CELLS), jnp.bfloat16),
        in_specs=in_vmem(5),
        out_specs=pl.BlockSpec(memory_space=pl.ANY),
        scratch_shapes=[
            pltpu.VMEM((2 * CELLS, entry_matrix_first.shape[2]), jnp.bfloat16),
            pltpu.VMEM((peers, SLOTS, CELLS), jnp.bfloat16),
            pltpu.SemaphoreType.DMA((peers // ROWS_STEP,)),
        ],
        compiler_params=pltpu.CompilerParams(vmem_limit_bytes=40 * 1024 * 1024),
        name="surrogate",
    )(
        arrived,
        entry_matrix_first[0],
        hidden_matrix_second[0],
        final_readout_matrix[0],
        electrical_zone_offset,
    )
    returned = lax.all_to_all(heat, ("gx", "gy"), split_axis=0, concat_axis=0, tiled=True)

    slot = lax.broadcasted_iota(jnp.int32, exhaust_source_tile.shape[1:], 1)
    outlet = jnp.where(slot < machine_tally_matrix[0][:, None], exhaust_source_tile[0], -1)
    final = pl.pallas_call(
        exhaust_kernel,
        out_shape=jax.ShapeDtypeStruct((nx * ny, nz), jnp.float32),
        in_specs=in_vmem(3),
        out_specs=in_vmem(1)[0],
        compiler_params=pltpu.CompilerParams(vmem_limit_bytes=32 * 1024 * 1024),
        name="exhaust",
    )(warmed, returned.reshape(peers * SLOTS, CELLS), outlet.reshape(-1, CELLS))
    return final.reshape(nx, ny, nz)


def solution(mesh):
    return jax.shard_map(
        shards,
        mesh=mesh,
        in_specs=(
            P("gx", "gy", None),
            P(None, "gx", "gy", None),
            P(("gx", "gy"), None, None),
            P(("gx", "gy"), None, None),
            P(("gx", "gy"), None, None),
            P(("gx", "gy"), None),
            P(("gx", "gy"), None, None),
            P(("gx", "gy"), None, None),
            P(("gx", "gy"), None),
            P(("gx", "gy"), None, None),
        ),
        out_specs=P("gx", "gy", None),
        check_vma=False,
    )
```

```python
import jax
import jax.numpy as jnp
from jax import lax
from jax.experimental import pallas as pl
from jax.experimental.pallas import tpu as pltpu
from jax.sharding import Mesh
from jax.sharding import PartitionSpec as P

time_step = 0.1
diffusivity = 0.5
buoyancy = 0.5

CELLS = 128
SLOTS = 32
ZONES = 16
HEAD_ROWS = 2 * SLOTS
MESSAGE_ROWS = HEAD_ROWS + 8
ROWS_STEP = 16


def advance(center, east, west, north, south, u0, u1, u2):
    lanes = center.shape[1]
    lane = lax.broadcasted_iota(jnp.int32, center.shape, 1)
    upper = jnp.where(lane == lanes - 1, 0.0, pltpu.roll(center, lanes - 1, 1))
    lower = jnp.where(lane == 0, 0.0, pltpu.roll(center, 1, 1))
    laplace = east + west + north + south + upper + lower - 6.0 * center
    transport = u0 * (east - west) + u1 * (north - south)
    transport = transport + (u2 + buoyancy * center) * (upper - lower)
    return center + time_step * (diffusivity * laplace - 0.5 * transport)


def by_core(table, odd_core):
    columns = table.shape[1]
    lane = lax.broadcasted_iota(jnp.int32, table.shape, 1)
    later, earlier = pltpu.roll(table, columns - 4, 1), pltpu.roll(table, 4, 1)
    return jnp.where(odd_core, jnp.where((lane & 4) == 0, later, earlier), table)


def faces_kernel(f_ref, u_ref, across_ref, beside_ref, held_ref, sems):
    nx = f_ref.shape[0]
    odd = lax.axis_index("core")
    copies = []
    for k, high in enumerate((odd, 1 - odd)):
        copies.append(
            (
                pltpu.make_async_copy(
                    f_ref.at[pl.ds(high * (nx - 2), 2)], held_ref.at[k, pl.ds(0, 2)], sems.at[k, 0]
                ),
                pltpu.make_async_copy(
                    u_ref.at[:, high * (nx - 1)], held_ref.at[k, pl.ds(2, 3)], sems.at[k, 1]
                ),
            )
        )
    for pair in copies:
        for copy in pair:
            copy.start()
    for k, ref in enumerate((across_ref, beside_ref)):
        for copy in copies[k]:
            copy.wait()
        ref[...] = held_ref[k].astype(jnp.bfloat16)


def interior_kernel(
    inside_ref,
    f_ref,
    u_ref,
    x_across_ref,
    x_beside_ref,
    intake_ref,
    zone_ref,
    outlet_ref,
    tally_ref,
    warmed_ref,
    edge_ref,
    pick_ref,
    side_ref,
    zone_out_ref,
    lanes_ref,
    first_ref,
    second_ref,
    hot_ref,
    zone_rows_ref,
    turned_ref,
):
    nx, ny, nz = f_ref.shape
    top = 8
    bottom = top + ny
    odd_x = inside_ref[4] > 0
    x_across = x_across_ref[...].astype(jnp.float32)
    x_beside = x_beside_ref[...].astype(jnp.float32)
    xlo, xhi = jnp.where(odd_x, x_beside, x_across), jnp.where(odd_x, x_across, x_beside)
    first_ref[0:2, top:bottom, :] = xlo[0:2]
    first_ref[2 : nx + 2, top:bottom, :] = f_ref[...]
    first_ref[nx + 2 : nx + 4, top:bottom, :] = xhi[0:2]
    for ref in (first_ref, second_ref):
        ref[:, top - 8 : top, :] = jnp.zeros((ref.shape[0], 8, nz), jnp.float32)
        ref[:, bottom : bottom + 8, :] = jnp.zeros((ref.shape[0], 8, nz), jnp.float32)

    def slab(ref, at, u0, u1, u2):
        return advance(
            ref[at, top:bottom, :],
            ref[at + 1, top:bottom, :],
            ref[at - 1, top:bottom, :],
            ref[at, top + 1 : bottom + 1, :],
            ref[at, top - 1 : bottom - 1, :],
            u0,
            u1,
            u2,
        )

    for x in range(nx):
        second_ref[x + 1, top:bottom, :] = slab(first_ref, x + 2, u_ref[0, x], u_ref[1, x], u_ref[2, x])
    west_face = slab(first_ref, 1, xlo[2], xlo[3], xlo[4])
    second_ref[0, top:bottom, :] = jnp.where(inside_ref[0] > 0, west_face, 0.0)
    east_face = slab(first_ref, nx + 2, xhi[2], xhi[3], xhi[4])
    second_ref[nx + 1, top:bottom, :] = jnp.where(inside_ref[1] > 0, east_face, 0.0)
    for x in range(nx):
        warmed_ref[x * ny : (x + 1) * ny, :] = slab(
            second_ref, x + 1, u_ref[0, x], u_ref[1, x], u_ref[2, x]
        )

    gap = jnp.zeros((1, nz), jnp.float32)
    rest = jnp.zeros((4, nz), jnp.float32)

    def keep(k, rows):
        edge_ref[k] = jnp.concatenate(rows + [rest], axis=0)

    for side, (y, inner, innermost) in enumerate(((0, 1, 2), (ny - 1, ny - 2, ny - 3))):
        at = side * 10
        cells = lambda ref, y, first, last: [ref[x, top + y : top + y + 1, :] for x in range(first, last)]
        keep(at, cells(first_ref, y, 0, nx + 4))
        keep(at + 1, cells(first_ref, inner, 0, nx + 4))
        keep(at + 2, [gap] + cells(second_ref, inner, 0, nx + 2) + [gap])
        keep(at + 3, [gap] + cells(second_ref, innermost, 0, nx + 2) + [gap])
        for k in range(3):
            wind = [u_ref[k, x, y : y + 1, :] for x in range(nx)]
            keep(at + 4 + k, [gap, xlo[2 + k, y : y + 1]] + wind + [xhi[2 + k, y : y + 1], gap])
            wind = [u_ref[k, x, inner : inner + 1, :] for x in range(nx)]
            keep(at + 7 + k, [gap, gap] + wind + [gap, gap])

    peers = intake_ref.shape[1]
    zones = jnp.transpose(by_core(zone_ref[...], odd_x).astype(jnp.float32)).astype(jnp.bfloat16)
    groups = SLOTS // 8
    wide = groups * CELLS
    slot = lax.broadcasted_iota(jnp.int32, (SLOTS, wide), 0)
    lane = lax.broadcasted_iota(jnp.int32, (SLOTS, wide), 1)
    spread = (lane // ZONES == slot).astype(jnp.float32).astype(jnp.bfloat16)
    zone_wide = jnp.dot(zones, spread, preferred_element_type=jnp.float32)
    which = lax.broadcasted_iota(jnp.int32, (peers, wide), 1) % ZONES
    hot = (zone_wide == which.astype(jnp.float32)).astype(jnp.float32)
    for j in range(groups):
        hot_ref[j * peers : (j + 1) * peers, :] = hot[:, j * CELLS : (j + 1) * CELLS]
    for z in range(4):
        for turn in range(2):
            for j in range(groups):
                zone_rows_ref[pl.ds(z * 8 + turn * 4 + j, peers // 8, stride=32), :] = hot_ref[
                    pl.ds(j * peers + turn * 4 + z, peers // 8, stride=8), :
                ]
    zone_out_ref[...] = zone_rows_ref[...].astype(jnp.bfloat16).reshape(peers // 2, 8, CELLS)

    intake = by_core(intake_ref[...], odd_x)
    lane = lax.broadcasted_iota(jnp.int32, (SLOTS, CELLS), 1)
    one, none = jnp.float32(1), jnp.float32(0)
    for d in range(peers):
        block = jnp.broadcast_to(intake[:, d : d + 1], (SLOTS, CELLS))
        row = block >> 1
        span = slice(d * SLOTS, (d + 1) * SLOTS)
        pick_ref[span, :CELLS] = jnp.where(row == lane, one, none).astype(jnp.bfloat16)
        pick_ref[span, CELLS:] = jnp.where(row == lane + CELLS, one, none).astype(jnp.bfloat16)
        side_ref[span, :] = (block & 1).astype(jnp.float32).astype(jnp.bfloat16)

    for zh, half in enumerate(outlet_lanes(odd_x, outlet_ref, tally_ref, turned_ref)):
        lanes_ref[zh] = half


def field_kernel(
    inside_ref,
    y_then_ref,
    y_first_ref,
    edge_ref,
    pick_ref,
    side_ref,
    zone_ref,
    interior_ref,
    warmed_ref,
    message_ref,
):
    nx = (edge_ref.shape[1] - 4) - 4
    ny = interior_ref.shape[0] // nx
    odd_y = inside_ref[5] > 0
    y_first = y_first_ref[...].astype(jnp.float32)
    y_then = y_then_ref[...].astype(jnp.float32)
    ylo, yhi = jnp.where(odd_y, y_first, y_then), jnp.where(odd_y, y_then, y_first)
    warmed_ref[...] = interior_ref[...]
    spot = lax.broadcasted_iota(jnp.int32, (nx + 2, edge_ref.shape[2]), 0)
    west = jnp.logical_and(spot == 0, inside_ref[0] == 0)
    east = jnp.logical_and(spot == nx + 1, inside_ref[1] == 0)
    outside = jnp.logical_or(west, east)
    for side, halo in enumerate((ylo, yhi)):
        at = side * 10
        def step(center, inward, outward, wind, first, last):
            middle = center[first:last]
            north, south = (inward, outward) if side == 0 else (outward, inward)
            return advance(
                middle, center[first + 1 : last + 1], center[first - 1 : last - 1], north, south, *wind
            )

        wind = [halo[24 + 8 * k : 32 + 8 * k] for k in range(3)]
        beyond = step(halo, edge_ref[at, 2 : nx + 2], halo[16 : 16 + nx], wind, 1, nx + 1)
        beyond = jnp.where(inside_ref[2 + side] > 0, beyond, 0.0)
        wind = [edge_ref[at + 4 + k] for k in range(3)]
        near = step(
            edge_ref[at],
            edge_ref[at + 1, 1 : nx + 3],
            halo[0 : nx + 2],
            [w[1 : nx + 3] for w in wind],
            1,
            nx + 3,
        )
        near = jnp.where(outside, 0.0, near)
        inner, innermost = edge_ref[at + 2], edge_ref[at + 3]
        outer_row = step(near, inner[2 : nx + 2], beyond, [w[2 : nx + 2] for w in wind], 1, nx + 1)
        wind = [edge_ref[at + 7 + k, 2 : nx + 2] for k in range(3)]
        inner_row = step(inner, innermost[2 : nx + 2], near[1 : nx + 1], wind, 2, nx + 2)
        rows = (outer_row, inner_row) if side == 0 else (inner_row, outer_row)
        for x in range(nx):
            y = x * ny + side * (ny - 2)
            warmed_ref[y : y + 1, :] = rows[0][x : x + 1]
            warmed_ref[y + 1 : y + 2, :] = rows[1][x : x + 1]

    message_ref[:, HEAD_ROWS:MESSAGE_ROWS, :] = zone_ref[...]
    brick = warmed_ref[...].astype(jnp.bfloat16)
    group = 8 * SLOTS
    for start in range(0, pick_ref.shape[0], group):
        span = slice(start, start + group)
        pair = jnp.dot(pick_ref[span, :], brick, preferred_element_type=jnp.float32)
        pair = pair.astype(jnp.bfloat16)
        rows = jnp.where(side_ref[span, :] > 0, pair[:, CELLS:], pair[:, :CELLS])
        peer = start // HEAD_ROWS
        for k in range(8):
            at = k // 4 * SLOTS
            message_ref[peer + k % 4, at : at + SLOTS, :] = rows[k * SLOTS : (k + 1) * SLOTS]


def outlet_lanes(odd_core, outlet_ref, tally_ref, turned_ref):
    slots, peers = outlet_ref.shape
    slot = lax.broadcasted_iota(jnp.int32, outlet_ref.shape, 0)
    outlet = jnp.where(slot < tally_ref[...], outlet_ref[...], -1)
    outlet = by_core(outlet, odd_core).astype(jnp.float32)
    turned_ref[...] = jnp.concatenate(
        [jnp.transpose(outlet), jnp.zeros((peers, CELLS - slots), jnp.float32)], axis=1
    )
    halves = []
    for zh in range(2):
        lanes = 0.0
        for q in range(4):
            part = turned_ref[pl.ds(2 * zh + q // 2 + 4 * (q % 2), peers // 8, stride=8), :]
            lanes = lanes + (pltpu.roll(part, q * slots, 1) if q else part)
        halves.append(lanes.astype(jnp.int32))
    return halves


def surrogate_kernel(
    message_ref,
    first_ref,
    second_ref,
    last_ref,
    offset_ref,
    first_other_ref,
    second_other_ref,
    last_other_ref,
    offset_other_ref,
    heat_ref,
    entry_ref,
):
    peers = message_ref.shape[0]
    sub = lax.broadcasted_iota(jnp.int32, (8, CELLS), 0)
    lane = lax.broadcasted_iota(jnp.int32, (8, CELLS), 1)
    mine = (lane // ZONES == sub).astype(jnp.float32)

    def silu(x):
        half = 0.5 * x
        return (half + half * jnp.tanh(half)).astype(jnp.bfloat16)

    other = (first_other_ref, second_other_ref, last_other_ref, offset_other_ref)
    own = (first_ref, second_ref, last_ref, offset_ref)
    for turn, (entry, middle, last, offset) in enumerate((own, other)):
        entry_ref[turn, 0:CELLS, :] = entry[...]
        for k in range(CELLS // ZONES):
            entry_ref[turn, CELLS + k * ZONES : CELLS + (k + 1) * ZONES, :] = offset[...]
        slots = slice(turn * SLOTS, (turn + 1) * SLOTS)
        for at in range(0, peers, ROWS_STEP):
            rows = message_ref[at : at + ROWS_STEP, slots, :].reshape(ROWS_STEP * SLOTS, CELLS)
            zone = message_ref[at : at + ROWS_STEP, HEAD_ROWS:MESSAGE_ROWS, :].astype(jnp.float32)
            hots = [
                jnp.broadcast_to(zone[s, j : j + 1, :], (8, CELLS)) * mine
                for s in range(ROWS_STEP)
                for j in range(turn * 4, turn * 4 + 4)
            ]
            hot = jnp.concatenate(hots, axis=0).astype(jnp.bfloat16)
            inputs = jnp.concatenate([rows, hot], axis=1)
            hidden = silu(jnp.dot(inputs, entry_ref[turn], preferred_element_type=jnp.float32))
            second = silu(jnp.dot(hidden, middle[...], preferred_element_type=jnp.float32))
            heat = jnp.dot(second, last[...], preferred_element_type=jnp.float32)
            heat_ref[at : at + ROWS_STEP, slots, :] = heat.astype(jnp.bfloat16).reshape(
                ROWS_STEP, SLOTS, CELLS
            )


def exhaust_kernel(warmed_ref, heat_ref, outlet_ref, out_ref):
    rows = warmed_ref.shape[0]
    halves, chunks = outlet_ref.shape[:2]
    place = lax.broadcasted_iota(jnp.int32, (rows, CELLS), 0)
    one, none = jnp.float32(1), jnp.float32(0)
    blocks, odds = [], []
    for zh in range(halves):
        outlet = outlet_ref[zh]
        blocks.append(outlet >> 1)
        odd = (outlet & 1).astype(jnp.float32)
        odds.append(jnp.transpose(jnp.concatenate([odd] * (CELLS // chunks), axis=0)))
    total = warmed_ref[...]
    step = 4
    for start in range(0, chunks, step):
        hits, sides = [], []
        for yx in range(start, start + step):
            for zh in range(halves):
                hit = jnp.where(place == blocks[zh][yx : yx + 1], one, none)
                hits.append(hit.astype(jnp.bfloat16))
                side = jnp.broadcast_to(odds[zh][:, yx : yx + 1], (CELLS, CELLS))
                sides.append(side.astype(jnp.bfloat16))
        heat = heat_ref[start * halves * CELLS : (start + step) * halves * CELLS, :]
        second = heat * jnp.concatenate(sides, axis=0)
        total = total + jnp.dot(
            jnp.concatenate(hits, axis=1),
            jnp.concatenate([heat - second, second], axis=1),
            preferred_element_type=jnp.float32,
        )
    out_ref[...] = total


def in_vmem(count):
    return [pl.BlockSpec(memory_space=pltpu.VMEM)] * count


def shards(
    thermal_anomaly_field,
    airflow_vector_field,
    entry_matrix_first,
    hidden_matrix_second,
    final_readout_matrix,
    electrical_zone_offset,
    intake_source_tile,
    machine_electrical_zone,
    machine_tally_matrix,
    exhaust_source_tile,
):
    f = thermal_anomaly_field
    u = airflow_vector_field
    nx, ny, nz = f.shape
    length = ("y", "x", "core")
    gx, gy = lax.axis_index(length), lax.axis_index("z")
    n_gx, n_gy = lax.axis_size(length), lax.axis_size("z")
    odd_x, odd_y = lax.axis_index("core"), gy % 2
    across = [(i, i + 1) for i in range(1, n_gx - 1, 2)] + [(i + 1, i) for i in range(1, n_gx - 1, 2)]
    beside = [(i, i ^ 1) for i in range(n_gx)]

    faces = jax.ShapeDtypeStruct((5, ny, nz), jnp.bfloat16)
    face_across, face_beside = pl.pallas_call(
        faces_kernel,
        out_shape=(faces, faces),
        in_specs=[pl.BlockSpec(memory_space=pl.ANY)] * 2,
        out_specs=tuple(in_vmem(2)),
        scratch_shapes=[
            pltpu.VMEM((2, 5, ny, nz), jnp.float32),
            pltpu.SemaphoreType.DMA((2, 2)),
        ],
        name="faces",
    )(f, u)
    own = (
        entry_matrix_first[0],
        hidden_matrix_second[0],
        final_readout_matrix[0],
        electrical_zone_offset,
    )
    face_across, *later = lax.optimization_barrier((face_across, *own))
    x_across = lax.ppermute(face_across, length, across)
    x_beside = lax.ppermute(face_beside, length, beside)
    other = tuple(lax.ppermute(w, "core", [(0, 1), (1, 0)]) for w in later)
    x_across, x_beside, *other = lax.optimization_barrier((x_across, x_beside, *other))
    first_y = [(i, i ^ 1) for i in range(n_gy)]
    then_y = [(i, i + 1) for i in range(1, n_gy - 1, 2)] + [(i + 1, i) for i in range(1, n_gy - 1, 2)]
    below = jnp.where(odd_x == 1, x_beside[1:2], x_across[1:2])
    above = jnp.where(odd_x == 1, x_across[0:1], x_beside[0:1])

    def face_y(high):
        edge, next_edge = high * (ny - 1), high * (ny - 3) + 1
        at = lambda a, i: lax.dynamic_index_in_dim(a, i, a.ndim - 2, False)
        own = at(f, edge).astype(jnp.bfloat16)
        near = jnp.concatenate([at(below, edge), own, at(above, edge)], axis=0)
        near = jnp.pad(near, ((0, 16 - near.shape[0]), (0, 0)))
        rest = jnp.concatenate([at(f, next_edge), at(u, edge).reshape(3 * nx, nz)], axis=0)
        return jnp.concatenate([near, rest.astype(jnp.bfloat16)], axis=0)

    y_then = lax.ppermute(face_y(odd_y), "z", then_y)
    y_first = lax.ppermute(face_y(1 - odd_y), "z", first_y)
    inside = jnp.stack(
        [gx > 0, gx < n_gx - 1, gy > 0, gy < n_gy - 1, odd_x == 1, odd_y == 1]
    ).astype(jnp.int32)

    peers = intake_source_tile.shape[1]
    smem = pl.BlockSpec(memory_space=pltpu.SMEM)
    interior, edges, picks, sides, zone_rows, outlets = pl.pallas_call(
        interior_kernel,
        out_shape=(
            jax.ShapeDtypeStruct((nx * ny, nz), jnp.float32),
            jax.ShapeDtypeStruct((20, nx + 8, nz), jnp.float32),
            jax.ShapeDtypeStruct((peers * SLOTS, 2 * CELLS), jnp.bfloat16),
            jax.ShapeDtypeStruct((peers * SLOTS, CELLS), jnp.bfloat16),
            jax.ShapeDtypeStruct((peers // 2, 8, CELLS), jnp.bfloat16),
            jax.ShapeDtypeStruct((2, peers // 8, CELLS), jnp.int32),
        ),
        in_specs=[smem] + in_vmem(8),
        out_specs=tuple(in_vmem(6)),
        scratch_shapes=[
            pltpu.VMEM((nx + 4, ny + 16, nz), jnp.float32),
            pltpu.VMEM((nx + 2, ny + 16, nz), jnp.float32),
            pltpu.VMEM((peers * 4, CELLS), jnp.float32),
            pltpu.VMEM((peers * 4, CELLS), jnp.float32),
            pltpu.VMEM((peers, CELLS), jnp.float32),
        ],
        compiler_params=pltpu.CompilerParams(vmem_limit_bytes=40 * 1024 * 1024),
        cost_estimate=pl.CostEstimate(flops=4 * 10**9, bytes_accessed=8 * 10**6, transcendentals=0),
        name="interior",
    )(
        inside,
        f,
        u,
        x_across,
        x_beside,
        jnp.transpose(intake_source_tile[0]),
        jnp.transpose(machine_electrical_zone[0]),
        jnp.transpose(exhaust_source_tile[0]),
        machine_tally_matrix,
    )
    warmed, message = pl.pallas_call(
        field_kernel,
        out_shape=(
            jax.ShapeDtypeStruct((nx * ny, nz), jnp.float32),
            jax.ShapeDtypeStruct((peers // 2, MESSAGE_ROWS, CELLS), jnp.bfloat16),
        ),
        in_specs=[smem] + in_vmem(7),
        out_specs=tuple(in_vmem(2)),
        compiler_params=pltpu.CompilerParams(vmem_limit_bytes=40 * 1024 * 1024),
        name="field",
    )(inside, y_then, y_first, edges, picks, sides, zone_rows, interior)

    half = ("y", "x", "z")
    arrived = lax.all_to_all(message, half, split_axis=0, concat_axis=0, tiled=True)
    heat = pl.pallas_call(
        surrogate_kernel,
        out_shape=jax.ShapeDtypeStruct((peers // 2, HEAD_ROWS, CELLS), jnp.bfloat16),
        in_specs=in_vmem(9),
        out_specs=in_vmem(1)[0],
        scratch_shapes=[
            pltpu.VMEM((2, 2 * CELLS, entry_matrix_first.shape[2]), jnp.bfloat16),
        ],
        compiler_params=pltpu.CompilerParams(vmem_limit_bytes=40 * 1024 * 1024),
        name="surrogate",
    )(arrived, *own, *other)
    returned = lax.all_to_all(heat, half, split_axis=0, concat_axis=0, tiled=True)

    final = pl.pallas_call(
        exhaust_kernel,
        out_shape=jax.ShapeDtypeStruct((nx * ny, nz), jnp.float32),
        in_specs=in_vmem(3),
        out_specs=in_vmem(1)[0],
        compiler_params=pltpu.CompilerParams(vmem_limit_bytes=40 * 1024 * 1024),
        name="exhaust",
    )(warmed, returned.reshape(peers * SLOTS, CELLS), outlets)
    return final.reshape(nx, ny, nz)


def solution(mesh):
    devices = mesh.devices
    split = Mesh(devices.reshape(4, 4, 2, devices.shape[1]), ("y", "x", "core", "z"))
    length = ("y", "x", "core")
    every = length + ("z",)
    return jax.shard_map(
        shards,
        mesh=split,
        in_specs=(
            P(length, "z", None),
            P(None, length, "z", None),
            P(every, None, None),
            P(every, None, None),
            P(every, None, None),
            P(every, None),
            P(every, None, None),
            P(every, None, None),
            P(every, None),
            P(every, None, None),
        ),
        out_specs=P(length, "z", None),
        check_vma=False,
    )
```

```python
import jax
import jax.numpy as jnp
from jax import lax
from jax.experimental import pallas as pl
from jax.experimental.pallas import tpu as pltpu
from jax.sharding import Mesh
from jax.sharding import PartitionSpec as P

time_step = 0.1
diffusivity = 0.5
buoyancy = 0.5

CELLS = 128
SLOTS = 32
ZONES = 16
HEAD_ROWS = 2 * SLOTS
MESSAGE_ROWS = HEAD_ROWS + 8
ROWS_STEP = 16


def advance(center, east, west, north, south, u0, u1, u2):
    lanes = center.shape[1]
    lane = lax.broadcasted_iota(jnp.int32, center.shape, 1)
    upper = jnp.where(lane == lanes - 1, 0.0, pltpu.roll(center, lanes - 1, 1))
    lower = jnp.where(lane == 0, 0.0, pltpu.roll(center, 1, 1))
    laplace = east + west + north + south + upper + lower - 6.0 * center
    transport = u0 * (east - west) + u1 * (north - south)
    transport = transport + (u2 + buoyancy * center) * (upper - lower)
    return center + time_step * (diffusivity * laplace - 0.5 * transport)


def by_core(table, odd_core):
    columns = table.shape[1]
    lane = lax.broadcasted_iota(jnp.int32, table.shape, 1)
    later, earlier = pltpu.roll(table, columns - 4, 1), pltpu.roll(table, 4, 1)
    return jnp.where(odd_core, jnp.where((lane & 4) == 0, later, earlier), table)


def faces_kernel(f_ref, u_ref, across_ref, beside_ref, held_ref, sems):
    nx = f_ref.shape[0]
    odd = lax.axis_index("core")
    copies = []
    for k, high in enumerate((odd, 1 - odd)):
        copies.append(
            (
                pltpu.make_async_copy(
                    f_ref.at[pl.ds(high * (nx - 2), 2)], held_ref.at[k, pl.ds(0, 2)], sems.at[k, 0]
                ),
                pltpu.make_async_copy(
                    u_ref.at[:, high * (nx - 1)], held_ref.at[k, pl.ds(2, 3)], sems.at[k, 1]
                ),
            )
        )
    for pair in copies:
        for copy in pair:
            copy.start()
    for k, ref in enumerate((across_ref, beside_ref)):
        for copy in copies[k]:
            copy.wait()
        ref[...] = held_ref[k].astype(jnp.bfloat16)


def interior_part(
    inside_ref,
    f_ref,
    u_ref,
    x_across_ref,
    x_beside_ref,
    intake_ref,
    zone_ref,
    warmed_ref,
    edge_ref,
    pick_ref,
    side_ref,
    zone_out_ref,
    first_ref,
    second_ref,
    hot_ref,
    zone_rows_ref,
):
    nx, ny, nz = f_ref.shape
    top = 8
    bottom = top + ny
    odd_x = inside_ref[4] > 0
    x_across = x_across_ref[...].astype(jnp.float32)
    x_beside = x_beside_ref[...].astype(jnp.float32)
    xlo, xhi = jnp.where(odd_x, x_beside, x_across), jnp.where(odd_x, x_across, x_beside)
    first_ref[0:2, top:bottom, :] = xlo[0:2]
    first_ref[2 : nx + 2, top:bottom, :] = f_ref[...]
    first_ref[nx + 2 : nx + 4, top:bottom, :] = xhi[0:2]
    for ref in (first_ref, second_ref):
        ref[:, top - 8 : top, :] = jnp.zeros((ref.shape[0], 8, nz), jnp.float32)
        ref[:, bottom : bottom + 8, :] = jnp.zeros((ref.shape[0], 8, nz), jnp.float32)

    def slab(ref, at, u0, u1, u2):
        return advance(
            ref[at, top:bottom, :],
            ref[at + 1, top:bottom, :],
            ref[at - 1, top:bottom, :],
            ref[at, top + 1 : bottom + 1, :],
            ref[at, top - 1 : bottom - 1, :],
            u0,
            u1,
            u2,
        )

    for x in range(nx):
        second_ref[x + 1, top:bottom, :] = slab(first_ref, x + 2, u_ref[0, x], u_ref[1, x], u_ref[2, x])
    west_face = slab(first_ref, 1, xlo[2], xlo[3], xlo[4])
    second_ref[0, top:bottom, :] = jnp.where(inside_ref[0] > 0, west_face, 0.0)
    east_face = slab(first_ref, nx + 2, xhi[2], xhi[3], xhi[4])
    second_ref[nx + 1, top:bottom, :] = jnp.where(inside_ref[1] > 0, east_face, 0.0)
    for x in range(nx):
        warmed_ref[x * ny : (x + 1) * ny, :] = slab(
            second_ref, x + 1, u_ref[0, x], u_ref[1, x], u_ref[2, x]
        )

    gap = jnp.zeros((1, nz), jnp.float32)
    rest = jnp.zeros((4, nz), jnp.float32)

    def keep(k, rows):
        edge_ref[k] = jnp.concatenate(rows + [rest], axis=0)

    for side, (y, inner, innermost) in enumerate(((0, 1, 2), (ny - 1, ny - 2, ny - 3))):
        at = side * 10
        cells = lambda ref, y, first, last: [ref[x, top + y : top + y + 1, :] for x in range(first, last)]
        keep(at, cells(first_ref, y, 0, nx + 4))
        keep(at + 1, cells(first_ref, inner, 0, nx + 4))
        keep(at + 2, [gap] + cells(second_ref, inner, 0, nx + 2) + [gap])
        keep(at + 3, [gap] + cells(second_ref, innermost, 0, nx + 2) + [gap])
        for k in range(3):
            wind = [u_ref[k, x, y : y + 1, :] for x in range(nx)]
            keep(at + 4 + k, [gap, xlo[2 + k, y : y + 1]] + wind + [xhi[2 + k, y : y + 1], gap])
            wind = [u_ref[k, x, inner : inner + 1, :] for x in range(nx)]
            keep(at + 7 + k, [gap, gap] + wind + [gap, gap])

    peers = intake_ref.shape[1]
    zones = jnp.transpose(by_core(zone_ref[...], odd_x).astype(jnp.float32)).astype(jnp.bfloat16)
    groups = SLOTS // 8
    wide = groups * CELLS
    slot = lax.broadcasted_iota(jnp.int32, (SLOTS, wide), 0)
    lane = lax.broadcasted_iota(jnp.int32, (SLOTS, wide), 1)
    spread = (lane // ZONES == slot).astype(jnp.float32).astype(jnp.bfloat16)
    zone_wide = jnp.dot(zones, spread, preferred_element_type=jnp.float32)
    which = lax.broadcasted_iota(jnp.int32, (peers, wide), 1) % ZONES
    hot = (zone_wide == which.astype(jnp.float32)).astype(jnp.float32)
    for j in range(groups):
        hot_ref[j * peers : (j + 1) * peers, :] = hot[:, j * CELLS : (j + 1) * CELLS]
    for z in range(4):
        for turn in range(2):
            for j in range(groups):
                zone_rows_ref[pl.ds(z * 8 + turn * 4 + j, peers // 8, stride=32), :] = hot_ref[
                    pl.ds(j * peers + turn * 4 + z, peers // 8, stride=8), :
                ]
    zone_out_ref[...] = zone_rows_ref[...].astype(jnp.bfloat16).reshape(peers // 2, 8, CELLS)

    intake = by_core(intake_ref[...], odd_x)
    lane = lax.broadcasted_iota(jnp.int32, (SLOTS, CELLS), 1)
    one, none = jnp.float32(1), jnp.float32(0)
    for d in range(peers):
        block = jnp.broadcast_to(intake[:, d : d + 1], (SLOTS, CELLS))
        row = block >> 1
        span = slice(d * SLOTS, (d + 1) * SLOTS)
        pick_ref[span, :CELLS] = jnp.where(row == lane, one, none).astype(jnp.bfloat16)
        pick_ref[span, CELLS:] = jnp.where(row == lane + CELLS, one, none).astype(jnp.bfloat16)
        side_ref[span, :] = (block & 1).astype(jnp.float32).astype(jnp.bfloat16)


def interior_kernel(*refs):
    given, (outlet_ref, tally_ref), made, lanes_ref = refs[:7], refs[7:9], refs[9:14], refs[14]
    scratch, turned_ref = refs[15:19], refs[19]
    odd_core = refs[0][4] > 0

    @pl.when(odd_core)
    def _():
        interior_part(*given, *made, *scratch)

    for zh, half in enumerate(outlet_lanes(odd_core, outlet_ref, tally_ref, turned_ref)):
        lanes_ref[zh] = half


def finish_part(
    inside_ref,
    y_then_ref,
    y_first_ref,
    interior_ref,
    edge_ref,
    pick_ref,
    side_ref,
    zone_ref,
    warmed_ref,
    message_ref,
):
    nx = (edge_ref.shape[1] - 4) - 4
    ny = interior_ref.shape[0] // nx
    odd_y = inside_ref[5] > 0
    y_first = y_first_ref[...].astype(jnp.float32)
    y_then = y_then_ref[...].astype(jnp.float32)
    ylo, yhi = jnp.where(odd_y, y_first, y_then), jnp.where(odd_y, y_then, y_first)
    warmed_ref[...] = interior_ref[...]
    spot = lax.broadcasted_iota(jnp.int32, (nx + 2, edge_ref.shape[2]), 0)
    west = jnp.logical_and(spot == 0, inside_ref[0] == 0)
    east = jnp.logical_and(spot == nx + 1, inside_ref[1] == 0)
    outside = jnp.logical_or(west, east)
    for side, halo in enumerate((ylo, yhi)):
        at = side * 10
        def step(center, inward, outward, wind, first, last):
            middle = center[first:last]
            north, south = (inward, outward) if side == 0 else (outward, inward)
            return advance(
                middle, center[first + 1 : last + 1], center[first - 1 : last - 1], north, south, *wind
            )

        wind = [halo[24 + 8 * k : 32 + 8 * k] for k in range(3)]
        beyond = step(halo, edge_ref[at, 2 : nx + 2], halo[16 : 16 + nx], wind, 1, nx + 1)
        beyond = jnp.where(inside_ref[2 + side] > 0, beyond, 0.0)
        wind = [edge_ref[at + 4 + k] for k in range(3)]
        near = step(
            edge_ref[at],
            edge_ref[at + 1, 1 : nx + 3],
            halo[0 : nx + 2],
            [w[1 : nx + 3] for w in wind],
            1,
            nx + 3,
        )
        near = jnp.where(outside, 0.0, near)
        inner, innermost = edge_ref[at + 2], edge_ref[at + 3]
        outer_row = step(near, inner[2 : nx + 2], beyond, [w[2 : nx + 2] for w in wind], 1, nx + 1)
        wind = [edge_ref[at + 7 + k, 2 : nx + 2] for k in range(3)]
        inner_row = step(inner, innermost[2 : nx + 2], near[1 : nx + 1], wind, 2, nx + 2)
        rows = (outer_row, inner_row) if side == 0 else (inner_row, outer_row)
        for x in range(nx):
            y = x * ny + side * (ny - 2)
            warmed_ref[y : y + 1, :] = rows[0][x : x + 1]
            warmed_ref[y + 1 : y + 2, :] = rows[1][x : x + 1]

    message_ref[:, HEAD_ROWS:MESSAGE_ROWS, :] = zone_ref[...]
    brick = warmed_ref[...].astype(jnp.bfloat16)
    group = 8 * SLOTS
    for start in range(0, pick_ref.shape[0], group):
        span = slice(start, start + group)
        pair = jnp.dot(pick_ref[span, :], brick, preferred_element_type=jnp.float32)
        pair = pair.astype(jnp.bfloat16)
        rows = jnp.where(side_ref[span, :] > 0, pair[:, CELLS:], pair[:, :CELLS])
        peer = start // HEAD_ROWS
        for k in range(8):
            at = k // 4 * SLOTS
            message_ref[peer + k % 4, at : at + SLOTS, :] = rows[k * SLOTS : (k + 1) * SLOTS]


def field_kernel(*refs):
    given, faces, early, out = refs[:7], refs[7:9], refs[9:14], refs[14:16]
    late, scratch = refs[16:21], refs[21:]
    inside_ref = refs[0]

    @pl.when(inside_ref[4] > 0)
    def _():
        finish_part(inside_ref, *faces, *early, *out)

    @pl.when(inside_ref[4] == 0)
    def _():
        interior_part(*given, *late, *scratch)
        finish_part(inside_ref, *faces, *late, *out)


def outlet_lanes(odd_core, outlet_ref, tally_ref, turned_ref):
    slots, peers = outlet_ref.shape
    slot = lax.broadcasted_iota(jnp.int32, outlet_ref.shape, 0)
    outlet = jnp.where(slot < tally_ref[...], outlet_ref[...], -1)
    outlet = by_core(outlet, odd_core).astype(jnp.float32)
    turned_ref[...] = jnp.concatenate(
        [jnp.transpose(outlet), jnp.zeros((peers, CELLS - slots), jnp.float32)], axis=1
    )
    halves = []
    for zh in range(2):
        lanes = 0.0
        for q in range(4):
            part = turned_ref[pl.ds(2 * zh + q // 2 + 4 * (q % 2), peers // 8, stride=8), :]
            lanes = lanes + (pltpu.roll(part, q * slots, 1) if q else part)
        halves.append(lanes.astype(jnp.int32))
    return halves


def surrogate_kernel(
    message_ref,
    first_ref,
    second_ref,
    last_ref,
    offset_ref,
    first_other_ref,
    second_other_ref,
    last_other_ref,
    offset_other_ref,
    heat_ref,
    entry_ref,
):
    peers = message_ref.shape[0]
    sub = lax.broadcasted_iota(jnp.int32, (8, CELLS), 0)
    lane = lax.broadcasted_iota(jnp.int32, (8, CELLS), 1)
    mine = (lane // ZONES == sub).astype(jnp.float32)

    def silu(x):
        half = 0.5 * x
        return (half + half * jnp.tanh(half)).astype(jnp.bfloat16)

    other = (first_other_ref, second_other_ref, last_other_ref, offset_other_ref)
    own = (first_ref, second_ref, last_ref, offset_ref)
    for turn, (entry, middle, last, offset) in enumerate((own, other)):
        entry_ref[turn, 0:CELLS, :] = entry[...]
        for k in range(CELLS // ZONES):
            entry_ref[turn, CELLS + k * ZONES : CELLS + (k + 1) * ZONES, :] = offset[...]
        slots = slice(turn * SLOTS, (turn + 1) * SLOTS)
        for at in range(0, peers, ROWS_STEP):
            rows = message_ref[at : at + ROWS_STEP, slots, :].reshape(ROWS_STEP * SLOTS, CELLS)
            zone = message_ref[at : at + ROWS_STEP, HEAD_ROWS:MESSAGE_ROWS, :].astype(jnp.float32)
            hots = [
                jnp.broadcast_to(zone[s, j : j + 1, :], (8, CELLS)) * mine
                for s in range(ROWS_STEP)
                for j in range(turn * 4, turn * 4 + 4)
            ]
            hot = jnp.concatenate(hots, axis=0).astype(jnp.bfloat16)
            inputs = jnp.concatenate([rows, hot], axis=1)
            hidden = silu(jnp.dot(inputs, entry_ref[turn], preferred_element_type=jnp.float32))
            second = silu(jnp.dot(hidden, middle[...], preferred_element_type=jnp.float32))
            heat = jnp.dot(second, last[...], preferred_element_type=jnp.float32)
            heat_ref[at : at + ROWS_STEP, slots, :] = heat.astype(jnp.bfloat16).reshape(
                ROWS_STEP, SLOTS, CELLS
            )


def exhaust_kernel(warmed_ref, heat_ref, outlet_ref, out_ref):
    rows = warmed_ref.shape[0]
    halves, chunks = outlet_ref.shape[:2]
    place = lax.broadcasted_iota(jnp.int32, (rows, CELLS), 0)
    one, none = jnp.float32(1), jnp.float32(0)
    blocks, odds = [], []
    for zh in range(halves):
        outlet = outlet_ref[zh]
        blocks.append(outlet >> 1)
        odd = (outlet & 1).astype(jnp.float32)
        odds.append(jnp.transpose(jnp.concatenate([odd] * (CELLS // chunks), axis=0)))
    total = warmed_ref[...]
    step = 4
    for start in range(0, chunks, step):
        hits, sides = [], []
        for yx in range(start, start + step):
            for zh in range(halves):
                hit = jnp.where(place == blocks[zh][yx : yx + 1], one, none)
                hits.append(hit.astype(jnp.bfloat16))
                side = jnp.broadcast_to(odds[zh][:, yx : yx + 1], (CELLS, CELLS))
                sides.append(side.astype(jnp.bfloat16))
        heat = heat_ref[start * halves * CELLS : (start + step) * halves * CELLS, :]
        second = heat * jnp.concatenate(sides, axis=0)
        total = total + jnp.dot(
            jnp.concatenate(hits, axis=1),
            jnp.concatenate([heat - second, second], axis=1),
            preferred_element_type=jnp.float32,
        )
    out_ref[...] = total


def in_vmem(count):
    return [pl.BlockSpec(memory_space=pltpu.VMEM)] * count


def shards(
    thermal_anomaly_field,
    airflow_vector_field,
    entry_matrix_first,
    hidden_matrix_second,
    final_readout_matrix,
    electrical_zone_offset,
    intake_source_tile,
    machine_electrical_zone,
    machine_tally_matrix,
    exhaust_source_tile,
):
    f = thermal_anomaly_field
    u = airflow_vector_field
    nx, ny, nz = f.shape
    length = ("y", "x", "core")
    gx, gy = lax.axis_index(length), lax.axis_index("z")
    n_gx, n_gy = lax.axis_size(length), lax.axis_size("z")
    odd_x, odd_y = lax.axis_index("core"), gy % 2
    across = [(i, i + 1) for i in range(1, n_gx - 1, 2)] + [(i + 1, i) for i in range(1, n_gx - 1, 2)]
    beside = [(i, i ^ 1) for i in range(n_gx)]

    faces = jax.ShapeDtypeStruct((5, ny, nz), jnp.bfloat16)
    face_across, face_beside = pl.pallas_call(
        faces_kernel,
        out_shape=(faces, faces),
        in_specs=[pl.BlockSpec(memory_space=pl.ANY)] * 2,
        out_specs=tuple(in_vmem(2)),
        scratch_shapes=[
            pltpu.VMEM((2, 5, ny, nz), jnp.float32),
            pltpu.SemaphoreType.DMA((2, 2)),
        ],
        name="faces",
    )(f, u)
    own = (
        entry_matrix_first[0],
        hidden_matrix_second[0],
        final_readout_matrix[0],
        electrical_zone_offset,
    )
    face_across, *later = lax.optimization_barrier((face_across, *own))
    x_across = lax.ppermute(face_across, length, across)
    x_beside = lax.ppermute(face_beside, length, beside)
    other = tuple(lax.ppermute(w, "core", [(0, 1), (1, 0)]) for w in later)
    first_y = [(i, i ^ 1) for i in range(n_gy)]
    then_y = [(i, i + 1) for i in range(1, n_gy - 1, 2)] + [(i + 1, i) for i in range(1, n_gy - 1, 2)]
    below = jnp.where(odd_x == 1, x_beside[1:2], x_across[1:2])
    above = jnp.where(odd_x == 1, x_across[0:1], x_beside[0:1])

    def face_y(high):
        edge, next_edge = high * (ny - 1), high * (ny - 3) + 1
        at = lambda a, i: lax.dynamic_index_in_dim(a, i, a.ndim - 2, False)
        own = at(f, edge).astype(jnp.bfloat16)
        near = jnp.concatenate([at(below, edge), own, at(above, edge)], axis=0)
        near = jnp.pad(near, ((0, 16 - near.shape[0]), (0, 0)))
        rest = jnp.concatenate([at(f, next_edge), at(u, edge).reshape(3 * nx, nz)], axis=0)
        return jnp.concatenate([near, rest.astype(jnp.bfloat16)], axis=0)

    y_then = lax.ppermute(face_y(odd_y), "z", then_y)
    y_first = lax.ppermute(face_y(1 - odd_y), "z", first_y)
    inside = jnp.stack(
        [gx > 0, gx < n_gx - 1, gy > 0, gy < n_gy - 1, odd_x == 1, odd_y == 1]
    ).astype(jnp.int32)

    peers = intake_source_tile.shape[1]
    y_then, y_first, *other = lax.optimization_barrier((y_then, y_first, *other))
    smem = pl.BlockSpec(memory_space=pltpu.SMEM)
    interior = (
        jax.ShapeDtypeStruct((nx * ny, nz), jnp.float32),
        jax.ShapeDtypeStruct((20, nx + 8, nz), jnp.float32),
        jax.ShapeDtypeStruct((peers * SLOTS, 2 * CELLS), jnp.bfloat16),
        jax.ShapeDtypeStruct((peers * SLOTS, CELLS), jnp.bfloat16),
        jax.ShapeDtypeStruct((peers // 2, 8, CELLS), jnp.bfloat16),
    )
    scratch = [
        pltpu.VMEM((nx + 4, ny + 16, nz), jnp.float32),
        pltpu.VMEM((nx + 2, ny + 16, nz), jnp.float32),
        pltpu.VMEM((peers * 4, CELLS), jnp.float32),
        pltpu.VMEM((peers * 4, CELLS), jnp.float32),
    ]
    given = (
        inside,
        f,
        u,
        x_across,
        x_beside,
        jnp.transpose(intake_source_tile[0]),
        jnp.transpose(machine_electrical_zone[0]),
    )
    *early, outlets = pl.pallas_call(
        interior_kernel,
        out_shape=(*interior, jax.ShapeDtypeStruct((2, peers // 8, CELLS), jnp.int32)),
        in_specs=[smem] + in_vmem(8),
        out_specs=tuple(in_vmem(6)),
        scratch_shapes=scratch + [pltpu.VMEM((peers, CELLS), jnp.float32)],
        compiler_params=pltpu.CompilerParams(vmem_limit_bytes=40 * 1024 * 1024),
        cost_estimate=pl.CostEstimate(flops=4 * 10**9, bytes_accessed=8 * 10**6, transcendentals=0),
        name="interior",
    )(*given, jnp.transpose(exhaust_source_tile[0]), machine_tally_matrix)
    warmed, message = pl.pallas_call(
        field_kernel,
        out_shape=(
            jax.ShapeDtypeStruct((nx * ny, nz), jnp.float32),
            jax.ShapeDtypeStruct((peers // 2, MESSAGE_ROWS, CELLS), jnp.bfloat16),
        ),
        in_specs=[smem] + in_vmem(13),
        out_specs=tuple(in_vmem(2)),
        scratch_shapes=[pltpu.VMEM(a.shape, a.dtype) for a in interior] + scratch,
        compiler_params=pltpu.CompilerParams(vmem_limit_bytes=40 * 1024 * 1024),
        name="field",
    )(*given, y_then, y_first, *early)

    half = ("y", "x", "z")
    arrived = lax.all_to_all(message, half, split_axis=0, concat_axis=0, tiled=True)
    heat = pl.pallas_call(
        surrogate_kernel,
        out_shape=jax.ShapeDtypeStruct((peers // 2, HEAD_ROWS, CELLS), jnp.bfloat16),
        in_specs=in_vmem(9),
        out_specs=in_vmem(1)[0],
        scratch_shapes=[
            pltpu.VMEM((2, 2 * CELLS, entry_matrix_first.shape[2]), jnp.bfloat16),
        ],
        compiler_params=pltpu.CompilerParams(vmem_limit_bytes=40 * 1024 * 1024),
        name="surrogate",
    )(arrived, *own, *other)
    returned = lax.all_to_all(heat, half, split_axis=0, concat_axis=0, tiled=True)

    final = pl.pallas_call(
        exhaust_kernel,
        out_shape=jax.ShapeDtypeStruct((nx * ny, nz), jnp.float32),
        in_specs=in_vmem(3),
        out_specs=in_vmem(1)[0],
        compiler_params=pltpu.CompilerParams(vmem_limit_bytes=40 * 1024 * 1024),
        name="exhaust",
    )(warmed, returned.reshape(peers * SLOTS, CELLS), outlets)
    return final.reshape(nx, ny, nz)


def solution(mesh):
    devices = mesh.devices
    split = Mesh(devices.reshape(4, 4, 2, devices.shape[1]), ("y", "x", "core", "z"))
    length = ("y", "x", "core")
    every = length + ("z",)
    return jax.shard_map(
        shards,
        mesh=split,
        in_specs=(
            P(length, "z", None),
            P(None, length, "z", None),
            P(every, None, None),
            P(every, None, None),
            P(every, None, None),
            P(every, None),
            P(every, None, None),
            P(every, None, None),
            P(every, None),
            P(every, None, None),
        ),
        out_specs=P(length, "z", None),
        check_vma=False,
    )
```

```python
import jax
import jax.numpy as jnp
from jax import lax
from jax.experimental import pallas as pl
from jax.experimental.pallas import tpu as pltpu
from jax.sharding import Mesh
from jax.sharding import PartitionSpec as P

time_step = 0.1
diffusivity = 0.5
buoyancy = 0.5

CELLS = 128
SLOTS = 32
ZONES = 16
HEAD_ROWS = 2 * SLOTS
MESSAGE_ROWS = HEAD_ROWS + 8
ROWS_STEP = 16


def advance(center, east, west, north, south, u0, u1, u2):
    lanes = center.shape[1]
    lane = lax.broadcasted_iota(jnp.int32, center.shape, 1)
    upper = jnp.where(lane == lanes - 1, 0.0, pltpu.roll(center, lanes - 1, 1))
    lower = jnp.where(lane == 0, 0.0, pltpu.roll(center, 1, 1))
    laplace = east + west + north + south + upper + lower - 6.0 * center
    transport = u0 * (east - west) + u1 * (north - south)
    transport = transport + (u2 + buoyancy * center) * (upper - lower)
    return center + time_step * (diffusivity * laplace - 0.5 * transport)


def by_core(table, odd_core):
    columns = table.shape[1]
    lane = lax.broadcasted_iota(jnp.int32, table.shape, 1)
    later, earlier = pltpu.roll(table, columns - 4, 1), pltpu.roll(table, 4, 1)
    return jnp.where(odd_core, jnp.where((lane & 4) == 0, later, earlier), table)


def faces_kernel(f_ref, u_ref, across_ref, beside_ref, held_ref, sems):
    nx = f_ref.shape[0]
    odd = lax.axis_index("core")
    copies = []
    for k, high in enumerate((odd, 1 - odd)):
        copies.append(
            (
                pltpu.make_async_copy(
                    f_ref.at[pl.ds(high * (nx - 2), 2)], held_ref.at[k, pl.ds(0, 2)], sems.at[k, 0]
                ),
                pltpu.make_async_copy(
                    u_ref.at[:, high * (nx - 1)], held_ref.at[k, pl.ds(2, 3)], sems.at[k, 1]
                ),
            )
        )
    for pair in copies:
        for copy in pair:
            copy.start()
    for k, ref in enumerate((across_ref, beside_ref)):
        for copy in copies[k]:
            copy.wait()
        ref[...] = held_ref[k].astype(jnp.bfloat16)


def interior_part(
    inside_ref,
    f_ref,
    u_ref,
    x_across_ref,
    x_beside_ref,
    intake_ref,
    zone_ref,
    warmed_ref,
    edge_ref,
    pick_ref,
    side_ref,
    zone_out_ref,
    first_ref,
    second_ref,
    hot_ref,
    zone_rows_ref,
):
    nx, ny, nz = f_ref.shape
    top = 8
    bottom = top + ny
    odd_x = inside_ref[4] > 0
    x_across = x_across_ref[...].astype(jnp.float32)
    x_beside = x_beside_ref[...].astype(jnp.float32)
    xlo, xhi = jnp.where(odd_x, x_beside, x_across), jnp.where(odd_x, x_across, x_beside)
    first_ref[0:2, top:bottom, :] = xlo[0:2]
    first_ref[2 : nx + 2, top:bottom, :] = f_ref[...]
    first_ref[nx + 2 : nx + 4, top:bottom, :] = xhi[0:2]
    for ref in (first_ref, second_ref):
        ref[:, top - 8 : top, :] = jnp.zeros((ref.shape[0], 8, nz), jnp.float32)
        ref[:, bottom : bottom + 8, :] = jnp.zeros((ref.shape[0], 8, nz), jnp.float32)

    def slab(ref, at, u0, u1, u2):
        return advance(
            ref[at, top:bottom, :],
            ref[at + 1, top:bottom, :],
            ref[at - 1, top:bottom, :],
            ref[at, top + 1 : bottom + 1, :],
            ref[at, top - 1 : bottom - 1, :],
            u0,
            u1,
            u2,
        )

    for x in range(nx):
        second_ref[x + 1, top:bottom, :] = slab(first_ref, x + 2, u_ref[0, x], u_ref[1, x], u_ref[2, x])
    west_face = slab(first_ref, 1, xlo[2], xlo[3], xlo[4])
    second_ref[0, top:bottom, :] = jnp.where(inside_ref[0] > 0, west_face, 0.0)
    east_face = slab(first_ref, nx + 2, xhi[2], xhi[3], xhi[4])
    second_ref[nx + 1, top:bottom, :] = jnp.where(inside_ref[1] > 0, east_face, 0.0)
    for x in range(nx):
        warmed_ref[x * ny : (x + 1) * ny, :] = slab(
            second_ref, x + 1, u_ref[0, x], u_ref[1, x], u_ref[2, x]
        )

    gap = jnp.zeros((1, nz), jnp.float32)
    rest = jnp.zeros((4, nz), jnp.float32)

    def keep(k, rows):
        edge_ref[k] = jnp.concatenate(rows + [rest], axis=0)

    for side, (y, inner, innermost) in enumerate(((0, 1, 2), (ny - 1, ny - 2, ny - 3))):
        at = side * 10
        cells = lambda ref, y, first, last: [ref[x, top + y : top + y + 1, :] for x in range(first, last)]
        keep(at, cells(first_ref, y, 0, nx + 4))
        keep(at + 1, cells(first_ref, inner, 0, nx + 4))
        keep(at + 2, [gap] + cells(second_ref, inner, 0, nx + 2) + [gap])
        keep(at + 3, [gap] + cells(second_ref, innermost, 0, nx + 2) + [gap])
        for k in range(3):
            wind = [u_ref[k, x, y : y + 1, :] for x in range(nx)]
            keep(at + 4 + k, [gap, xlo[2 + k, y : y + 1]] + wind + [xhi[2 + k, y : y + 1], gap])
            wind = [u_ref[k, x, inner : inner + 1, :] for x in range(nx)]
            keep(at + 7 + k, [gap, gap] + wind + [gap, gap])

    peers = intake_ref.shape[1]
    zones = jnp.transpose(by_core(zone_ref[...], odd_x).astype(jnp.float32)).astype(jnp.bfloat16)
    groups = SLOTS // 8
    wide = groups * CELLS
    slot = lax.broadcasted_iota(jnp.int32, (SLOTS, wide), 0)
    lane = lax.broadcasted_iota(jnp.int32, (SLOTS, wide), 1)
    spread = (lane // ZONES == slot).astype(jnp.float32).astype(jnp.bfloat16)
    zone_wide = jnp.dot(zones, spread, preferred_element_type=jnp.float32)
    which = lax.broadcasted_iota(jnp.int32, (peers, wide), 1) % ZONES
    hot = (zone_wide == which.astype(jnp.float32)).astype(jnp.float32)
    for j in range(groups):
        hot_ref[j * peers : (j + 1) * peers, :] = hot[:, j * CELLS : (j + 1) * CELLS]
    for z in range(4):
        for turn in range(2):
            for j in range(groups):
                zone_rows_ref[pl.ds(z * 8 + turn * 4 + j, peers // 8, stride=32), :] = hot_ref[
                    pl.ds(j * peers + turn * 4 + z, peers // 8, stride=8), :
                ]
    zone_rows = zone_rows_ref[0 : peers * 4, :].astype(jnp.bfloat16)
    zone_out_ref[...] = zone_rows.reshape(peers // 2, 8, CELLS)

    intake = by_core(intake_ref[...], odd_x)
    lane = lax.broadcasted_iota(jnp.int32, (SLOTS, CELLS), 1)
    one, none = jnp.float32(1), jnp.float32(0)
    for d in range(peers):
        block = jnp.broadcast_to(intake[:, d : d + 1], (SLOTS, CELLS))
        row = block >> 1
        span = slice(d * SLOTS, (d + 1) * SLOTS)
        pick_ref[span, :CELLS] = jnp.where(row == lane, one, none).astype(jnp.bfloat16)
        pick_ref[span, CELLS:] = jnp.where(row == lane + CELLS, one, none).astype(jnp.bfloat16)
        side_ref[span, :] = (block & 1).astype(jnp.float32).astype(jnp.bfloat16)


def interior_kernel(*refs):
    given, (outlet_ref, tally_ref), made, lanes_ref = refs[:7], refs[7:9], refs[9:14], refs[14]
    scratch, turned_ref = refs[15:19], refs[19]
    odd_core = refs[0][4] > 0

    @pl.when(odd_core)
    def _():
        interior_part(*given, *made, *scratch)

    for zh, half in enumerate(outlet_lanes(odd_core, outlet_ref, tally_ref, turned_ref)):
        lanes_ref[zh] = half


def finish_part(
    inside_ref,
    y_then_ref,
    y_first_ref,
    interior_ref,
    edge_ref,
    pick_ref,
    side_ref,
    zone_ref,
    warmed_ref,
    message_ref,
):
    nx = (edge_ref.shape[1] - 4) - 4
    ny = interior_ref.shape[0] // nx
    odd_y = inside_ref[5] > 0
    y_first = y_first_ref[...].astype(jnp.float32)
    y_then = y_then_ref[...].astype(jnp.float32)
    ylo, yhi = jnp.where(odd_y, y_first, y_then), jnp.where(odd_y, y_then, y_first)
    warmed_ref[...] = interior_ref[...]
    spot = lax.broadcasted_iota(jnp.int32, (nx + 2, edge_ref.shape[2]), 0)
    west = jnp.logical_and(spot == 0, inside_ref[0] == 0)
    east = jnp.logical_and(spot == nx + 1, inside_ref[1] == 0)
    outside = jnp.logical_or(west, east)
    for side, halo in enumerate((ylo, yhi)):
        at = side * 10
        def step(center, inward, outward, wind, first, last):
            middle = center[first:last]
            north, south = (inward, outward) if side == 0 else (outward, inward)
            return advance(
                middle, center[first + 1 : last + 1], center[first - 1 : last - 1], north, south, *wind
            )

        wind = [halo[24 + 8 * k : 32 + 8 * k] for k in range(3)]
        beyond = step(halo, edge_ref[at, 2 : nx + 2], halo[16 : 16 + nx], wind, 1, nx + 1)
        beyond = jnp.where(inside_ref[2 + side] > 0, beyond, 0.0)
        wind = [edge_ref[at + 4 + k] for k in range(3)]
        near = step(
            edge_ref[at],
            edge_ref[at + 1, 1 : nx + 3],
            halo[0 : nx + 2],
            [w[1 : nx + 3] for w in wind],
            1,
            nx + 3,
        )
        near = jnp.where(outside, 0.0, near)
        inner, innermost = edge_ref[at + 2], edge_ref[at + 3]
        outer_row = step(near, inner[2 : nx + 2], beyond, [w[2 : nx + 2] for w in wind], 1, nx + 1)
        wind = [edge_ref[at + 7 + k, 2 : nx + 2] for k in range(3)]
        inner_row = step(inner, innermost[2 : nx + 2], near[1 : nx + 1], wind, 2, nx + 2)
        rows = (outer_row, inner_row) if side == 0 else (inner_row, outer_row)
        for x in range(nx):
            y = x * ny + side * (ny - 2)
            warmed_ref[y : y + 1, :] = rows[0][x : x + 1]
            warmed_ref[y + 1 : y + 2, :] = rows[1][x : x + 1]

    message_ref[:, HEAD_ROWS:MESSAGE_ROWS, :] = zone_ref[...]
    brick = warmed_ref[...].astype(jnp.bfloat16)
    group = 8 * SLOTS
    for start in range(0, pick_ref.shape[0], group):
        span = slice(start, start + group)
        pair = jnp.dot(pick_ref[span, :], brick, preferred_element_type=jnp.float32)
        pair = pair.astype(jnp.bfloat16)
        rows = jnp.where(side_ref[span, :] > 0, pair[:, CELLS:], pair[:, :CELLS])
        peer = start // HEAD_ROWS
        for k in range(8):
            at = k // 4 * SLOTS
            message_ref[peer + k % 4, at : at + SLOTS, :] = rows[k * SLOTS : (k + 1) * SLOTS]


def field_kernel(*refs):
    given, faces, early, out = refs[:7], refs[7:9], refs[9:14], refs[14:16]
    late, scratch = refs[16:21], refs[21:]
    inside_ref = refs[0]

    @pl.when(inside_ref[4] > 0)
    def _():
        finish_part(inside_ref, *faces, *early, *out)

    @pl.when(inside_ref[4] == 0)
    def _():
        interior_part(*given, *late, *scratch)
        finish_part(inside_ref, *faces, *late, *out)


def outlet_lanes(odd_core, outlet_ref, tally_ref, turned_ref):
    slots, peers = outlet_ref.shape
    slot = lax.broadcasted_iota(jnp.int32, outlet_ref.shape, 0)
    outlet = jnp.where(slot < tally_ref[...], outlet_ref[...], -1)
    outlet = by_core(outlet, odd_core).astype(jnp.float32)
    turned_ref[0:peers, :] = jnp.concatenate(
        [jnp.transpose(outlet), jnp.zeros((peers, CELLS - slots), jnp.float32)], axis=1
    )
    halves = []
    for zh in range(2):
        lanes = 0.0
        for q in range(4):
            part = turned_ref[pl.ds(2 * zh + q // 2 + 4 * (q % 2), peers // 8, stride=8), :]
            lanes = lanes + (pltpu.roll(part, q * slots, 1) if q else part)
        halves.append(lanes.astype(jnp.int32))
    return halves


def surrogate_kernel(
    message_ref,
    first_ref,
    second_ref,
    last_ref,
    offset_ref,
    first_other_ref,
    second_other_ref,
    last_other_ref,
    offset_other_ref,
    heat_ref,
    entry_ref,
):
    peers = message_ref.shape[0]
    sub = lax.broadcasted_iota(jnp.int32, (8, CELLS), 0)
    lane = lax.broadcasted_iota(jnp.int32, (8, CELLS), 1)
    mine = (lane // ZONES == sub).astype(jnp.float32)

    def silu(x):
        half = 0.5 * x
        return (half + half * jnp.tanh(half)).astype(jnp.bfloat16)

    other = (first_other_ref, second_other_ref, last_other_ref, offset_other_ref)
    own = (first_ref, second_ref, last_ref, offset_ref)
    for turn, (entry, middle, last, offset) in enumerate((own, other)):
        entry_ref[turn, 0:CELLS, :] = entry[...]
        for k in range(CELLS // ZONES):
            entry_ref[turn, CELLS + k * ZONES : CELLS + (k + 1) * ZONES, :] = offset[...]
        slots = slice(turn * SLOTS, (turn + 1) * SLOTS)
        for at in range(0, peers, ROWS_STEP):
            rows = message_ref[at : at + ROWS_STEP, slots, :].reshape(ROWS_STEP * SLOTS, CELLS)
            zone = message_ref[at : at + ROWS_STEP, HEAD_ROWS:MESSAGE_ROWS, :].astype(jnp.float32)
            hots = [
                jnp.broadcast_to(zone[s, j : j + 1, :], (8, CELLS)) * mine
                for s in range(ROWS_STEP)
                for j in range(turn * 4, turn * 4 + 4)
            ]
            hot = jnp.concatenate(hots, axis=0).astype(jnp.bfloat16)
            inputs = jnp.concatenate([rows, hot], axis=1)
            hidden = silu(jnp.dot(inputs, entry_ref[turn], preferred_element_type=jnp.float32))
            second = silu(jnp.dot(hidden, middle[...], preferred_element_type=jnp.float32))
            heat = jnp.dot(second, last[...], preferred_element_type=jnp.float32)
            heat_ref[at : at + ROWS_STEP, slots, :] = heat.astype(jnp.bfloat16).reshape(
                ROWS_STEP, SLOTS, CELLS
            )


def exhaust_kernel(warmed_ref, heat_ref, outlet_ref, out_ref):
    rows = warmed_ref.shape[0]
    halves, chunks = outlet_ref.shape[:2]
    place = lax.broadcasted_iota(jnp.int32, (rows, CELLS), 0)
    one, none = jnp.float32(1), jnp.float32(0)
    blocks, odds = [], []
    for zh in range(halves):
        outlet = outlet_ref[zh]
        blocks.append(outlet >> 1)
        odd = (outlet & 1).astype(jnp.float32)
        odds.append(jnp.transpose(jnp.concatenate([odd] * (CELLS // chunks), axis=0)))
    total = warmed_ref[...]
    step = 4
    for start in range(0, chunks, step):
        hits, sides = [], []
        for yx in range(start, start + step):
            for zh in range(halves):
                hit = jnp.where(place == blocks[zh][yx : yx + 1], one, none)
                hits.append(hit.astype(jnp.bfloat16))
                side = jnp.broadcast_to(odds[zh][:, yx : yx + 1], (CELLS, CELLS))
                sides.append(side.astype(jnp.bfloat16))
        heat = heat_ref[start * halves * CELLS : (start + step) * halves * CELLS, :]
        second = heat * jnp.concatenate(sides, axis=0)
        total = total + jnp.dot(
            jnp.concatenate(hits, axis=1),
            jnp.concatenate([heat - second, second], axis=1),
            preferred_element_type=jnp.float32,
        )
    out_ref[...] = total


def in_vmem(count):
    return [pl.BlockSpec(memory_space=pltpu.VMEM)] * count


def shards(
    thermal_anomaly_field,
    airflow_vector_field,
    entry_matrix_first,
    hidden_matrix_second,
    final_readout_matrix,
    electrical_zone_offset,
    intake_source_tile,
    machine_electrical_zone,
    machine_tally_matrix,
    exhaust_source_tile,
):
    f = thermal_anomaly_field
    u = airflow_vector_field
    nx, ny, nz = f.shape
    length = ("y", "x", "core")
    gx, gy = lax.axis_index(length), lax.axis_index("z")
    n_gx, n_gy = lax.axis_size(length), lax.axis_size("z")
    odd_x, odd_y = lax.axis_index("core"), gy % 2
    across = [(i, i + 1) for i in range(1, n_gx - 1, 2)] + [(i + 1, i) for i in range(1, n_gx - 1, 2)]
    beside = [(i, i ^ 1) for i in range(n_gx)]

    faces = jax.ShapeDtypeStruct((5, ny, nz), jnp.bfloat16)
    face_across, face_beside = pl.pallas_call(
        faces_kernel,
        out_shape=(faces, faces),
        in_specs=[pl.BlockSpec(memory_space=pl.ANY)] * 2,
        out_specs=tuple(in_vmem(2)),
        scratch_shapes=[
            pltpu.VMEM((2, 5, ny, nz), jnp.float32),
            pltpu.SemaphoreType.DMA((2, 2)),
        ],
        name="faces",
    )(f, u)
    own = (
        entry_matrix_first[0],
        hidden_matrix_second[0],
        final_readout_matrix[0],
        electrical_zone_offset,
    )
    face_across, *later = lax.optimization_barrier((face_across, *own))
    x_across = lax.ppermute(face_across, length, across)
    x_beside = lax.ppermute(face_beside, length, beside)
    other = tuple(lax.ppermute(w, "core", [(0, 1), (1, 0)]) for w in later)
    first_y = [(i, i ^ 1) for i in range(n_gy)]
    then_y = [(i, i + 1) for i in range(1, n_gy - 1, 2)] + [(i + 1, i) for i in range(1, n_gy - 1, 2)]
    below = jnp.where(odd_x == 1, x_beside[1:2], x_across[1:2])
    above = jnp.where(odd_x == 1, x_across[0:1], x_beside[0:1])

    def face_y(high):
        edge, next_edge = high * (ny - 1), high * (ny - 3) + 1
        at = lambda a, i: lax.dynamic_index_in_dim(a, i, a.ndim - 2, False)
        own = at(f, edge).astype(jnp.bfloat16)
        near = jnp.concatenate([at(below, edge), own, at(above, edge)], axis=0)
        near = jnp.pad(near, ((0, 16 - near.shape[0]), (0, 0)))
        rest = jnp.concatenate([at(f, next_edge), at(u, edge).reshape(3 * nx, nz)], axis=0)
        return jnp.concatenate([near, rest.astype(jnp.bfloat16)], axis=0)

    y_then = lax.ppermute(face_y(odd_y), "z", then_y)
    y_first = lax.ppermute(face_y(1 - odd_y), "z", first_y)
    inside = jnp.stack(
        [gx > 0, gx < n_gx - 1, gy > 0, gy < n_gy - 1, odd_x == 1, odd_y == 1]
    ).astype(jnp.int32)

    peers = intake_source_tile.shape[1]
    y_then, y_first, *other = lax.optimization_barrier((y_then, y_first, *other))
    smem = pl.BlockSpec(memory_space=pltpu.SMEM)
    interior = (
        jax.ShapeDtypeStruct((nx * ny, nz), jnp.float32),
        jax.ShapeDtypeStruct((20, nx + 8, nz), jnp.float32),
        jax.ShapeDtypeStruct((peers * SLOTS, 2 * CELLS), jnp.bfloat16),
        jax.ShapeDtypeStruct((peers * SLOTS, CELLS), jnp.bfloat16),
        jax.ShapeDtypeStruct((peers // 2, 8, CELLS), jnp.bfloat16),
    )
    scratch = [
        pltpu.VMEM((nx + 4, ny + 16, nz), jnp.float32),
        pltpu.VMEM((nx + 2, ny + 16, nz), jnp.float32),
        pltpu.VMEM((peers * 4 + 8, CELLS), jnp.float32),
        pltpu.VMEM((peers * 4 + 32, CELLS), jnp.float32),
    ]
    given = (
        inside,
        f,
        u,
        x_across,
        x_beside,
        jnp.transpose(intake_source_tile[0]),
        jnp.transpose(machine_electrical_zone[0]),
    )
    *early, outlets = pl.pallas_call(
        interior_kernel,
        out_shape=(*interior, jax.ShapeDtypeStruct((2, peers // 8, CELLS), jnp.int32)),
        in_specs=[smem] + in_vmem(8),
        out_specs=tuple(in_vmem(6)),
        scratch_shapes=scratch + [pltpu.VMEM((peers + 8, CELLS), jnp.float32)],
        compiler_params=pltpu.CompilerParams(vmem_limit_bytes=40 * 1024 * 1024),
        cost_estimate=pl.CostEstimate(flops=4 * 10**9, bytes_accessed=8 * 10**6, transcendentals=0),
        name="interior",
    )(*given, jnp.transpose(exhaust_source_tile[0]), machine_tally_matrix)
    warmed, message = pl.pallas_call(
        field_kernel,
        out_shape=(
            jax.ShapeDtypeStruct((nx * ny, nz), jnp.float32),
            jax.ShapeDtypeStruct((peers // 2, MESSAGE_ROWS, CELLS), jnp.bfloat16),
        ),
        in_specs=[smem] + in_vmem(13),
        out_specs=tuple(in_vmem(2)),
        scratch_shapes=[pltpu.VMEM(a.shape, a.dtype) for a in interior] + scratch,
        compiler_params=pltpu.CompilerParams(vmem_limit_bytes=40 * 1024 * 1024),
        name="field",
    )(*given, y_then, y_first, *early)

    half = ("y", "x", "z")
    arrived = lax.all_to_all(message, half, split_axis=0, concat_axis=0, tiled=True)
    heat = pl.pallas_call(
        surrogate_kernel,
        out_shape=jax.ShapeDtypeStruct((peers // 2, HEAD_ROWS, CELLS), jnp.bfloat16),
        in_specs=in_vmem(9),
        out_specs=in_vmem(1)[0],
        scratch_shapes=[
            pltpu.VMEM((2, 2 * CELLS, entry_matrix_first.shape[2]), jnp.bfloat16),
        ],
        compiler_params=pltpu.CompilerParams(vmem_limit_bytes=40 * 1024 * 1024),
        name="surrogate",
    )(arrived, *own, *other)
    returned = lax.all_to_all(heat, half, split_axis=0, concat_axis=0, tiled=True)

    final = pl.pallas_call(
        exhaust_kernel,
        out_shape=jax.ShapeDtypeStruct((nx * ny, nz), jnp.float32),
        in_specs=in_vmem(3),
        out_specs=in_vmem(1)[0],
        compiler_params=pltpu.CompilerParams(vmem_limit_bytes=40 * 1024 * 1024),
        name="exhaust",
    )(warmed, returned.reshape(peers * SLOTS, CELLS), outlets)
    return final.reshape(nx, ny, nz)


def solution(mesh):
    devices = mesh.devices
    split = Mesh(devices.reshape(4, 4, 2, devices.shape[1]), ("y", "x", "core", "z"))
    length = ("y", "x", "core")
    every = length + ("z",)
    return jax.shard_map(
        shards,
        mesh=split,
        in_specs=(
            P(length, "z", None),
            P(None, length, "z", None),
            P(every, None, None),
            P(every, None, None),
            P(every, None, None),
            P(every, None),
            P(every, None, None),
            P(every, None, None),
            P(every, None),
            P(every, None, None),
        ),
        out_specs=P(length, "z", None),
        check_vma=False,
    )
```

```python
import jax
import jax.numpy as jnp
from jax import lax
from jax.experimental import pallas as pl
from jax.experimental.pallas import tpu as pltpu
from jax.sharding import Mesh
from jax.sharding import PartitionSpec as P

time_step = 0.1
diffusivity = 0.5
buoyancy = 0.5

CELLS = 128
SLOTS = 32
ZONES = 16
HEAD_ROWS = 2 * SLOTS
MESSAGE_ROWS = HEAD_ROWS + 8
ROWS_STEP = 16


def advance(center, east, west, north, south, u0, u1, u2):
    lanes = center.shape[1]
    lane = lax.broadcasted_iota(jnp.int32, center.shape, 1)
    upper = jnp.where(lane == lanes - 1, 0.0, pltpu.roll(center, lanes - 1, 1))
    lower = jnp.where(lane == 0, 0.0, pltpu.roll(center, 1, 1))
    laplace = east + west + north + south + upper + lower - 6.0 * center
    transport = u0 * (east - west) + u1 * (north - south)
    transport = transport + (u2 + buoyancy * center) * (upper - lower)
    return center + time_step * (diffusivity * laplace - 0.5 * transport)


def by_core(table, odd_core):
    columns = table.shape[1]
    lane = lax.broadcasted_iota(jnp.int32, table.shape, 1)
    later, earlier = pltpu.roll(table, columns - 4, 1), pltpu.roll(table, 4, 1)
    return jnp.where(odd_core, jnp.where((lane & 4) == 0, later, earlier), table)


def faces_kernel(f_ref, u_ref, across_ref, beside_ref, held_ref, sems):
    nx = f_ref.shape[0]
    odd = lax.axis_index("core")
    copies = []
    for k, high in enumerate((odd, 1 - odd)):
        copies.append(
            (
                pltpu.make_async_copy(
                    f_ref.at[pl.ds(high * (nx - 2), 2)], held_ref.at[k, pl.ds(0, 2)], sems.at[k, 0]
                ),
                pltpu.make_async_copy(
                    u_ref.at[:, high * (nx - 1)], held_ref.at[k, pl.ds(2, 3)], sems.at[k, 1]
                ),
            )
        )
    for pair in copies:
        for copy in pair:
            copy.start()
    for k, ref in enumerate((across_ref, beside_ref)):
        for copy in copies[k]:
            copy.wait()
        ref[...] = held_ref[k].astype(jnp.bfloat16)


def position():
    at = [lax.axis_index(axis) for axis in ("y", "x", "core", "z")]
    size = [lax.axis_size(axis) for axis in ("y", "x", "core", "z")]
    along = at[0] + at[1] + at[2]
    flags = (along > 0, along < sum(size[:3]) - 3, at[3] > 0, at[3] < size[3] - 1)
    return tuple(jnp.where(flag, 1, 0) for flag in flags) + (at[2], at[3] % 2)


def interior_part(
    inside,
    f_ref,
    u_ref,
    x_across_ref,
    x_beside_ref,
    intake_ref,
    zone_ref,
    warmed_ref,
    edge_ref,
    pick_ref,
    side_ref,
    zone_out_ref,
    first_ref,
    second_ref,
    hot_ref,
    zone_rows_ref,
):
    nx, ny, nz = f_ref.shape
    top = 8
    bottom = top + ny
    odd_x = inside[4] > 0
    x_across = x_across_ref[...].astype(jnp.float32)
    x_beside = x_beside_ref[...].astype(jnp.float32)
    xlo, xhi = jnp.where(odd_x, x_beside, x_across), jnp.where(odd_x, x_across, x_beside)
    first_ref[0:2, top:bottom, :] = xlo[0:2]
    first_ref[2 : nx + 2, top:bottom, :] = f_ref[...]
    first_ref[nx + 2 : nx + 4, top:bottom, :] = xhi[0:2]
    for ref in (first_ref, second_ref):
        ref[:, top - 8 : top, :] = jnp.zeros((ref.shape[0], 8, nz), jnp.float32)
        ref[:, bottom : bottom + 8, :] = jnp.zeros((ref.shape[0], 8, nz), jnp.float32)

    def slab(ref, at, u0, u1, u2):
        return advance(
            ref[at, top:bottom, :],
            ref[at + 1, top:bottom, :],
            ref[at - 1, top:bottom, :],
            ref[at, top + 1 : bottom + 1, :],
            ref[at, top - 1 : bottom - 1, :],
            u0,
            u1,
            u2,
        )

    for x in range(nx):
        second_ref[x + 1, top:bottom, :] = slab(first_ref, x + 2, u_ref[0, x], u_ref[1, x], u_ref[2, x])
    west_face = slab(first_ref, 1, xlo[2], xlo[3], xlo[4])
    second_ref[0, top:bottom, :] = jnp.where(inside[0] > 0, west_face, 0.0)
    east_face = slab(first_ref, nx + 2, xhi[2], xhi[3], xhi[4])
    second_ref[nx + 1, top:bottom, :] = jnp.where(inside[1] > 0, east_face, 0.0)
    for x in range(nx):
        warmed_ref[x * ny : (x + 1) * ny, :] = slab(
            second_ref, x + 1, u_ref[0, x], u_ref[1, x], u_ref[2, x]
        )

    gap = jnp.zeros((1, nz), jnp.float32)
    rest = jnp.zeros((4, nz), jnp.float32)

    def keep(k, rows):
        edge_ref[k] = jnp.concatenate(rows + [rest], axis=0)

    for side, (y, inner, innermost) in enumerate(((0, 1, 2), (ny - 1, ny - 2, ny - 3))):
        at = side * 10
        cells = lambda ref, y, first, last: [ref[x, top + y : top + y + 1, :] for x in range(first, last)]
        keep(at, cells(first_ref, y, 0, nx + 4))
        keep(at + 1, cells(first_ref, inner, 0, nx + 4))
        keep(at + 2, [gap] + cells(second_ref, inner, 0, nx + 2) + [gap])
        keep(at + 3, [gap] + cells(second_ref, innermost, 0, nx + 2) + [gap])
        for k in range(3):
            wind = [u_ref[k, x, y : y + 1, :] for x in range(nx)]
            keep(at + 4 + k, [gap, xlo[2 + k, y : y + 1]] + wind + [xhi[2 + k, y : y + 1], gap])
            wind = [u_ref[k, x, inner : inner + 1, :] for x in range(nx)]
            keep(at + 7 + k, [gap, gap] + wind + [gap, gap])

    peers = intake_ref.shape[1]
    zones = jnp.transpose(by_core(zone_ref[...], odd_x).astype(jnp.float32)).astype(jnp.bfloat16)
    groups = SLOTS // 8
    wide = groups * CELLS
    slot = lax.broadcasted_iota(jnp.int32, (SLOTS, wide), 0)
    lane = lax.broadcasted_iota(jnp.int32, (SLOTS, wide), 1)
    spread = (lane // ZONES == slot).astype(jnp.float32).astype(jnp.bfloat16)
    zone_wide = jnp.dot(zones, spread, preferred_element_type=jnp.float32)
    which = lax.broadcasted_iota(jnp.int32, (peers, wide), 1) % ZONES
    hot = (zone_wide == which.astype(jnp.float32)).astype(jnp.float32)
    for j in range(groups):
        hot_ref[j * peers : (j + 1) * peers, :] = hot[:, j * CELLS : (j + 1) * CELLS]
    for z in range(4):
        for turn in range(2):
            for j in range(groups):
                zone_rows_ref[pl.ds(z * 8 + turn * 4 + j, peers // 8, stride=32), :] = hot_ref[
                    pl.ds(j * peers + turn * 4 + z, peers // 8, stride=8), :
                ]
    zone_rows = zone_rows_ref[0 : peers * 4, :].astype(jnp.bfloat16)
    zone_out_ref[...] = zone_rows.reshape(peers // 2, 8, CELLS)

    intake = by_core(intake_ref[...], odd_x)
    lane = lax.broadcasted_iota(jnp.int32, (SLOTS, CELLS), 1)
    one, none = jnp.float32(1), jnp.float32(0)
    for d in range(peers):
        block = jnp.broadcast_to(intake[:, d : d + 1], (SLOTS, CELLS))
        row = block >> 1
        span = slice(d * SLOTS, (d + 1) * SLOTS)
        pick_ref[span, :CELLS] = jnp.where(row == lane, one, none).astype(jnp.bfloat16)
        pick_ref[span, CELLS:] = jnp.where(row == lane + CELLS, one, none).astype(jnp.bfloat16)
        side_ref[span, :] = (block & 1).astype(jnp.float32).astype(jnp.bfloat16)


def interior_kernel(*refs):
    inside = position()
    given, (outlet_ref, tally_ref), made, lanes_ref = refs[:6], refs[6:8], refs[8:13], refs[13]
    scratch, turned_ref = refs[14:18], refs[18]
    odd_core = inside[4] > 0

    @pl.when(odd_core)
    def _():
        interior_part(inside, *given, *made, *scratch)

    for zh, half in enumerate(outlet_lanes(odd_core, outlet_ref, tally_ref, turned_ref)):
        lanes_ref[zh] = half

    @pl.when(jnp.logical_not(odd_core))
    def _():
        outlet_hits(lanes_ref, made[2], made[3])


def finish_part(
    inside,
    y_then_ref,
    y_first_ref,
    interior_ref,
    edge_ref,
    pick_ref,
    side_ref,
    zone_ref,
    warmed_ref,
    message_ref,
):
    nx = (edge_ref.shape[1] - 4) - 4
    ny = interior_ref.shape[0] // nx
    odd_y = inside[5] > 0
    y_first = y_first_ref[...].astype(jnp.float32)
    y_then = y_then_ref[...].astype(jnp.float32)
    ylo, yhi = jnp.where(odd_y, y_first, y_then), jnp.where(odd_y, y_then, y_first)
    warmed_ref[...] = interior_ref[...]
    spot = lax.broadcasted_iota(jnp.int32, (nx + 2, edge_ref.shape[2]), 0)
    west = jnp.logical_and(spot == 0, inside[0] == 0)
    east = jnp.logical_and(spot == nx + 1, inside[1] == 0)
    outside = jnp.logical_or(west, east)
    for side, halo in enumerate((ylo, yhi)):
        at = side * 10
        def step(center, inward, outward, wind, first, last):
            middle = center[first:last]
            north, south = (inward, outward) if side == 0 else (outward, inward)
            return advance(
                middle, center[first + 1 : last + 1], center[first - 1 : last - 1], north, south, *wind
            )

        wind = [halo[24 + 8 * k : 32 + 8 * k] for k in range(3)]
        beyond = step(halo, edge_ref[at, 2 : nx + 2], halo[16 : 16 + nx], wind, 1, nx + 1)
        beyond = jnp.where(inside[2 + side] > 0, beyond, 0.0)
        wind = [edge_ref[at + 4 + k] for k in range(3)]
        near = step(
            edge_ref[at],
            edge_ref[at + 1, 1 : nx + 3],
            halo[0 : nx + 2],
            [w[1 : nx + 3] for w in wind],
            1,
            nx + 3,
        )
        near = jnp.where(outside, 0.0, near)
        inner, innermost = edge_ref[at + 2], edge_ref[at + 3]
        outer_row = step(near, inner[2 : nx + 2], beyond, [w[2 : nx + 2] for w in wind], 1, nx + 1)
        wind = [edge_ref[at + 7 + k, 2 : nx + 2] for k in range(3)]
        inner_row = step(inner, innermost[2 : nx + 2], near[1 : nx + 1], wind, 2, nx + 2)
        rows = (outer_row, inner_row) if side == 0 else (inner_row, outer_row)
        for x in range(nx):
            y = x * ny + side * (ny - 2)
            warmed_ref[y : y + 1, :] = rows[0][x : x + 1]
            warmed_ref[y + 1 : y + 2, :] = rows[1][x : x + 1]

    message_ref[:, HEAD_ROWS:MESSAGE_ROWS, :] = zone_ref[...]
    brick = warmed_ref[...].astype(jnp.bfloat16)
    group = 8 * SLOTS
    for start in range(0, pick_ref.shape[0], group):
        span = slice(start, start + group)
        pair = jnp.dot(pick_ref[span, :], brick, preferred_element_type=jnp.float32)
        pair = pair.astype(jnp.bfloat16)
        rows = jnp.where(side_ref[span, :] > 0, pair[:, CELLS:], pair[:, :CELLS])
        peer = start // HEAD_ROWS
        for k in range(8):
            at = k // 4 * SLOTS
            message_ref[peer + k % 4, at : at + SLOTS, :] = rows[k * SLOTS : (k + 1) * SLOTS]


def field_kernel(*refs):
    inside = position()
    given, faces, early, out = refs[:6], refs[6:8], refs[8:13], refs[13:15]
    late, scratch = refs[15:20], refs[20:]

    @pl.when(inside[4] > 0)
    def _():
        finish_part(inside, *faces, *early, *out)

    @pl.when(inside[4] == 0)
    def _():
        interior_part(inside, *given, *late, *scratch)
        finish_part(inside, *faces, *late, *out)


def outlet_lanes(odd_core, outlet_ref, tally_ref, turned_ref):
    slots, peers = outlet_ref.shape
    slot = lax.broadcasted_iota(jnp.int32, outlet_ref.shape, 0)
    outlet = jnp.where(slot < tally_ref[...], outlet_ref[...], -1)
    outlet = by_core(outlet, odd_core).astype(jnp.float32)
    turned_ref[0:peers, :] = jnp.concatenate(
        [jnp.transpose(outlet), jnp.zeros((peers, CELLS - slots), jnp.float32)], axis=1
    )
    halves = []
    for zh in range(2):
        lanes = 0.0
        for q in range(4):
            part = turned_ref[pl.ds(2 * zh + q // 2 + 4 * (q % 2), peers // 8, stride=8), :]
            lanes = lanes + (pltpu.roll(part, q * slots, 1) if q else part)
        halves.append(lanes.astype(jnp.int32))
    return halves


def surrogate_kernel(
    message_ref,
    first_ref,
    second_ref,
    last_ref,
    offset_ref,
    first_other_ref,
    second_other_ref,
    last_other_ref,
    offset_other_ref,
    heat_ref,
    entry_ref,
):
    peers = message_ref.shape[0]
    sub = lax.broadcasted_iota(jnp.int32, (8, CELLS), 0)
    lane = lax.broadcasted_iota(jnp.int32, (8, CELLS), 1)
    mine = (lane // ZONES == sub).astype(jnp.float32)

    def silu(x):
        half = 0.5 * x
        return (half + half * jnp.tanh(half)).astype(jnp.bfloat16)

    other = (first_other_ref, second_other_ref, last_other_ref, offset_other_ref)
    own = (first_ref, second_ref, last_ref, offset_ref)
    for turn, (entry, middle, last, offset) in enumerate((own, other)):
        entry_ref[turn, 0:CELLS, :] = entry[...]
        for k in range(CELLS // ZONES):
            entry_ref[turn, CELLS + k * ZONES : CELLS + (k + 1) * ZONES, :] = offset[...]
        slots = slice(turn * SLOTS, (turn + 1) * SLOTS)
        for at in range(0, peers, ROWS_STEP):
            rows = message_ref[at : at + ROWS_STEP, slots, :].reshape(ROWS_STEP * SLOTS, CELLS)
            zone = message_ref[at : at + ROWS_STEP, HEAD_ROWS:MESSAGE_ROWS, :].astype(jnp.float32)
            hots = [
                jnp.broadcast_to(zone[s, j : j + 1, :], (8, CELLS)) * mine
                for s in range(ROWS_STEP)
                for j in range(turn * 4, turn * 4 + 4)
            ]
            hot = jnp.concatenate(hots, axis=0).astype(jnp.bfloat16)
            inputs = jnp.concatenate([rows, hot], axis=1)
            hidden = silu(jnp.dot(inputs, entry_ref[turn], preferred_element_type=jnp.float32))
            second = silu(jnp.dot(hidden, middle[...], preferred_element_type=jnp.float32))
            heat = jnp.dot(second, last[...], preferred_element_type=jnp.float32)
            heat_ref[at : at + ROWS_STEP, slots, :] = heat.astype(jnp.bfloat16).reshape(
                ROWS_STEP, SLOTS, CELLS
            )


def outlet_hits(outlet_ref, hit_ref, side_ref):
    halves, chunks = outlet_ref.shape[:2]
    place = lax.broadcasted_iota(jnp.int32, (hit_ref.shape[0] // chunks, CELLS), 0)
    one, none = jnp.float32(1), jnp.float32(0)
    for zh in range(halves):
        outlet = outlet_ref[zh]
        block, odd = outlet >> 1, (outlet & 1).astype(jnp.float32)
        odd = jnp.transpose(jnp.concatenate([odd] * (CELLS // chunks), axis=0))
        for yx in range(chunks):
            at = (yx * halves + zh) * CELLS
            hit = jnp.where(place == block[yx : yx + 1], one, none)
            rows = slice(yx * hit.shape[0], (yx + 1) * hit.shape[0])
            hit_ref[rows, zh * CELLS : (zh + 1) * CELLS] = hit.astype(jnp.bfloat16)
            side = jnp.broadcast_to(odd[:, yx : yx + 1], (CELLS, CELLS))
            side_ref[at : at + CELLS, :] = side.astype(jnp.bfloat16)


def exhaust_kernel(
    warmed_ref, heat_ref, outlet_ref, hit_ref, side_ref, out_ref, late_hit_ref, late_side_ref
):
    odd_core = lax.axis_index("core")

    def add(hits, sides):
        step = 8 * CELLS
        rows = warmed_ref.shape[0]
        total = warmed_ref[...]
        for at in range(0, heat_ref.shape[0], step):
            heat = heat_ref[at : at + step, :]
            second = heat * sides[at : at + step, :]
            total = total + jnp.dot(
                jnp.concatenate([hits[k : k + rows, :] for k in range(at, at + step, rows)], axis=1),
                jnp.concatenate([heat - second, second], axis=1),
                preferred_element_type=jnp.float32,
            )
        out_ref[...] = total

    @pl.when(odd_core == 0)
    def _():
        add(hit_ref, side_ref)

    @pl.when(odd_core != 0)
    def _():
        outlet_hits(outlet_ref, late_hit_ref, late_side_ref)
        add(late_hit_ref, late_side_ref)


def in_vmem(count):
    return [pl.BlockSpec(memory_space=pltpu.VMEM)] * count


def shards(
    thermal_anomaly_field,
    airflow_vector_field,
    entry_matrix_first,
    hidden_matrix_second,
    final_readout_matrix,
    electrical_zone_offset,
    intake_source_tile,
    machine_electrical_zone,
    machine_tally_matrix,
    exhaust_source_tile,
):
    f = thermal_anomaly_field
    u = airflow_vector_field
    nx, ny, nz = f.shape
    length = ("y", "x", "core")
    gx, gy = lax.axis_index(length), lax.axis_index("z")
    n_gx, n_gy = lax.axis_size(length), lax.axis_size("z")
    odd_x, odd_y = lax.axis_index("core"), gy % 2
    across = [(i, i + 1) for i in range(1, n_gx - 1, 2)] + [(i + 1, i) for i in range(1, n_gx - 1, 2)]
    beside = [(i, i ^ 1) for i in range(n_gx)]

    faces = jax.ShapeDtypeStruct((5, ny, nz), jnp.bfloat16)
    face_across, face_beside = pl.pallas_call(
        faces_kernel,
        out_shape=(faces, faces),
        in_specs=[pl.BlockSpec(memory_space=pl.ANY)] * 2,
        out_specs=tuple(in_vmem(2)),
        scratch_shapes=[
            pltpu.VMEM((2, 5, ny, nz), jnp.float32),
            pltpu.SemaphoreType.DMA((2, 2)),
        ],
        name="faces",
    )(f, u)
    own = (
        entry_matrix_first[0],
        hidden_matrix_second[0],
        final_readout_matrix[0],
        electrical_zone_offset,
    )
    face_across, *later = lax.optimization_barrier((face_across, *own))
    x_across = lax.ppermute(face_across, length, across)
    x_beside = lax.ppermute(face_beside, length, beside)
    other = tuple(lax.ppermute(w, "core", [(0, 1), (1, 0)]) for w in later)
    first_y = [(i, i ^ 1) for i in range(n_gy)]
    then_y = [(i, i + 1) for i in range(1, n_gy - 1, 2)] + [(i + 1, i) for i in range(1, n_gy - 1, 2)]
    below = jnp.where(odd_x == 1, x_beside[1:2], x_across[1:2])
    above = jnp.where(odd_x == 1, x_across[0:1], x_beside[0:1])

    def face_y(high):
        edge, next_edge = high * (ny - 1), high * (ny - 3) + 1
        at = lambda a, i: lax.dynamic_index_in_dim(a, i, a.ndim - 2, False)
        own = at(f, edge).astype(jnp.bfloat16)
        near = jnp.concatenate([at(below, edge), own, at(above, edge)], axis=0)
        near = jnp.pad(near, ((0, 16 - near.shape[0]), (0, 0)))
        rest = jnp.concatenate([at(f, next_edge), at(u, edge).reshape(3 * nx, nz)], axis=0)
        return jnp.concatenate([near, rest.astype(jnp.bfloat16)], axis=0)

    y_then = lax.ppermute(face_y(odd_y), "z", then_y)
    y_first = lax.ppermute(face_y(1 - odd_y), "z", first_y)
    peers = intake_source_tile.shape[1]
    y_then, y_first, *other = lax.optimization_barrier((y_then, y_first, *other))
    interior = (
        jax.ShapeDtypeStruct((nx * ny, nz), jnp.float32),
        jax.ShapeDtypeStruct((20, nx + 8, nz), jnp.float32),
        jax.ShapeDtypeStruct((peers * SLOTS, 2 * CELLS), jnp.bfloat16),
        jax.ShapeDtypeStruct((peers * SLOTS, CELLS), jnp.bfloat16),
        jax.ShapeDtypeStruct((peers // 2, 8, CELLS), jnp.bfloat16),
    )
    scratch = [
        pltpu.VMEM((nx + 4, ny + 16, nz), jnp.float32),
        pltpu.VMEM((nx + 2, ny + 16, nz), jnp.float32),
        pltpu.VMEM((peers * 4 + 8, CELLS), jnp.float32),
        pltpu.VMEM((peers * 4 + 32, CELLS), jnp.float32),
    ]
    given = (
        f,
        u,
        x_across,
        x_beside,
        jnp.transpose(intake_source_tile[0]),
        jnp.transpose(machine_electrical_zone[0]),
    )
    *early, outlets = pl.pallas_call(
        interior_kernel,
        out_shape=(*interior, jax.ShapeDtypeStruct((2, peers // 8, CELLS), jnp.int32)),
        in_specs=in_vmem(8),
        out_specs=tuple(in_vmem(6)),
        scratch_shapes=scratch + [pltpu.VMEM((peers + 8, CELLS), jnp.float32)],
        compiler_params=pltpu.CompilerParams(vmem_limit_bytes=40 * 1024 * 1024),
        cost_estimate=pl.CostEstimate(flops=4 * 10**9, bytes_accessed=8 * 10**6, transcendentals=0),
        name="interior",
    )(*given, jnp.transpose(exhaust_source_tile[0]), machine_tally_matrix)
    warmed, message = pl.pallas_call(
        field_kernel,
        out_shape=(
            jax.ShapeDtypeStruct((nx * ny, nz), jnp.float32),
            jax.ShapeDtypeStruct((peers // 2, MESSAGE_ROWS, CELLS), jnp.bfloat16),
        ),
        in_specs=in_vmem(13),
        out_specs=tuple(in_vmem(2)),
        scratch_shapes=[pltpu.VMEM(a.shape, a.dtype) for a in interior] + scratch,
        compiler_params=pltpu.CompilerParams(vmem_limit_bytes=40 * 1024 * 1024),
        name="field",
    )(*given, y_then, y_first, *early)

    half = ("y", "x", "z")
    arrived = lax.all_to_all(message, half, split_axis=0, concat_axis=0, tiled=True)
    heat = pl.pallas_call(
        surrogate_kernel,
        out_shape=jax.ShapeDtypeStruct((peers // 2, HEAD_ROWS, CELLS), jnp.bfloat16),
        in_specs=in_vmem(9),
        out_specs=in_vmem(1)[0],
        scratch_shapes=[
            pltpu.VMEM((2, 2 * CELLS, entry_matrix_first.shape[2]), jnp.bfloat16),
        ],
        compiler_params=pltpu.CompilerParams(vmem_limit_bytes=40 * 1024 * 1024),
        name="surrogate",
    )(arrived, *own, *other)
    returned = lax.all_to_all(heat, half, split_axis=0, concat_axis=0, tiled=True)

    final = pl.pallas_call(
        exhaust_kernel,
        out_shape=jax.ShapeDtypeStruct((nx * ny, nz), jnp.float32),
        in_specs=in_vmem(5),
        out_specs=in_vmem(1)[0],
        scratch_shapes=[pltpu.VMEM(a.shape, a.dtype) for a in early[2:4]],
        compiler_params=pltpu.CompilerParams(vmem_limit_bytes=40 * 1024 * 1024),
        name="exhaust",
    )(warmed, returned.reshape(peers * SLOTS, CELLS), outlets, early[2], early[3])
    return final.reshape(nx, ny, nz)


def solution(mesh):
    devices = mesh.devices
    split = Mesh(devices.reshape(4, 4, 2, devices.shape[1]), ("y", "x", "core", "z"))
    length = ("y", "x", "core")
    every = length + ("z",)
    return jax.shard_map(
        shards,
        mesh=split,
        in_specs=(
            P(length, "z", None),
            P(None, length, "z", None),
            P(every, None, None),
            P(every, None, None),
            P(every, None, None),
            P(every, None),
            P(every, None, None),
            P(every, None, None),
            P(every, None),
            P(every, None, None),
        ),
        out_specs=P(length, "z", None),
        check_vma=False,
    )
```

```python
import jax
import jax.numpy as jnp
from jax import lax
from jax.experimental import pallas as pl
from jax.experimental.pallas import tpu as pltpu
from jax.sharding import Mesh
from jax.sharding import PartitionSpec as P

time_step = 0.1
diffusivity = 0.5
buoyancy = 0.5

CELLS = 128
SLOTS = 32
ZONES = 16
HEAD_ROWS = 2 * SLOTS
MESSAGE_ROWS = HEAD_ROWS + 8
ROWS_STEP = 16


def advance(center, east, west, north, south, u0, u1, u2):
    lanes = center.shape[1]
    lane = lax.broadcasted_iota(jnp.int32, center.shape, 1)
    upper = jnp.where(lane == lanes - 1, 0.0, pltpu.roll(center, lanes - 1, 1))
    lower = jnp.where(lane == 0, 0.0, pltpu.roll(center, 1, 1))
    laplace = east + west + north + south + upper + lower - 6.0 * center
    transport = u0 * (east - west) + u1 * (north - south)
    transport = transport + (u2 + buoyancy * center) * (upper - lower)
    return center + time_step * (diffusivity * laplace - 0.5 * transport)


def by_core(table, odd_core):
    columns = table.shape[1]
    lane = lax.broadcasted_iota(jnp.int32, table.shape, 1)
    later, earlier = pltpu.roll(table, columns - 4, 1), pltpu.roll(table, 4, 1)
    return jnp.where(odd_core, jnp.where((lane & 4) == 0, later, earlier), table)


def faces_kernel(f_ref, u_ref, across_ref, beside_ref, held_ref, sems):
    nx = f_ref.shape[0]
    odd = lax.axis_index("core")
    copies = []
    for k, high in enumerate((odd, 1 - odd)):
        copies.append(
            (
                pltpu.make_async_copy(
                    f_ref.at[pl.ds(high * (nx - 2), 2)], held_ref.at[k, pl.ds(0, 2)], sems.at[k, 0]
                ),
                pltpu.make_async_copy(
                    u_ref.at[:, high * (nx - 1)], held_ref.at[k, pl.ds(2, 3)], sems.at[k, 1]
                ),
            )
        )
    for pair in copies:
        for copy in pair:
            copy.start()
    for k, ref in enumerate((across_ref, beside_ref)):
        for copy in copies[k]:
            copy.wait()
        ref[...] = held_ref[k].astype(jnp.bfloat16)


def position():
    at = [lax.axis_index(axis) for axis in ("y", "x", "core", "z")]
    size = [lax.axis_size(axis) for axis in ("y", "x", "core", "z")]
    along = at[0] + at[1] + at[2]
    flags = (along > 0, along < sum(size[:3]) - 3, at[3] > 0, at[3] < size[3] - 1)
    return tuple(jnp.where(flag, 1, 0) for flag in flags) + (at[2], at[3] % 2)


def interior_part(
    inside,
    f_ref,
    u_ref,
    x_across_ref,
    x_beside_ref,
    intake_ref,
    zone_ref,
    warmed_ref,
    edge_ref,
    pick_ref,
    side_ref,
    zone_out_ref,
    first_ref,
    second_ref,
    hot_ref,
    zone_rows_ref,
):
    nx, ny, nz = f_ref.shape
    top = 8
    bottom = top + ny
    odd_x = inside[4] > 0
    x_across = x_across_ref[...].astype(jnp.float32)
    x_beside = x_beside_ref[...].astype(jnp.float32)
    xlo, xhi = jnp.where(odd_x, x_beside, x_across), jnp.where(odd_x, x_across, x_beside)
    first_ref[0:2, top:bottom, :] = xlo[0:2]
    first_ref[2 : nx + 2, top:bottom, :] = f_ref[...]
    first_ref[nx + 2 : nx + 4, top:bottom, :] = xhi[0:2]
    for ref in (first_ref, second_ref):
        ref[:, top - 8 : top, :] = jnp.zeros((ref.shape[0], 8, nz), jnp.float32)
        ref[:, bottom : bottom + 8, :] = jnp.zeros((ref.shape[0], 8, nz), jnp.float32)

    def slab(ref, at, u0, u1, u2):
        return advance(
            ref[at, top:bottom, :],
            ref[at + 1, top:bottom, :],
            ref[at - 1, top:bottom, :],
            ref[at, top + 1 : bottom + 1, :],
            ref[at, top - 1 : bottom - 1, :],
            u0,
            u1,
            u2,
        )

    for x in range(nx):
        second_ref[x + 1, top:bottom, :] = slab(first_ref, x + 2, u_ref[0, x], u_ref[1, x], u_ref[2, x])
    west_face = slab(first_ref, 1, xlo[2], xlo[3], xlo[4])
    second_ref[0, top:bottom, :] = jnp.where(inside[0] > 0, west_face, 0.0)
    east_face = slab(first_ref, nx + 2, xhi[2], xhi[3], xhi[4])
    second_ref[nx + 1, top:bottom, :] = jnp.where(inside[1] > 0, east_face, 0.0)
    for x in range(nx):
        warmed_ref[x * ny : (x + 1) * ny, :] = slab(
            second_ref, x + 1, u_ref[0, x], u_ref[1, x], u_ref[2, x]
        )

    gap = jnp.zeros((1, nz), jnp.float32)
    rest = jnp.zeros((4, nz), jnp.float32)

    def keep(k, rows):
        edge_ref[k] = jnp.concatenate(rows + [rest], axis=0)

    for side, (y, inner, innermost) in enumerate(((0, 1, 2), (ny - 1, ny - 2, ny - 3))):
        at = side * 10
        cells = lambda ref, y, first, last: [ref[x, top + y : top + y + 1, :] for x in range(first, last)]
        keep(at, cells(first_ref, y, 0, nx + 4))
        keep(at + 1, cells(first_ref, inner, 0, nx + 4))
        keep(at + 2, [gap] + cells(second_ref, inner, 0, nx + 2) + [gap])
        keep(at + 3, [gap] + cells(second_ref, innermost, 0, nx + 2) + [gap])
        for k in range(3):
            wind = [u_ref[k, x, y : y + 1, :] for x in range(nx)]
            keep(at + 4 + k, [gap, xlo[2 + k, y : y + 1]] + wind + [xhi[2 + k, y : y + 1], gap])
            wind = [u_ref[k, x, inner : inner + 1, :] for x in range(nx)]
            keep(at + 7 + k, [gap, gap] + wind + [gap, gap])

    peers = intake_ref.shape[1]
    zones = jnp.transpose(by_core(zone_ref[...], odd_x).astype(jnp.float32)).astype(jnp.bfloat16)
    groups = SLOTS // 8
    wide = groups * CELLS
    slot = lax.broadcasted_iota(jnp.int32, (SLOTS, wide), 0)
    lane = lax.broadcasted_iota(jnp.int32, (SLOTS, wide), 1)
    spread = (lane // ZONES == slot).astype(jnp.float32).astype(jnp.bfloat16)
    zone_wide = jnp.dot(zones, spread, preferred_element_type=jnp.float32)
    which = lax.broadcasted_iota(jnp.int32, (peers, wide), 1) % ZONES
    hot = (zone_wide == which.astype(jnp.float32)).astype(jnp.float32)
    for j in range(groups):
        hot_ref[j * peers : (j + 1) * peers, :] = hot[:, j * CELLS : (j + 1) * CELLS]
    for z in range(4):
        for turn in range(2):
            for j in range(groups):
                zone_rows_ref[pl.ds(z * 8 + turn * 4 + j, peers // 8, stride=32), :] = hot_ref[
                    pl.ds(j * peers + turn * 4 + z, peers // 8, stride=8), :
                ]
    zone_rows = zone_rows_ref[0 : peers * 4, :].astype(jnp.bfloat16)
    zone_out_ref[...] = zone_rows.reshape(peers // 2, 8, CELLS)

    intake = by_core(intake_ref[...], odd_x)
    lane = lax.broadcasted_iota(jnp.int32, (SLOTS, CELLS), 1)
    one, none = jnp.float32(1), jnp.float32(0)
    for d in range(peers):
        block = jnp.broadcast_to(intake[:, d : d + 1], (SLOTS, CELLS))
        row = block >> 1
        span = slice(d * SLOTS, (d + 1) * SLOTS)
        pick_ref[span, :CELLS] = jnp.where(row == lane, one, none).astype(jnp.bfloat16)
        pick_ref[span, CELLS:] = jnp.where(row == lane + CELLS, one, none).astype(jnp.bfloat16)
        side_ref[span, :] = (block & 1).astype(jnp.float32).astype(jnp.bfloat16)


def interior_kernel(*refs):
    inside = position()
    given, (outlet_ref, tally_ref), made, lanes_ref = refs[:6], refs[6:8], refs[8:13], refs[13]
    scratch, turned_ref = refs[14:18], refs[18]
    odd_core = inside[4] > 0

    @pl.when(odd_core)
    def _():
        interior_part(inside, *given, *made, *scratch)

    for zh, half in enumerate(outlet_lanes(odd_core, outlet_ref, tally_ref, turned_ref)):
        lanes_ref[zh] = half

    @pl.when(jnp.logical_not(odd_core))
    def _():
        outlet_hits(lanes_ref, made[2], made[3])


def finish_part(
    inside,
    y_first_ref,
    y_then_ref,
    interior_ref,
    edge_ref,
    pick_ref,
    side_ref,
    zone_ref,
    warmed_ref,
    message_ref,
):
    nx = (edge_ref.shape[1] - 4) - 4
    ny = interior_ref.shape[0] // nx
    odd_y = inside[5] > 0
    y_first = y_first_ref[...].astype(jnp.float32)
    y_then = y_then_ref[...].astype(jnp.float32)
    ylo, yhi = jnp.where(odd_y, y_first, y_then), jnp.where(odd_y, y_then, y_first)
    warmed_ref[...] = interior_ref[...]
    spot = lax.broadcasted_iota(jnp.int32, (nx + 2, edge_ref.shape[2]), 0)
    west = jnp.logical_and(spot == 0, inside[0] == 0)
    east = jnp.logical_and(spot == nx + 1, inside[1] == 0)
    outside = jnp.logical_or(west, east)
    for side, halo in enumerate((ylo, yhi)):
        at = side * 10
        def step(center, inward, outward, wind, first, last):
            middle = center[first:last]
            north, south = (inward, outward) if side == 0 else (outward, inward)
            return advance(
                middle, center[first + 1 : last + 1], center[first - 1 : last - 1], north, south, *wind
            )

        wind = [halo[24 + 8 * k : 32 + 8 * k] for k in range(3)]
        beyond = step(halo, edge_ref[at, 2 : nx + 2], halo[16 : 16 + nx], wind, 1, nx + 1)
        beyond = jnp.where(inside[2 + side] > 0, beyond, 0.0)
        wind = [edge_ref[at + 4 + k] for k in range(3)]
        near = step(
            edge_ref[at],
            edge_ref[at + 1, 1 : nx + 3],
            halo[0 : nx + 2],
            [w[1 : nx + 3] for w in wind],
            1,
            nx + 3,
        )
        near = jnp.where(outside, 0.0, near)
        inner, innermost = edge_ref[at + 2], edge_ref[at + 3]
        outer_row = step(near, inner[2 : nx + 2], beyond, [w[2 : nx + 2] for w in wind], 1, nx + 1)
        wind = [edge_ref[at + 7 + k, 2 : nx + 2] for k in range(3)]
        inner_row = step(inner, innermost[2 : nx + 2], near[1 : nx + 1], wind, 2, nx + 2)
        rows = (outer_row, inner_row) if side == 0 else (inner_row, outer_row)
        for x in range(nx):
            y = x * ny + side * (ny - 2)
            warmed_ref[y : y + 1, :] = rows[0][x : x + 1]
            warmed_ref[y + 1 : y + 2, :] = rows[1][x : x + 1]

    message_ref[:, HEAD_ROWS:MESSAGE_ROWS, :] = zone_ref[...]
    brick = warmed_ref[...].astype(jnp.bfloat16)
    group = 8 * SLOTS
    group = 4 * group
    for start in range(0, pick_ref.shape[0], group):
        span = slice(start, start + group)
        pair = jnp.dot(pick_ref[span, :], brick, preferred_element_type=jnp.float32)
        pair = pair.astype(jnp.bfloat16)
        rows = jnp.where(side_ref[span, :] > 0, pair[:, CELLS:], pair[:, :CELLS])
        for k in range(group // SLOTS):
            peer, at = start // HEAD_ROWS + k // 8 * 4 + k % 4, k % 8 // 4 * SLOTS
            message_ref[peer, at : at + SLOTS, :] = rows[k * SLOTS : (k + 1) * SLOTS]


def field_kernel(*refs):
    inside = position()
    given, faces, early, out = refs[:6], refs[6:8], refs[8:13], refs[13:15]
    late, scratch = refs[15:20], refs[20:]

    @pl.when(inside[4] > 0)
    def _():
        finish_part(inside, *faces, *early, *out)

    @pl.when(inside[4] == 0)
    def _():
        interior_part(inside, *given, *late, *scratch)
        finish_part(inside, *faces, *late, *out)


def outlet_lanes(odd_core, outlet_ref, tally_ref, turned_ref):
    slots, peers = outlet_ref.shape
    slot = lax.broadcasted_iota(jnp.int32, outlet_ref.shape, 0)
    outlet = jnp.where(slot < tally_ref[...], outlet_ref[...], -1)
    outlet = by_core(outlet, odd_core).astype(jnp.float32)
    turned_ref[0:peers, :] = jnp.concatenate(
        [jnp.transpose(outlet), jnp.zeros((peers, CELLS - slots), jnp.float32)], axis=1
    )
    halves = []
    for zh in range(2):
        lanes = 0.0
        for q in range(4):
            part = turned_ref[pl.ds(2 * zh + q // 2 + 4 * (q % 2), peers // 8, stride=8), :]
            lanes = lanes + (pltpu.roll(part, q * slots, 1) if q else part)
        halves.append(lanes.astype(jnp.int32))
    return halves


def surrogate_kernel(
    message_ref,
    first_ref,
    second_ref,
    last_ref,
    offset_ref,
    first_other_ref,
    second_other_ref,
    last_other_ref,
    offset_other_ref,
    heat_ref,
    entry_ref,
):
    peers = message_ref.shape[0]
    sub = lax.broadcasted_iota(jnp.int32, (8, CELLS), 0)
    lane = lax.broadcasted_iota(jnp.int32, (8, CELLS), 1)
    mine = (lane // ZONES == sub).astype(jnp.float32)

    def silu(x):
        half = 0.5 * x
        return (half + half * jnp.tanh(half)).astype(jnp.bfloat16)

    other = (first_other_ref, second_other_ref, last_other_ref, offset_other_ref)
    own = (first_ref, second_ref, last_ref, offset_ref)
    for turn, (entry, middle, last, offset) in enumerate((own, other)):
        entry_ref[turn, 0:CELLS, :] = entry[...]
        for k in range(CELLS // ZONES):
            entry_ref[turn, CELLS + k * ZONES : CELLS + (k + 1) * ZONES, :] = offset[...]
        slots = slice(turn * SLOTS, (turn + 1) * SLOTS)
        for at in range(0, peers, ROWS_STEP):
            rows = message_ref[at : at + ROWS_STEP, slots, :].reshape(ROWS_STEP * SLOTS, CELLS)
            zone = message_ref[at : at + ROWS_STEP, HEAD_ROWS:MESSAGE_ROWS, :].astype(jnp.float32)
            hots = [
                jnp.broadcast_to(zone[s, j : j + 1, :], (8, CELLS)) * mine
                for s in range(ROWS_STEP)
                for j in range(turn * 4, turn * 4 + 4)
            ]
            hot = jnp.concatenate(hots, axis=0).astype(jnp.bfloat16)
            inputs = jnp.concatenate([rows, hot], axis=1)
            hidden = silu(jnp.dot(inputs, entry_ref[turn], preferred_element_type=jnp.float32))
            second = silu(jnp.dot(hidden, middle[...], preferred_element_type=jnp.float32))
            heat = jnp.dot(second, last[...], preferred_element_type=jnp.float32)
            heat_ref[at : at + ROWS_STEP, slots, :] = heat.astype(jnp.bfloat16).reshape(
                ROWS_STEP, SLOTS, CELLS
            )


def outlet_hits(outlet_ref, hit_ref, side_ref):
    halves, chunks = outlet_ref.shape[:2]
    place = lax.broadcasted_iota(jnp.int32, (hit_ref.shape[0] // chunks, CELLS), 0)
    one, none = jnp.float32(1), jnp.float32(0)
    for zh in range(halves):
        outlet = outlet_ref[zh]
        block, odd = outlet >> 1, (outlet & 1).astype(jnp.float32)
        odd = jnp.transpose(jnp.concatenate([odd] * (CELLS // chunks), axis=0))
        for yx in range(chunks):
            at = (yx * halves + zh) * CELLS
            hit = jnp.where(place == block[yx : yx + 1], one, none)
            rows = slice(yx * hit.shape[0], (yx + 1) * hit.shape[0])
            hit_ref[rows, zh * CELLS : (zh + 1) * CELLS] = hit.astype(jnp.bfloat16)
            side = jnp.broadcast_to(odd[:, yx : yx + 1], (CELLS, CELLS))
            side_ref[at : at + CELLS, :] = side.astype(jnp.bfloat16)


def exhaust_kernel(
    warmed_ref, heat_ref, outlet_ref, hit_ref, side_ref, out_ref, late_hit_ref, late_side_ref
):
    odd_core = lax.axis_index("core")

    def add(hits, sides):
        step = 8 * CELLS
        rows = warmed_ref.shape[0]
        total = warmed_ref[...]
        for at in range(0, heat_ref.shape[0], step):
            heat = heat_ref[at : at + step, :]
            second = heat * sides[at : at + step, :]
            total = total + jnp.dot(
                jnp.concatenate([hits[k : k + rows, :] for k in range(at, at + step, rows)], axis=1),
                jnp.concatenate([heat - second, second], axis=1),
                preferred_element_type=jnp.float32,
            )
        out_ref[...] = total

    @pl.when(odd_core == 0)
    def _():
        add(hit_ref, side_ref)

    @pl.when(odd_core != 0)
    def _():
        outlet_hits(outlet_ref, late_hit_ref, late_side_ref)
        add(late_hit_ref, late_side_ref)


def in_vmem(count):
    return [pl.BlockSpec(memory_space=pltpu.VMEM)] * count


def shards(
    thermal_anomaly_field,
    airflow_vector_field,
    entry_matrix_first,
    hidden_matrix_second,
    final_readout_matrix,
    electrical_zone_offset,
    intake_source_tile,
    machine_electrical_zone,
    machine_tally_matrix,
    exhaust_source_tile,
):
    f = thermal_anomaly_field
    u = airflow_vector_field
    nx, ny, nz = f.shape
    length = ("y", "x", "core")
    gx, gy = lax.axis_index(length), lax.axis_index("z")
    n_gx, n_gy = lax.axis_size(length), lax.axis_size("z")
    odd_x, odd_y = lax.axis_index("core"), gy % 2
    across = [(i, i + 1) for i in range(1, n_gx - 1, 2)] + [(i + 1, i) for i in range(1, n_gx - 1, 2)]
    beside = [(i, i ^ 1) for i in range(n_gx)]

    faces = jax.ShapeDtypeStruct((5, ny, nz), jnp.bfloat16)
    face_across, face_beside = pl.pallas_call(
        faces_kernel,
        out_shape=(faces, faces),
        in_specs=[pl.BlockSpec(memory_space=pl.ANY)] * 2,
        out_specs=tuple(in_vmem(2)),
        scratch_shapes=[
            pltpu.VMEM((2, 5, ny, nz), jnp.float32),
            pltpu.SemaphoreType.DMA((2, 2)),
        ],
        name="faces",
    )(f, u)
    own = (
        entry_matrix_first[0],
        hidden_matrix_second[0],
        final_readout_matrix[0],
        electrical_zone_offset,
    )
    face_across, *later = lax.optimization_barrier((face_across, *own))
    x_across = lax.ppermute(face_across, length, across)
    x_beside = lax.ppermute(face_beside, length, beside)
    other = tuple(lax.ppermute(w, "core", [(0, 1), (1, 0)]) for w in later)
    first_y = [(i, i ^ 1) for i in range(n_gy)]
    then_y = [(i, i + 1) for i in range(1, n_gy - 1, 2)] + [(i + 1, i) for i in range(1, n_gy - 1, 2)]
    below = jnp.where(odd_x == 1, x_beside[1:2], x_across[1:2])
    above = jnp.where(odd_x == 1, x_across[0:1], x_beside[0:1])

    def face_y(high):
        edge, next_edge = high * (ny - 1), high * (ny - 3) + 1
        at = lambda a, i: lax.dynamic_index_in_dim(a, i, a.ndim - 2, False)
        own = at(f, edge).astype(jnp.bfloat16)
        near = jnp.concatenate([at(below, edge), own, at(above, edge)], axis=0)
        near = jnp.pad(near, ((0, 16 - near.shape[0]), (0, 0)))
        rest = jnp.concatenate([at(f, next_edge), at(u, edge).reshape(3 * nx, nz)], axis=0)
        return jnp.concatenate([near, rest.astype(jnp.bfloat16)], axis=0)

    y_then = lax.ppermute(face_y(odd_y), "z", then_y)
    y_first = lax.ppermute(face_y(1 - odd_y), "z", first_y)
    peers = intake_source_tile.shape[1]
    y_then, y_first, *other = lax.optimization_barrier((y_then, y_first, *other))
    interior = (
        jax.ShapeDtypeStruct((nx * ny, nz), jnp.float32),
        jax.ShapeDtypeStruct((20, nx + 8, nz), jnp.float32),
        jax.ShapeDtypeStruct((peers * SLOTS, 2 * CELLS), jnp.bfloat16),
        jax.ShapeDtypeStruct((peers * SLOTS, CELLS), jnp.bfloat16),
        jax.ShapeDtypeStruct((peers // 2, 8, CELLS), jnp.bfloat16),
    )
    scratch = [
        pltpu.VMEM((nx + 4, ny + 16, nz), jnp.float32),
        pltpu.VMEM((nx + 2, ny + 16, nz), jnp.float32),
        pltpu.VMEM((peers * 4 + 8, CELLS), jnp.float32),
        pltpu.VMEM((peers * 4 + 32, CELLS), jnp.float32),
    ]
    given = (
        f,
        u,
        x_across,
        x_beside,
        jnp.transpose(intake_source_tile[0]),
        jnp.transpose(machine_electrical_zone[0]),
    )
    *early, outlets = pl.pallas_call(
        interior_kernel,
        out_shape=(*interior, jax.ShapeDtypeStruct((2, peers // 8, CELLS), jnp.int32)),
        in_specs=in_vmem(8),
        out_specs=tuple(in_vmem(6)),
        scratch_shapes=scratch + [pltpu.VMEM((peers + 8, CELLS), jnp.float32)],
        compiler_params=pltpu.CompilerParams(vmem_limit_bytes=40 * 1024 * 1024),
        cost_estimate=pl.CostEstimate(flops=4 * 10**9, bytes_accessed=8 * 10**6, transcendentals=0),
        name="interior",
    )(*given, jnp.transpose(exhaust_source_tile[0]), machine_tally_matrix)
    warmed, message = pl.pallas_call(
        field_kernel,
        out_shape=(
            jax.ShapeDtypeStruct((nx * ny, nz), jnp.float32),
            jax.ShapeDtypeStruct((peers // 2, MESSAGE_ROWS, CELLS), jnp.bfloat16),
        ),
        in_specs=in_vmem(13),
        out_specs=tuple(in_vmem(2)),
        scratch_shapes=[pltpu.VMEM(a.shape, a.dtype) for a in interior] + scratch,
        compiler_params=pltpu.CompilerParams(vmem_limit_bytes=40 * 1024 * 1024),
        name="field",
    )(*given, y_first, y_then, *early)

    half = ("y", "x", "z")
    arrived = lax.all_to_all(message, half, split_axis=0, concat_axis=0, tiled=True)
    heat = pl.pallas_call(
        surrogate_kernel,
        out_shape=jax.ShapeDtypeStruct((peers // 2, HEAD_ROWS, CELLS), jnp.bfloat16),
        in_specs=in_vmem(9),
        out_specs=in_vmem(1)[0],
        scratch_shapes=[
            pltpu.VMEM((2, 2 * CELLS, entry_matrix_first.shape[2]), jnp.bfloat16),
        ],
        compiler_params=pltpu.CompilerParams(vmem_limit_bytes=40 * 1024 * 1024),
        name="surrogate",
    )(arrived, *own, *other)
    returned = lax.all_to_all(heat, half, split_axis=0, concat_axis=0, tiled=True)

    final = pl.pallas_call(
        exhaust_kernel,
        out_shape=jax.ShapeDtypeStruct((nx * ny, nz), jnp.float32),
        in_specs=in_vmem(5),
        out_specs=in_vmem(1)[0],
        scratch_shapes=[pltpu.VMEM(a.shape, a.dtype) for a in early[2:4]],
        compiler_params=pltpu.CompilerParams(vmem_limit_bytes=40 * 1024 * 1024),
        name="exhaust",
    )(warmed, returned.reshape(peers * SLOTS, CELLS), outlets, early[2], early[3])
    return final.reshape(nx, ny, nz)


def solution(mesh):
    devices = mesh.devices
    split = Mesh(devices.reshape(4, 4, 2, devices.shape[1]), ("y", "x", "core", "z"))
    length = ("y", "x", "core")
    every = length + ("z",)
    return jax.shard_map(
        shards,
        mesh=split,
        in_specs=(
            P(length, "z", None),
            P(None, length, "z", None),
            P(every, None, None),
            P(every, None, None),
            P(every, None, None),
            P(every, None),
            P(every, None, None),
            P(every, None, None),
            P(every, None),
            P(every, None, None),
        ),
        out_specs=P(length, "z", None),
        check_vma=False,
    )
```

```python
import jax
import jax.numpy as jnp
from jax import lax
from jax.experimental import pallas as pl
from jax.experimental.pallas import tpu as pltpu
from jax.sharding import Mesh
from jax.sharding import PartitionSpec as P

time_step = 0.1
diffusivity = 0.5
buoyancy = 0.5

CELLS = 128
SLOTS = 32
ZONES = 16
HEAD_ROWS = 2 * SLOTS
MESSAGE_ROWS = HEAD_ROWS + 8
ROWS_STEP = 16


def advance(center, east, west, north, south, u0, u1, u2):
    lanes = center.shape[1]
    lane = lax.broadcasted_iota(jnp.int32, center.shape, 1)
    upper = jnp.where(lane == lanes - 1, 0.0, pltpu.roll(center, lanes - 1, 1))
    lower = jnp.where(lane == 0, 0.0, pltpu.roll(center, 1, 1))
    laplace = east + west + north + south + upper + lower - 6.0 * center
    transport = u0 * (east - west) + u1 * (north - south)
    transport = transport + (u2 + buoyancy * center) * (upper - lower)
    return center + time_step * (diffusivity * laplace - 0.5 * transport)


def by_core(table, odd_core):
    columns = table.shape[1]
    lane = lax.broadcasted_iota(jnp.int32, table.shape, 1)
    later, earlier = pltpu.roll(table, columns - 4, 1), pltpu.roll(table, 4, 1)
    return jnp.where(odd_core, jnp.where((lane & 4) == 0, later, earlier), table)


def faces_kernel(f_ref, u_ref, across_ref, beside_ref, held_ref, sems):
    nx = f_ref.shape[0]
    odd = lax.axis_index("core")
    copies = []
    for k, high in enumerate((odd, 1 - odd)):
        copies.append(
            (
                pltpu.make_async_copy(
                    f_ref.at[pl.ds(high * (nx - 2), 2)], held_ref.at[k, pl.ds(0, 2)], sems.at[k, 0]
                ),
                pltpu.make_async_copy(
                    u_ref.at[:, high * (nx - 1)], held_ref.at[k, pl.ds(2, 3)], sems.at[k, 1]
                ),
            )
        )
    for pair in copies:
        for copy in pair:
            copy.start()
    for k, ref in enumerate((across_ref, beside_ref)):
        for copy in copies[k]:
            copy.wait()
        ref[...] = held_ref[k].astype(jnp.bfloat16)


def position():
    at = [lax.axis_index(axis) for axis in ("y", "x", "core", "z")]
    size = [lax.axis_size(axis) for axis in ("y", "x", "core", "z")]
    along = at[0] + at[1] + at[2]
    flags = (along > 0, along < sum(size[:3]) - 3, at[3] > 0, at[3] < size[3] - 1)
    return tuple(jnp.where(flag, 1, 0) for flag in flags) + (at[2], at[3] % 2)


def interior_part(
    inside,
    f_ref,
    u_ref,
    x_across_ref,
    x_beside_ref,
    intake_ref,
    zone_ref,
    warmed_ref,
    edge_ref,
    pick_ref,
    side_ref,
    zone_out_ref,
    first_ref,
    second_ref,
    hot_ref,
    zone_rows_ref,
):
    nx, ny, nz = f_ref.shape
    top = 8
    bottom = top + ny
    odd_x = inside[4] > 0
    x_across = x_across_ref[...].astype(jnp.float32)
    x_beside = x_beside_ref[...].astype(jnp.float32)
    xlo, xhi = jnp.where(odd_x, x_beside, x_across), jnp.where(odd_x, x_across, x_beside)
    first_ref[0:2, top:bottom, :] = xlo[0:2]
    first_ref[2 : nx + 2, top:bottom, :] = f_ref[...]
    first_ref[nx + 2 : nx + 4, top:bottom, :] = xhi[0:2]
    for ref in (first_ref, second_ref):
        ref[:, top - 8 : top, :] = jnp.zeros((ref.shape[0], 8, nz), jnp.float32)
        ref[:, bottom : bottom + 8, :] = jnp.zeros((ref.shape[0], 8, nz), jnp.float32)

    def slab(ref, at, u0, u1, u2):
        return advance(
            ref[at, top:bottom, :],
            ref[at + 1, top:bottom, :],
            ref[at - 1, top:bottom, :],
            ref[at, top + 1 : bottom + 1, :],
            ref[at, top - 1 : bottom - 1, :],
            u0,
            u1,
            u2,
        )

    for x in range(nx):
        second_ref[x + 1, top:bottom, :] = slab(first_ref, x + 2, u_ref[0, x], u_ref[1, x], u_ref[2, x])
    west_face = slab(first_ref, 1, xlo[2], xlo[3], xlo[4])
    second_ref[0, top:bottom, :] = jnp.where(inside[0] > 0, west_face, 0.0)
    east_face = slab(first_ref, nx + 2, xhi[2], xhi[3], xhi[4])
    second_ref[nx + 1, top:bottom, :] = jnp.where(inside[1] > 0, east_face, 0.0)
    for x in range(nx):
        warmed_ref[x * ny : (x + 1) * ny, :] = slab(
            second_ref, x + 1, u_ref[0, x], u_ref[1, x], u_ref[2, x]
        )

    gap = jnp.zeros((1, nz), jnp.float32)
    rest = jnp.zeros((4, nz), jnp.float32)

    def keep(k, rows):
        edge_ref[k] = jnp.concatenate(rows + [rest], axis=0)

    for side, (y, inner, innermost) in enumerate(((0, 1, 2), (ny - 1, ny - 2, ny - 3))):
        at = side * 10
        cells = lambda ref, y, first, last: [ref[x, top + y : top + y + 1, :] for x in range(first, last)]
        keep(at, cells(first_ref, y, 0, nx + 4))
        keep(at + 1, cells(first_ref, inner, 0, nx + 4))
        keep(at + 2, [gap] + cells(second_ref, inner, 0, nx + 2) + [gap])
        keep(at + 3, [gap] + cells(second_ref, innermost, 0, nx + 2) + [gap])
        for k in range(3):
            wind = [u_ref[k, x, y : y + 1, :] for x in range(nx)]
            keep(at + 4 + k, [gap, xlo[2 + k, y : y + 1]] + wind + [xhi[2 + k, y : y + 1], gap])
            wind = [u_ref[k, x, inner : inner + 1, :] for x in range(nx)]
            keep(at + 7 + k, [gap, gap] + wind + [gap, gap])

    peers = intake_ref.shape[1]
    zones = jnp.transpose(by_core(zone_ref[...], odd_x).astype(jnp.float32)).astype(jnp.bfloat16)
    groups = SLOTS // 8
    wide = groups * CELLS
    slot = lax.broadcasted_iota(jnp.int32, (SLOTS, wide), 0)
    lane = lax.broadcasted_iota(jnp.int32, (SLOTS, wide), 1)
    spread = (lane // ZONES == slot).astype(jnp.float32).astype(jnp.bfloat16)
    zone_wide = jnp.dot(zones, spread, preferred_element_type=jnp.float32)
    which = lax.broadcasted_iota(jnp.int32, (peers, wide), 1) % ZONES
    hot = (zone_wide == which.astype(jnp.float32)).astype(jnp.float32)
    for j in range(groups):
        hot_ref[j * peers : (j + 1) * peers, :] = hot[:, j * CELLS : (j + 1) * CELLS]
    for z in range(4):
        for turn in range(2):
            for j in range(groups):
                zone_rows_ref[pl.ds(z * 8 + turn * 4 + j, peers // 8, stride=32), :] = hot_ref[
                    pl.ds(j * peers + turn * 4 + z, peers // 8, stride=8), :
                ]
    zone_rows = zone_rows_ref[0 : peers * 4, :].astype(jnp.bfloat16)
    zone_out_ref[...] = zone_rows.reshape(peers // 2, 8, CELLS)

    intake = by_core(intake_ref[...], odd_x)
    lane = lax.broadcasted_iota(jnp.int32, (SLOTS, CELLS), 1)
    one, none = jnp.float32(1), jnp.float32(0)
    for d in range(peers):
        block = jnp.broadcast_to(intake[:, d : d + 1], (SLOTS, CELLS))
        row = block >> 1
        span = slice(d * SLOTS, (d + 1) * SLOTS)
        pick_ref[span, :CELLS] = jnp.where(row == lane, one, none).astype(jnp.bfloat16)
        pick_ref[span, CELLS:] = jnp.where(row == lane + CELLS, one, none).astype(jnp.bfloat16)
        side_ref[span, :] = (block & 1).astype(jnp.float32).astype(jnp.bfloat16)


def interior_kernel(*refs):
    inside = position()
    given, (outlet_ref, tally_ref), made, lanes_ref = refs[:6], refs[6:8], refs[8:13], refs[13]
    scratch, turned_ref = refs[14:18], refs[18]
    odd_core = inside[4] > 0

    @pl.when(odd_core)
    def _():
        interior_part(inside, *given, *made, *scratch)

    for zh, half in enumerate(outlet_lanes(odd_core, outlet_ref, tally_ref, turned_ref)):
        lanes_ref[zh] = half

    @pl.when(jnp.logical_not(odd_core))
    def _():
        outlet_hits(lanes_ref, made[2], made[3])


def finish_part(
    inside,
    y_first_ref,
    y_then_ref,
    interior_ref,
    edge_ref,
    pick_ref,
    side_ref,
    zone_ref,
    warmed_ref,
    message_ref,
):
    nx = (edge_ref.shape[1] - 4) - 4
    ny = interior_ref.shape[0] // nx
    odd_y = inside[5] > 0
    y_first = y_first_ref[...].astype(jnp.float32)
    y_then = y_then_ref[...].astype(jnp.float32)
    ylo, yhi = jnp.where(odd_y, y_first, y_then), jnp.where(odd_y, y_then, y_first)
    warmed_ref[...] = interior_ref[...]
    spot = lax.broadcasted_iota(jnp.int32, (nx + 2, edge_ref.shape[2]), 0)
    west = jnp.logical_and(spot == 0, inside[0] == 0)
    east = jnp.logical_and(spot == nx + 1, inside[1] == 0)
    outside = jnp.logical_or(west, east)
    for side, halo in enumerate((ylo, yhi)):
        at = side * 10
        def step(center, inward, outward, wind, first, last):
            middle = center[first:last]
            north, south = (inward, outward) if side == 0 else (outward, inward)
            return advance(
                middle, center[first + 1 : last + 1], center[first - 1 : last - 1], north, south, *wind
            )

        wind = [halo[24 + 8 * k : 32 + 8 * k] for k in range(3)]
        beyond = step(halo, edge_ref[at, 2 : nx + 2], halo[16 : 16 + nx], wind, 1, nx + 1)
        beyond = jnp.where(inside[2 + side] > 0, beyond, 0.0)
        wind = [edge_ref[at + 4 + k] for k in range(3)]
        near = step(
            edge_ref[at],
            edge_ref[at + 1, 1 : nx + 3],
            halo[0 : nx + 2],
            [w[1 : nx + 3] for w in wind],
            1,
            nx + 3,
        )
        near = jnp.where(outside, 0.0, near)
        inner, innermost = edge_ref[at + 2], edge_ref[at + 3]
        outer_row = step(near, inner[2 : nx + 2], beyond, [w[2 : nx + 2] for w in wind], 1, nx + 1)
        wind = [edge_ref[at + 7 + k, 2 : nx + 2] for k in range(3)]
        inner_row = step(inner, innermost[2 : nx + 2], near[1 : nx + 1], wind, 2, nx + 2)
        rows = (outer_row, inner_row) if side == 0 else (inner_row, outer_row)
        for x in range(nx):
            y = x * ny + side * (ny - 2)
            warmed_ref[y : y + 1, :] = rows[0][x : x + 1]
            warmed_ref[y + 1 : y + 2, :] = rows[1][x : x + 1]

    message_ref[:, HEAD_ROWS:MESSAGE_ROWS, :] = zone_ref[...]
    brick = warmed_ref[...].astype(jnp.bfloat16)
    group = 8 * SLOTS
    group = 4 * group
    for start in range(0, pick_ref.shape[0], group):
        span = slice(start, start + group)
        pair = jnp.dot(pick_ref[span, :], brick, preferred_element_type=jnp.float32)
        pair = pair.astype(jnp.bfloat16)
        rows = jnp.where(side_ref[span, :] > 0, pair[:, CELLS:], pair[:, :CELLS])
        for k in range(group // SLOTS):
            peer, at = start // HEAD_ROWS + k // 8 * 4 + k % 4, k % 8 // 4 * SLOTS
            message_ref[peer, at : at + SLOTS, :] = rows[k * SLOTS : (k + 1) * SLOTS]


def field_kernel(*refs):
    inside = position()
    given, faces, early, out = refs[:6], refs[6:8], refs[8:13], refs[13:15]
    late, scratch = refs[15:20], refs[20:]

    @pl.when(inside[4] > 0)
    def _():
        finish_part(inside, *faces, *early, *out)

    @pl.when(inside[4] == 0)
    def _():
        interior_part(inside, *given, *late, *scratch)
        finish_part(inside, *faces, *late, *out)


def outlet_lanes(odd_core, outlet_ref, tally_ref, turned_ref):
    slots, peers = outlet_ref.shape
    slot = lax.broadcasted_iota(jnp.int32, outlet_ref.shape, 0)
    outlet = jnp.where(slot < tally_ref[...], outlet_ref[...], -1)
    outlet = by_core(outlet, odd_core).astype(jnp.float32)
    turned_ref[0:peers, :] = jnp.concatenate(
        [jnp.transpose(outlet), jnp.zeros((peers, CELLS - slots), jnp.float32)], axis=1
    )
    halves = []
    for zh in range(2):
        lanes = 0.0
        for q in range(4):
            part = turned_ref[pl.ds(2 * zh + q // 2 + 4 * (q % 2), peers // 8, stride=8), :]
            lanes = lanes + (pltpu.roll(part, q * slots, 1) if q else part)
        halves.append(lanes.astype(jnp.int32))
    return halves


def surrogate_kernel(
    message_ref,
    first_ref,
    second_ref,
    last_ref,
    offset_ref,
    first_other_ref,
    second_other_ref,
    last_other_ref,
    offset_other_ref,
    heat_ref,
    entry_ref,
):
    peers = message_ref.shape[0]
    sub = lax.broadcasted_iota(jnp.int32, (8, CELLS), 0)
    lane = lax.broadcasted_iota(jnp.int32, (8, CELLS), 1)
    mine = (lane // ZONES == sub).astype(jnp.float32)

    def silu(x):
        half = 0.5 * x
        return (half + half * jnp.tanh(half)).astype(jnp.bfloat16)

    other = (first_other_ref, second_other_ref, last_other_ref, offset_other_ref)
    own = (first_ref, second_ref, last_ref, offset_ref)
    for turn, (entry, middle, last, offset) in enumerate((own, other)):
        entry_ref[turn, 0:CELLS, :] = entry[...]
        for k in range(CELLS // ZONES):
            entry_ref[turn, CELLS + k * ZONES : CELLS + (k + 1) * ZONES, :] = offset[...]
        slots = slice(turn * SLOTS, (turn + 1) * SLOTS)
        for at in range(0, peers, ROWS_STEP):
            rows = message_ref[at : at + ROWS_STEP, slots, :].reshape(ROWS_STEP * SLOTS, CELLS)
            zone = message_ref[at : at + ROWS_STEP, HEAD_ROWS:MESSAGE_ROWS, :].astype(jnp.float32)
            hots = [
                jnp.broadcast_to(zone[s, j : j + 1, :], (8, CELLS)) * mine
                for s in range(ROWS_STEP)
                for j in range(turn * 4, turn * 4 + 4)
            ]
            hot = jnp.concatenate(hots, axis=0).astype(jnp.bfloat16)
            inputs = jnp.concatenate([rows, hot], axis=1)
            hidden = silu(jnp.dot(inputs, entry_ref[turn], preferred_element_type=jnp.float32))
            second = silu(jnp.dot(hidden, middle[...], preferred_element_type=jnp.float32))
            heat = jnp.dot(second, last[...], preferred_element_type=jnp.float32)
            heat_ref[at : at + ROWS_STEP, slots, :] = heat.astype(jnp.bfloat16).reshape(
                ROWS_STEP, SLOTS, CELLS
            )


def outlet_hits(outlet_ref, hit_ref, side_ref):
    halves, chunks = outlet_ref.shape[:2]
    place = lax.broadcasted_iota(jnp.int32, (hit_ref.shape[0] // chunks, CELLS), 0)
    one, none = jnp.float32(1), jnp.float32(0)
    for zh in range(halves):
        outlet = outlet_ref[zh]
        block, odd = outlet >> 1, (outlet & 1).astype(jnp.float32)
        odd = jnp.transpose(jnp.concatenate([odd] * (CELLS // chunks), axis=0))
        for yx in range(chunks):
            at = (yx * halves + zh) * CELLS
            hit = jnp.where(place == block[yx : yx + 1], one, none)
            rows = slice(yx * hit.shape[0], (yx + 1) * hit.shape[0])
            hit_ref[rows, zh * CELLS : (zh + 1) * CELLS] = hit.astype(jnp.bfloat16)
            side = jnp.broadcast_to(odd[:, yx : yx + 1], (CELLS, CELLS))
            side_ref[at : at + CELLS, :] = side.astype(jnp.bfloat16)


def exhaust_kernel(
    warmed_ref, heat_ref, outlet_ref, hit_ref, side_ref, out_ref, late_hit_ref, late_side_ref
):
    odd_core = lax.axis_index("core")

    def add(hits, sides):
        step = 16 * CELLS
        rows = warmed_ref.shape[0]
        total = warmed_ref[...]
        for at in range(0, heat_ref.shape[0], step):
            heat = heat_ref[at : at + step, :]
            second = heat * sides[at : at + step, :]
            total = total + jnp.dot(
                jnp.concatenate([hits[k : k + rows, :] for k in range(at, at + step, rows)], axis=1),
                jnp.concatenate([heat - second, second], axis=1),
                preferred_element_type=jnp.float32,
            )
        out_ref[...] = total

    @pl.when(odd_core == 0)
    def _():
        add(hit_ref, side_ref)

    @pl.when(odd_core != 0)
    def _():
        outlet_hits(outlet_ref, late_hit_ref, late_side_ref)
        add(late_hit_ref, late_side_ref)


def in_vmem(count):
    return [pl.BlockSpec(memory_space=pltpu.VMEM)] * count


def shards(
    thermal_anomaly_field,
    airflow_vector_field,
    entry_matrix_first,
    hidden_matrix_second,
    final_readout_matrix,
    electrical_zone_offset,
    intake_source_tile,
    machine_electrical_zone,
    machine_tally_matrix,
    exhaust_source_tile,
):
    f = thermal_anomaly_field
    u = airflow_vector_field
    nx, ny, nz = f.shape
    length = ("y", "x", "core")
    gx, gy = lax.axis_index(length), lax.axis_index("z")
    n_gx, n_gy = lax.axis_size(length), lax.axis_size("z")
    odd_x, odd_y = lax.axis_index("core"), gy % 2
    across = [(i, i + 1) for i in range(1, n_gx - 1, 2)] + [(i + 1, i) for i in range(1, n_gx - 1, 2)]
    beside = [(i, i ^ 1) for i in range(n_gx)]

    faces = jax.ShapeDtypeStruct((5, ny, nz), jnp.bfloat16)
    face_across, face_beside = pl.pallas_call(
        faces_kernel,
        out_shape=(faces, faces),
        in_specs=[pl.BlockSpec(memory_space=pl.ANY)] * 2,
        out_specs=tuple(in_vmem(2)),
        scratch_shapes=[
            pltpu.VMEM((2, 5, ny, nz), jnp.float32),
            pltpu.SemaphoreType.DMA((2, 2)),
        ],
        name="faces",
    )(f, u)
    own = (
        entry_matrix_first[0],
        hidden_matrix_second[0],
        final_readout_matrix[0],
        electrical_zone_offset,
    )
    face_across, *later = lax.optimization_barrier((face_across, *own))
    x_across = lax.ppermute(face_across, length, across)
    x_beside = lax.ppermute(face_beside, length, beside)
    other = tuple(lax.ppermute(w, "core", [(0, 1), (1, 0)]) for w in later)
    first_y = [(i, i ^ 1) for i in range(n_gy)]
    then_y = [(i, i + 1) for i in range(1, n_gy - 1, 2)] + [(i + 1, i) for i in range(1, n_gy - 1, 2)]
    below = jnp.where(odd_x == 1, x_beside[1:2], x_across[1:2])
    above = jnp.where(odd_x == 1, x_across[0:1], x_beside[0:1])

    def face_y(high):
        edge, next_edge = high * (ny - 1), high * (ny - 3) + 1
        at = lambda a, i: lax.dynamic_index_in_dim(a, i, a.ndim - 2, False)
        own = at(f, edge).astype(jnp.bfloat16)
        near = jnp.concatenate([at(below, edge), own, at(above, edge)], axis=0)
        near = jnp.pad(near, ((0, 16 - near.shape[0]), (0, 0)))
        rest = jnp.concatenate([at(f, next_edge), at(u, edge).reshape(3 * nx, nz)], axis=0)
        return jnp.concatenate([near, rest.astype(jnp.bfloat16)], axis=0)

    y_then = lax.ppermute(face_y(odd_y), "z", then_y)
    y_first = lax.ppermute(face_y(1 - odd_y), "z", first_y)
    peers = intake_source_tile.shape[1]
    y_then, y_first, *other = lax.optimization_barrier((y_then, y_first, *other))
    interior = (
        jax.ShapeDtypeStruct((nx * ny, nz), jnp.float32),
        jax.ShapeDtypeStruct((20, nx + 8, nz), jnp.float32),
        jax.ShapeDtypeStruct((peers * SLOTS, 2 * CELLS), jnp.bfloat16),
        jax.ShapeDtypeStruct((peers * SLOTS, CELLS), jnp.bfloat16),
        jax.ShapeDtypeStruct((peers // 2, 8, CELLS), jnp.bfloat16),
    )
    scratch = [
        pltpu.VMEM((nx + 4, ny + 16, nz), jnp.float32),
        pltpu.VMEM((nx + 2, ny + 16, nz), jnp.float32),
        pltpu.VMEM((peers * 4 + 8, CELLS), jnp.float32),
        pltpu.VMEM((peers * 4 + 32, CELLS), jnp.float32),
    ]
    given = (
        f,
        u,
        x_across,
        x_beside,
        jnp.transpose(intake_source_tile[0]),
        jnp.transpose(machine_electrical_zone[0]),
    )
    *early, outlets = pl.pallas_call(
        interior_kernel,
        out_shape=(*interior, jax.ShapeDtypeStruct((2, peers // 8, CELLS), jnp.int32)),
        in_specs=in_vmem(8),
        out_specs=tuple(in_vmem(6)),
        scratch_shapes=scratch + [pltpu.VMEM((peers + 8, CELLS), jnp.float32)],
        compiler_params=pltpu.CompilerParams(vmem_limit_bytes=40 * 1024 * 1024),
        cost_estimate=pl.CostEstimate(flops=4 * 10**9, bytes_accessed=8 * 10**6, transcendentals=0),
        name="interior",
    )(*given, jnp.transpose(exhaust_source_tile[0]), machine_tally_matrix)
    warmed, message = pl.pallas_call(
        field_kernel,
        out_shape=(
            jax.ShapeDtypeStruct((nx * ny, nz), jnp.float32),
            jax.ShapeDtypeStruct((peers // 2, MESSAGE_ROWS, CELLS), jnp.bfloat16),
        ),
        in_specs=in_vmem(13),
        out_specs=tuple(in_vmem(2)),
        scratch_shapes=[pltpu.VMEM(a.shape, a.dtype) for a in interior] + scratch,
        compiler_params=pltpu.CompilerParams(vmem_limit_bytes=40 * 1024 * 1024),
        name="field",
    )(*given, y_first, y_then, *early)

    half = ("y", "x", "z")
    arrived = lax.all_to_all(message, half, split_axis=0, concat_axis=0, tiled=True)
    heat = pl.pallas_call(
        surrogate_kernel,
        out_shape=jax.ShapeDtypeStruct((peers // 2, HEAD_ROWS, CELLS), jnp.bfloat16),
        in_specs=in_vmem(9),
        out_specs=in_vmem(1)[0],
        scratch_shapes=[
            pltpu.VMEM((2, 2 * CELLS, entry_matrix_first.shape[2]), jnp.bfloat16),
        ],
        compiler_params=pltpu.CompilerParams(vmem_limit_bytes=40 * 1024 * 1024),
        name="surrogate",
    )(arrived, *own, *other)
    returned = lax.all_to_all(heat, half, split_axis=0, concat_axis=0, tiled=True)

    final = pl.pallas_call(
        exhaust_kernel,
        out_shape=jax.ShapeDtypeStruct((nx * ny, nz), jnp.float32),
        in_specs=in_vmem(5),
        out_specs=in_vmem(1)[0],
        scratch_shapes=[pltpu.VMEM(a.shape, a.dtype) for a in early[2:4]],
        compiler_params=pltpu.CompilerParams(vmem_limit_bytes=40 * 1024 * 1024),
        name="exhaust",
    )(warmed, returned.reshape(peers * SLOTS, CELLS), outlets, early[2], early[3])
    return final.reshape(nx, ny, nz)


def solution(mesh):
    devices = mesh.devices
    split = Mesh(devices.reshape(4, 4, 2, devices.shape[1]), ("y", "x", "core", "z"))
    length = ("y", "x", "core")
    every = length + ("z",)
    return jax.shard_map(
        shards,
        mesh=split,
        in_specs=(
            P(length, "z", None),
            P(None, length, "z", None),
            P(every, None, None),
            P(every, None, None),
            P(every, None, None),
            P(every, None),
            P(every, None, None),
            P(every, None, None),
            P(every, None),
            P(every, None, None),
        ),
        out_specs=P(length, "z", None),
        check_vma=False,
    )
```
